32 devices in a mesh: space: 4 (over z), mode: 8 (over y, x, core).
Axes of the slice: x: 2, y: 2, z: 4, core: 2. Of those that a mesh axis runs over, the one named last changes fastest.
Arguments:
- sqrt_factors: bfloat16 [512, 3, 192, 512], P('mode', None, 'space'), may hold values from -10 to 10
- model_error: bfloat16 [256, 3, 192, 512], P(None, None, ('space', 'mode')), may hold values from -6 to 6
- water_depth: float32 [192, 512], P('space'), may hold values from 0.5 to 2
- sea_mask: int32 [192, 512], P('space'), may hold values 0 or 1
- givens_transform: bfloat16 [768, 512], replicated, may hold values from -0.2 to 1.2
Outputs:
- reduced_modes: bfloat16 [512, 3, 192, 512], P('mode', None, 'space')
- gram_matrix: float32 [768, 768], P(('space', 'mode'))
- inflation: float32 [], replicated
The draws below stay inside these ranges and needn't reach their ends.
All inputs are finite; a program needn't handle non-finite values. No bound on the sum of `sea_mask` on one device may be relied on, other than what follows from the above.
Results may differ from the reference program's by a relative error of at most 0.0049.
Values may be sent and summed in bfloat16 or wider, within the bound.
No kernel may reach another device: no remote copies, remote signals or barrier semaphores. Data moves between devices by JAX's collectives and lax.ppermute only.
A program may use at most 128 MiB of HBM per device.

```python
import math
import jax
import jax.numpy as jnp
from jax import lax

ERROR_FACTORS = 512
NOISE = 256
COLS = 512
LATITUDE_BANDS = 48
NROWS = 192
N_SPACE = 4


def draw_sqrt_factors(key, part):
    position = jnp.arange(NROWS, dtype=jnp.float32) / NROWS
    amplitude = 0.5 * jnp.exp(jnp.log(4.0) * position)
    array_shape = (ERROR_FACTORS, 3, NROWS, COLS)
    values = jnp.clip(jax.random.normal(key, array_shape, jnp.float32), -4.0, 4.0)
    return (values * amplitude[:, None]).astype(jnp.bfloat16)


def draw_givens_transform(key, part):
    columns = ERROR_FACTORS + NOISE
    identity = (jnp.arange(columns)[:, None] == jnp.arange(ERROR_FACTORS)[None, :]).astype(jnp.float32)
    values = jnp.clip(jax.random.normal(key, (columns, ERROR_FACTORS), jnp.float32), -3.0, 3.0)
    return (identity + 0.6 * values / math.sqrt(columns)).astype(jnp.bfloat16)


def set_ends(entries, stream_key, low, top_value):
    index_at = [jax.random.randint(jax.random.fold_in(stream_key, axis), (), 0, length) for axis, length in enumerate(entries.shape)]
    longest = entries.shape.index(max(entries.shape))
    beside = index_at[:longest] + [(index_at[longest] + 1) % entries.shape[longest]] + index_at[longest + 1:]
    return entries.at[tuple(index_at)].set(low).at[tuple(beside)].set(top_value)


def shard_levels(rng, dims, shards, smallest, largest):
    gain = 1.0
    for dim, parts in shards:
        draws = jax.random.uniform(jax.random.fold_in(jax.random.fold_in(rng, 6), dim), (parts,), jnp.float32, smallest / len(shards), largest / len(shards))
        gain = gain * jnp.repeat(jnp.exp(draws), dims[dim] // parts).reshape((-1,) + (1,) * (len(dims) - 1 - dim))
    return gain


def noise(own_key, extent, deviation, reach, cuts=(), held_as=jnp.bfloat16):
    drawn = jax.random.normal(own_key, extent, jnp.float32) * deviation
    if len(cuts) > 0:
        drawn = shard_levels(own_key, extent, cuts, -0.22, 0.18) * drawn
    return jnp.clip(drawn, min=-reach, max=reach).astype(held_as)


def setup_inputs(seed: int = 0) -> dict:
    seeds = jax.random.split(jax.random.key(seed), 6)
    return {
        "sqrt_factors": draw_sqrt_factors(jax.random.fold_in(seeds[5], 71), 0),
        "model_error": noise(seeds[1], (NOISE, 3, NROWS, COLS), 1.0, 6.0, ((2, 32),)),
        "water_depth": jnp.clip(jnp.exp(math.log(2.0) - 1.3862944 * jax.random.uniform(seeds[2], (NROWS, COLS), jnp.float32) ** shard_levels(seeds[2], (NROWS, COLS), ((0, 4),), -0.2, 0.2)), 0.5, 2.0),
        "sea_mask": set_ends((jax.random.randint(seeds[3], (NROWS, COLS), 0, 5) < 4).astype(jnp.int32), jax.random.fold_in(seeds[3], 1), 0, 1),
        "givens_transform": draw_givens_transform(jax.random.fold_in(seeds[5], 71), 0),
    }


flux_coef = 0.2
slope_coef = 0.2
turn_coef = 0.1
keep_coef = 0.95

def column_diff(field):
    widths = [(0, 0)] * (field.ndim - 1) + [(1, 1)]
    padded = jnp.pad(field, widths)
    return padded[..., 2:] - padded[..., :-2]

def advance(layered_surfaces, static):
    depth_cells = static[0]
    wet_cells = static[1]
    surface = layered_surfaces[:, 0]
    flow_east = layered_surfaces[:, 1]
    flow_north = layered_surfaces[:, 2]
    flux_east = depth_cells * flow_east
    flux_north = depth_cells * flow_north
    divergence = column_diff(flux_east[:, 1:-1]) + (flux_north[:, 2:] - flux_north[:, :-2])
    surface_new = wet_cells[1:-1] * (surface[:, 1:-1] - flux_coef * divergence)
    slope_east = column_diff(surface_new[:, 1:-1])
    slope_north = surface_new[:, 2:] - surface_new[:, :-2]
    wet_inner = wet_cells[2:-2]
    east_inner = flow_east[:, 2:-2]
    north_inner = flow_north[:, 2:-2]
    east_new = wet_inner * (keep_coef * east_inner + turn_coef * north_inner - slope_coef * slope_east)
    north_new = wet_inner * (keep_coef * north_inner - turn_coef * east_inner - slope_coef * slope_north)
    return (jnp.stack([surface_new[:, 1:-1], east_new, north_new], axis=1), static[:, 2:-2])

def reference(sqrt_factors, model_error, water_depth, sea_mask, givens_transform):
    static = jnp.stack([water_depth, sea_mask.astype(jnp.float32)])
    static_pad = jnp.pad(static, ((0, 0), (2, 2), (0, 0)))

    def prior_factor_set(factor_collection):
        layered_surfaces = factor_collection.astype(jnp.float32)
        for iteration in range(2):
            padded = jnp.pad(layered_surfaces, ((0, 0), (0, 0), (2, 2), (0, 0)))
            layered_surfaces, unused = advance(padded, static_pad)
        return layered_surfaces.astype(jnp.bfloat16)
    banded_factors = sqrt_factors.reshape((16, ERROR_FACTORS // 16) + sqrt_factors.shape[1:])
    prior_factors = lax.map(prior_factor_set, banded_factors).reshape(sqrt_factors.shape)
    rotation_wide = givens_transform.astype(jnp.float32)
    transform_head = rotation_wide[:ERROR_FACTORS]
    rotation_low = rotation_wide[ERROR_FACTORS:]
    inner_sum_fn = (((1,), (1,)), ((), ()))
    pairwise_entries = (((0,), (0,)), ((), ()))
    largest_level = lax.Precision.HIGHEST

    def partition_latitudes(partition_place):
        first_latitude = (partition_place * LATITUDE_BANDS).astype(jnp.int32)
        prior_latitudes = lax.dynamic_slice_in_dim(prior_factors, first_latitude, LATITUDE_BANDS, 2).astype(jnp.float32).reshape(ERROR_FACTORS, -1)
        model_fault_part = lax.dynamic_slice_in_dim(model_error, first_latitude, LATITUDE_BANDS, 2).astype(jnp.float32).reshape(NOISE, -1)
        return (prior_latitudes, model_fault_part)

    def gram_step(partition_place, carry):
        prior_latitudes, model_fault_part = partition_latitudes(partition_place)
        prior_moments = lax.dot_general(prior_latitudes, prior_latitudes, inner_sum_fn, precision=largest_level)
        mixed_moments = lax.dot_general(prior_latitudes, model_fault_part, inner_sum_fn, precision=largest_level)
        error_gram = lax.dot_general(model_fault_part, model_fault_part, inner_sum_fn, precision=largest_level)
        upper = jnp.concatenate([prior_moments, mixed_moments], 1)
        lower = jnp.concatenate([mixed_moments.T, error_gram], 1)
        return carry + jnp.concatenate([upper, lower], 0)
    summed = lax.fori_loop(0, N_SPACE, gram_step, jnp.zeros((ERROR_FACTORS + NOISE, ERROR_FACTORS + NOISE), jnp.float32))
    cell_count = 3.0 * NROWS * COLS
    gram_matrix = summed / cell_count
    trace_full = jnp.trace(gram_matrix)
    trace_kept = jnp.sum(jnp.dot(gram_matrix, rotation_wide, precision=largest_level) * rotation_wide)
    inflation = jnp.sqrt(trace_full / trace_kept)

    def rotate_step(partition_place, carry):
        prior_latitudes, model_fault_part = partition_latitudes(partition_place)
        truncated_factors = lax.dot_general(transform_head, prior_latitudes, pairwise_entries, precision=largest_level)
        truncated_factors = truncated_factors + lax.dot_general(rotation_low, model_fault_part, pairwise_entries, precision=largest_level)
        scaled = (inflation * truncated_factors).reshape(ERROR_FACTORS, 3, LATITUDE_BANDS, COLS).astype(jnp.bfloat16)
        first_latitude = (partition_place * LATITUDE_BANDS).astype(jnp.int32)
        return lax.dynamic_update_slice_in_dim(carry, scaled, first_latitude, 2)
    reduced_modes = lax.fori_loop(0, N_SPACE, rotate_step, jnp.zeros(sqrt_factors.shape, jnp.bfloat16))
    return (reduced_modes, gram_matrix, inflation)
```

```python
import functools

import jax
import jax.numpy as jnp
from jax import lax
from jax.experimental import pallas as pl
from jax.experimental.pallas import tpu as pltpu
from jax.sharding import PartitionSpec as P

flux_coef = 0.2
slope_coef = 0.2
turn_coef = 0.1
keep_coef = 0.95

GROUP = 16
HALO = 4
LANES = 128
VMEM_BYTES = 48 * 1024 * 1024


def column_diff(tiles):
    lane = lax.broadcasted_iota(jnp.int32, tiles[0].shape, 1)
    from_left = [pltpu.roll(tile, 1, 1) for tile in tiles]
    from_right = [pltpu.roll(tile, LANES - 1, 1) for tile in tiles]
    zero = jnp.zeros_like(tiles[0])
    out = []
    for t in range(len(tiles)):
        left = from_left[t - 1] if t > 0 else zero
        right = from_right[t + 1] if t + 1 < len(tiles) else zero
        previous = jnp.where(lane == 0, left, from_left[t])
        following = jnp.where(lane == LANES - 1, right, from_right[t])
        out.append(following - previous)
    return out


def forecast_kernel(rows, width, x_ref, low_ref, high_ref, depth_ref, wet_ref, out_ref,
                    cells, surf1, east1, north1, surf2):
    tiles = width // LANES
    padded = rows + 2 * HALO

    def spread(m, carry):
        for field in range(3):
            own = x_ref[m, field].astype(jnp.float32)
            high = high_ref[m, field].astype(jnp.float32)
            low = low_ref[m, field].astype(jnp.float32)
            ends = jnp.concatenate([high, low], axis=0)
            for t in range(tiles):
                at = pl.multiple_of(m * padded, 8)
                lanes = slice(t * LANES, (t + 1) * LANES)
                cells[field, t, pl.ds(at, rows)] = own[:, lanes]
                cells[field, t, pl.ds(at + rows, 2 * HALO)] = ends[:, lanes]
        return carry

    lax.fori_loop(0, GROUP, spread, 0)

    def start(field, i):
        place = jnp.where(i < 0, i + padded, i)
        return [cells[field, t, pl.ds(place, GROUP, stride=padded)] for t in range(tiles)]

    def split(ref, i):
        value = ref[i]
        return [value[:, t * LANES:(t + 1) * LANES] for t in range(tiles)]

    def static(ref, i):
        value = jnp.broadcast_to(ref[i + HALO], (8, width))
        value = jnp.concatenate([value, value], axis=0)
        return [value[:, t * LANES:(t + 1) * LANES] for t in range(tiles)]

    def store(ref, i, values):
        for t in range(tiles):
            ref[i, :, t * LANES:(t + 1) * LANES] = values[t]

    def surface_step(i, surface, east, north_after, north_before):
        flux = [d * e for d, e in zip(static(depth_ref, i), east)]
        divergence = column_diff(flux)
        after, before, wet = static(depth_ref, i + 1), static(depth_ref, i - 1), static(wet_ref, i)
        return [
            wet[t] * (surface[t] - (divergence[t] + (after[t] * north_after[t] - before[t] * north_before[t])))
            for t in range(tiles)
        ]

    def flow_step(i, surface, surface_after, surface_before, east, north, with_north):
        wet = static(wet_ref, i)
        slope_north = [a - b for a, b in zip(surface_after, surface_before)]
        north_new = [
            wet[t] * (keep_coef * north[t] - turn_coef * east[t] - slope_coef * slope_north[t])
            for t in range(tiles)
        ]
        if not with_north:
            return None, north_new
        slope_east = column_diff(surface)
        east_new = [
            wet[t] * (keep_coef * east[t] + turn_coef * north[t] - slope_coef * slope_east[t])
            for t in range(tiles)
        ]
        return east_new, north_new

    def first_surface(i, carry):
        value = surface_step(i, start(0, i), start(1, i), start(2, i + 1), start(2, i - 1))
        store(surf1, i + 3, value)
        return carry

    lax.fori_loop(-3, rows + 3, first_surface, 0, unroll=2)

    def first_flow(i, carry):
        east, north = flow_step(
            i, split(surf1, i + 3), split(surf1, i + 4), split(surf1, i + 2),
            start(1, i), start(2, i), True,
        )
        store(east1, i + 2, east)
        store(north1, i + 2, north)
        return carry

    lax.fori_loop(-2, rows + 2, first_flow, 0, unroll=2)

    def second_surface(i, carry):
        value = surface_step(
            i, split(surf1, i + 3), split(east1, i + 2), split(north1, i + 3), split(north1, i + 1)
        )
        store(surf2, i + 1, value)
        return carry

    lax.fori_loop(-1, rows + 1, second_surface, 0, unroll=2)

    def second_flow(i, carry):
        surface = split(surf2, i + 1)
        east, north = flow_step(
            i, surface, split(surf2, i + 2), split(surf2, i),
            split(east1, i + 2), split(north1, i + 2), True,
        )
        for field, values in enumerate((surface, east, north)):
            for t in range(tiles):
                out_ref[i, field, :, t * LANES:(t + 1) * LANES] = values[t].astype(jnp.bfloat16)
        return carry

    lax.fori_loop(0, rows, second_flow, 0, unroll=2)


def forecast_chunk(chunk, factors, low, high, low_chunk, depth, wet):
    modes, fields, rows, width = factors.shape
    tiles = width // LANES
    padded = rows + 2 * HALO
    row = pltpu.VMEM((1, GROUP, width), jnp.float32)

    def rows_of(count):
        return pltpu.VMEM((count, GROUP, width), jnp.float32)

    return pl.pallas_call(
        functools.partial(forecast_kernel, rows, width),
        grid=(1,),
        out_shape=jax.ShapeDtypeStruct((rows, fields, GROUP, width), jnp.bfloat16),
        in_specs=[
            pl.BlockSpec((GROUP, fields, rows, width), lambda i: (chunk, 0, 0, 0)),
            pl.BlockSpec((GROUP, fields, HALO, width), lambda i: (low_chunk, 0, 0, 0)),
            pl.BlockSpec((GROUP, fields, HALO, width), lambda i: (low_chunk, 0, 0, 0)),
            pl.BlockSpec((padded, 1, width), lambda i: (0, 0, 0)),
            pl.BlockSpec((padded, 1, width), lambda i: (0, 0, 0)),
        ],
        out_specs=pl.BlockSpec((rows, fields, GROUP, width), lambda i: (0, 0, 0, 0)),
        scratch_shapes=[
            pltpu.VMEM((fields, tiles, GROUP * padded, LANES), jnp.float32),
            rows_of(rows + 6),
            rows_of(rows + 4),
            rows_of(rows + 4),
            rows_of(rows + 2),
        ],
        compiler_params=pltpu.CompilerParams(vmem_limit_bytes=VMEM_BYTES),
        cost_estimate=pl.CostEstimate(
            flops=60 * GROUP * rows * width,
            bytes_accessed=2 * 2 * GROUP * fields * rows * width,
            transcendentals=0,
        ),
        name="forecast",
    )(factors, low, high, depth, wet)


def all_columns(chunk_refs, fault_ref, j):
    own = [ref[:, j, 0] for ref in chunk_refs]
    joined = jnp.concatenate(own, axis=1)
    return joined.reshape(-1, joined.shape[-1]), fault_ref[0, j]


def rotate_kernel(count, *refs):
    chunk_refs = refs[:count]
    fault_ref, turn_ref, out_ref, power_ref, total = refs[count:]
    j = pl.program_id(0)
    prior, fault = all_columns(chunk_refs, fault_ref, 0)
    columns = prior.shape[0]
    value = jnp.dot(turn_ref[:, :columns], prior, preferred_element_type=jnp.float32)
    value = value + jnp.dot(turn_ref[:, columns:], fault, preferred_element_type=jnp.float32)
    out_ref[...] = value.astype(jnp.bfloat16).reshape(out_ref.shape)
    square = jnp.sum((value * value).reshape(-1, 8, value.shape[-1]), axis=0)

    @pl.when(j == 0)
    def _():
        total[...] = square

    @pl.when(j > 0)
    def _():
        total[...] += square

    power_ref[...] = total[...]


def rotate_field(field, chunks, fault, turn, parts):
    width = chunks[0].shape[-1]
    each = chunks[0].shape[0] // parts
    kept = turn.shape[0]
    noise = fault.shape[2]
    modes = kept // parts
    views = [c.reshape(parts, each, 3, GROUP, width) for c in chunks]
    return pl.pallas_call(
        functools.partial(rotate_kernel, len(views)),
        grid=(each,),
        out_shape=(
            jax.ShapeDtypeStruct((parts, each, modes, width), jnp.bfloat16),
            jax.ShapeDtypeStruct((8, width), jnp.float32),
        ),
        in_specs=[
            pl.BlockSpec((parts, 1, 1, GROUP, width), lambda j: (0, j, field, 0, 0)) for _ in views
        ] + [
            pl.BlockSpec((1, 1, noise, width), lambda j: (field, j, 0, 0)),
            pl.BlockSpec(turn.shape, lambda j: (0, 0)),
        ],
        out_specs=(
            pl.BlockSpec((parts, 1, modes, width), lambda j: (0, j, 0, 0)),
            pl.BlockSpec((8, width), lambda j: (0, 0)),
        ),
        scratch_shapes=[pltpu.VMEM((8, width), jnp.float32)],
        compiler_params=pltpu.CompilerParams(vmem_limit_bytes=VMEM_BYTES),
        cost_estimate=pl.CostEstimate(
            flops=2 * each * width * kept * turn.shape[1],
            bytes_accessed=2 * each * width * (kept + turn.shape[1]),
            transcendentals=0,
        ),
        name="rotate",
    )(*views, fault, turn)


def gram_kernel(count, each, *refs):
    chunk_refs = refs[:count]
    fault_ref, out_ref = refs[count:]
    pairs = [all_columns(chunk_refs, fault_ref, j) for j in range(each)]
    columns = jnp.concatenate(
        [jnp.concatenate([prior, fault], axis=0) for prior, fault in pairs], axis=1
    )
    value = lax.dot_general(
        columns, columns, (((1,), (1,)), ((), ())), preferred_element_type=jnp.float32
    )

    @pl.when(pl.program_id(0) == 0)
    def _():
        out_ref[...] = value

    @pl.when(pl.program_id(0) > 0)
    def _():
        out_ref[...] += value


def local_gram(chunks, fault, parts):
    width = chunks[0].shape[-1]
    each = chunks[0].shape[0] // parts
    noise = fault.shape[2]
    columns = parts * GROUP * len(chunks) + noise
    views = [c.reshape(parts, each, 3, GROUP, width) for c in chunks]
    return pl.pallas_call(
        functools.partial(gram_kernel, len(views), each),
        grid=(3,),
        out_shape=jax.ShapeDtypeStruct((columns, columns), jnp.float32),
        in_specs=[
            pl.BlockSpec((parts, each, 1, GROUP, width), lambda f: (0, 0, f, 0, 0)) for _ in views
        ] + [pl.BlockSpec((1, each, noise, width), lambda f: (f, 0, 0, 0))],
        out_specs=pl.BlockSpec((columns, columns), lambda f: (0, 0)),
        compiler_params=pltpu.CompilerParams(vmem_limit_bytes=VMEM_BYTES),
        cost_estimate=pl.CostEstimate(
            flops=2 * 3 * each * width * columns * columns,
            bytes_accessed=2 * 3 * each * width * columns,
            transcendentals=0,
        ),
        name="gram",
    )(*views, fault)


def finish_kernel(aliased, scale_ref, x_ref, *refs):
    out_ref, cells = refs[aliased:]
    parts, each, _, width = x_ref.shape
    rows = parts * each
    tiles = width // LANES

    def spread(i, carry):
        value = x_ref[i // each, i % each].astype(jnp.float32)
        for t in range(tiles):
            cells[t, pl.ds(i, GROUP, stride=rows)] = value[:, t * LANES:(t + 1) * LANES]
        return carry

    lax.fori_loop(0, rows, spread, 0, unroll=2)
    scale = scale_ref[0, 0]

    def gather(m, carry):
        at = pl.multiple_of(m * rows, 8)
        for t in range(tiles):
            value = cells[t, pl.ds(at, rows)] * scale
            out_ref[m, 0, :, t * LANES:(t + 1) * LANES] = value.astype(jnp.bfloat16)
        return carry

    lax.fori_loop(0, GROUP, gather, 0, unroll=2)


def finish_field(field, arrived, scale, previous):
    parts, each, modes, width = arrived.shape
    rows = parts * each
    operands = [scale.reshape(1, 1), arrived]
    specs = [
        pl.BlockSpec(memory_space=pltpu.SMEM),
        pl.BlockSpec((parts, each, GROUP, width), lambda m: (0, 0, m, 0)),
    ]
    aliases = {}
    if previous is not None:
        operands.append(previous)
        specs.append(pl.BlockSpec(memory_space=pl.ANY))
        aliases = {2: 0}
    return pl.pallas_call(
        functools.partial(finish_kernel, len(aliases)),
        grid=(modes // GROUP,),
        out_shape=jax.ShapeDtypeStruct((modes, 3, rows, width), jnp.bfloat16),
        in_specs=specs,
        out_specs=pl.BlockSpec((GROUP, 1, rows, width), lambda m: (m, field, 0, 0)),
        scratch_shapes=[pltpu.VMEM((width // LANES, GROUP * rows, LANES), jnp.float32)],
        input_output_aliases=aliases,
        compiler_params=pltpu.CompilerParams(vmem_limit_bytes=VMEM_BYTES),
        cost_estimate=pl.CostEstimate(
            flops=modes * rows * width,
            bytes_accessed=4 * modes * rows * width,
            transcendentals=0,
        ),
        name="finish",
    )(*operands)


def total_over(value, axis):
    count = lax.axis_size(axis)
    step = 1
    if count & (count - 1):
        return lax.psum(value, axis)
    while step < count:
        value = value + lax.ppermute(value, axis, [(i, i ^ step) for i in range(count)])
        step *= 2
    return value


def edges(block, dim):
    count = lax.axis_size("space")
    forward = [(i, i + 1) for i in range(count - 1)]
    backward = [(target, source) for source, target in forward]
    size = block.shape[dim]
    low = lax.ppermute(lax.slice_in_dim(block, size - HALO, size, axis=dim), "space", forward)
    high = lax.ppermute(lax.slice_in_dim(block, 0, HALO, axis=dim), "space", backward)
    return low, high


def shards(sqrt_factors, model_error, water_depth, sea_mask, givens_transform):
    modes, fields, rows, width = sqrt_factors.shape
    parts = lax.axis_size("mode")
    count = modes // GROUP

    static = jnp.stack([flux_coef * water_depth, sea_mask.astype(jnp.float32)])
    static_low, static_high = edges(static, 1)
    static = jnp.concatenate([static_low, static, static_high], axis=1)[:, :, None]
    head = edges(sqrt_factors[:GROUP], 2)
    tail = edges(sqrt_factors[GROUP:], 2)

    chunks = []
    for c in range(count):
        low, high = head if c == 0 else tail
        chunk = forecast_chunk(
            c, sqrt_factors, low, high, max(c - 1, 0), static[0], static[1]
        )
        chunks.append(lax.all_to_all(chunk, "mode", split_axis=0, concat_axis=0, tiled=True))

    fault = model_error.transpose(1, 2, 0, 3)
    turn = givens_transform.T
    arrived, power = [], 0.0
    for field in range(fields):
        rotated, square = rotate_field(field, chunks, fault, turn, parts)
        power = power + jnp.sum(square)
        arrived.append(
            lax.all_to_all(rotated, "mode", split_axis=0, concat_axis=0, tiled=True)
        )
    gram = local_gram(chunks, fault, parts)
    cell_count = float(fields * rows * lax.axis_size("space") * width)
    traces = jnp.stack([jnp.trace(gram), power])
    traces = total_over(total_over(traces, "mode"), "space")
    inflation = jnp.sqrt(traces[0] / traces[1])

    gram = lax.psum_scatter(gram, "space", scatter_dimension=0, tiled=True)
    gram = lax.psum_scatter(gram, "mode", scatter_dimension=0, tiled=True) / cell_count

    reduced = None
    for field in range(fields):
        reduced = finish_field(field, arrived[field], inflation, reduced)
    return (reduced, gram, inflation)


def solution(mesh):
    in_specs = (
        P("mode", None, "space", None),
        P(None, None, ("space", "mode"), None),
        P("space", None),
        P("space", None),
        P(),
    )
    out_specs = (P("mode", None, "space", None), P(("space", "mode"), None), P())
    return jax.shard_map(shards, mesh=mesh, in_specs=in_specs, out_specs=out_specs, check_vma=False)
```

```python
import functools

import jax
import jax.numpy as jnp
from jax import lax
from jax.experimental import pallas as pl
from jax.experimental.pallas import tpu as pltpu
from jax.sharding import PartitionSpec as P

flux_coef = 0.2
slope_coef = 0.2
turn_coef = 0.1
keep_coef = 0.95

GROUP = 16
HALO = 4
LANES = 128
VMEM_BYTES = 48 * 1024 * 1024


def odd(count):
    return count + 1 - count % 2


def column_diff(tiles):
    lane = lax.broadcasted_iota(jnp.int32, tiles[0].shape, 1)
    from_left = [pltpu.roll(tile, 1, 1) for tile in tiles]
    from_right = [pltpu.roll(tile, LANES - 1, 1) for tile in tiles]
    zero = jnp.zeros_like(tiles[0])
    out = []
    for t in range(len(tiles)):
        left = from_left[t - 1] if t > 0 else zero
        right = from_right[t + 1] if t + 1 < len(tiles) else zero
        previous = jnp.where(lane == 0, left, from_left[t])
        following = jnp.where(lane == LANES - 1, right, from_right[t])
        out.append(following - previous)
    return out


def forecast_kernel(rows, width, x_ref, low_ref, high_ref, depth_ref, wet_ref, out_ref,
                    cells, surf1, east1, north1, surf2):
    tiles = width // LANES
    padded = rows + 2 * HALO
    pitch = odd(padded)

    def spread(m, carry):
        for field in range(3):
            own = x_ref[m, field].astype(jnp.float32)
            high = high_ref[m, field].astype(jnp.float32)
            low = low_ref[m, field].astype(jnp.float32)
            ends = jnp.concatenate([high, low], axis=0)
            for t in range(tiles):
                at = m * pitch
                lanes = slice(t * LANES, (t + 1) * LANES)
                cells[field, t, pl.ds(at, rows)] = own[:, lanes]
                cells[field, t, pl.ds(at + rows, 2 * HALO)] = ends[:, lanes]
        return carry

    lax.fori_loop(0, GROUP, spread, 0)

    def start(field, i):
        place = jnp.where(i < 0, i + padded, i)
        return [cells[field, t, pl.ds(place, GROUP, stride=pitch)] for t in range(tiles)]

    def split(ref, i):
        value = ref[i]
        return [value[:, t * LANES:(t + 1) * LANES] for t in range(tiles)]

    def static(ref, i):
        value = jnp.broadcast_to(ref[i + HALO], (8, width))
        value = jnp.concatenate([value, value], axis=0)
        return [value[:, t * LANES:(t + 1) * LANES] for t in range(tiles)]

    def store(ref, i, values):
        for t in range(tiles):
            ref[i, :, t * LANES:(t + 1) * LANES] = values[t]

    def surface_step(i, surface, east, north_after, north_before):
        flux = [d * e for d, e in zip(static(depth_ref, i), east)]
        divergence = column_diff(flux)
        after, before, wet = static(depth_ref, i + 1), static(depth_ref, i - 1), static(wet_ref, i)
        return [
            wet[t] * (surface[t] - (divergence[t] + (after[t] * north_after[t] - before[t] * north_before[t])))
            for t in range(tiles)
        ]

    def flow_step(i, surface, surface_after, surface_before, east, north, with_north):
        wet = static(wet_ref, i)
        slope_north = [a - b for a, b in zip(surface_after, surface_before)]
        north_new = [
            wet[t] * (keep_coef * north[t] - turn_coef * east[t] - slope_coef * slope_north[t])
            for t in range(tiles)
        ]
        if not with_north:
            return None, north_new
        slope_east = column_diff(surface)
        east_new = [
            wet[t] * (keep_coef * east[t] + turn_coef * north[t] - slope_coef * slope_east[t])
            for t in range(tiles)
        ]
        return east_new, north_new

    def first_surface(i, carry):
        value = surface_step(i, start(0, i), start(1, i), start(2, i + 1), start(2, i - 1))
        store(surf1, i + 3, value)
        return carry

    lax.fori_loop(-3, rows + 3, first_surface, 0, unroll=2)

    def first_flow(i, carry):
        east, north = flow_step(
            i, split(surf1, i + 3), split(surf1, i + 4), split(surf1, i + 2),
            start(1, i), start(2, i), True,
        )
        store(east1, i + 2, east)
        store(north1, i + 2, north)
        return carry

    lax.fori_loop(-2, rows + 2, first_flow, 0, unroll=2)

    def second_surface(i, carry):
        value = surface_step(
            i, split(surf1, i + 3), split(east1, i + 2), split(north1, i + 3), split(north1, i + 1)
        )
        store(surf2, i + 1, value)
        return carry

    lax.fori_loop(-1, rows + 1, second_surface, 0, unroll=2)

    def second_flow(i, carry):
        surface = split(surf2, i + 1)
        east, north = flow_step(
            i, surface, split(surf2, i + 2), split(surf2, i),
            split(east1, i + 2), split(north1, i + 2), True,
        )
        for field, values in enumerate((surface, east, north)):
            for t in range(tiles):
                out_ref[i, field, :, t * LANES:(t + 1) * LANES] = values[t].astype(jnp.bfloat16)
        return carry

    lax.fori_loop(0, rows, second_flow, 0, unroll=2)


def forecast_groups(first, count, factors, low, high, depth, wet):
    modes, fields, rows, width = factors.shape
    tiles = width // LANES
    padded = rows + 2 * HALO

    def rows_of(count):
        return pltpu.VMEM((count, GROUP, width), jnp.float32)

    return pl.pallas_call(
        functools.partial(forecast_kernel, rows, width),
        grid=(count,),
        out_shape=jax.ShapeDtypeStruct((rows, fields, count * GROUP, width), jnp.bfloat16),
        in_specs=[
            pl.BlockSpec((GROUP, fields, rows, width), lambda i: (first + i, 0, 0, 0)),
            pl.BlockSpec((GROUP, fields, HALO, width), lambda i: (i, 0, 0, 0)),
            pl.BlockSpec((GROUP, fields, HALO, width), lambda i: (i, 0, 0, 0)),
            pl.BlockSpec((padded, 1, width), lambda i: (0, 0, 0)),
            pl.BlockSpec((padded, 1, width), lambda i: (0, 0, 0)),
        ],
        out_specs=pl.BlockSpec((rows, fields, GROUP, width), lambda i: (0, 0, i, 0)),
        scratch_shapes=[
            pltpu.VMEM((fields, tiles, GROUP * odd(padded), LANES), jnp.float32),
            rows_of(rows + 6),
            rows_of(rows + 4),
            rows_of(rows + 4),
            rows_of(rows + 2),
        ],
        compiler_params=pltpu.CompilerParams(vmem_limit_bytes=VMEM_BYTES),
        cost_estimate=pl.CostEstimate(
            flops=60 * count * GROUP * rows * width,
            bytes_accessed=2 * 2 * count * GROUP * fields * rows * width,
            transcendentals=0,
        ),
        name="forecast",
    )(factors, low, high, depth, wet)


def all_columns(chunk_refs, fault_ref, j):
    own = [ref[:, j, 0] for ref in chunk_refs]
    joined = jnp.concatenate(own, axis=1)
    return joined.reshape(-1, joined.shape[-1]), fault_ref[0, j]


def rotate_kernel(count, *refs):
    chunk_refs = refs[:count]
    fault_ref, turn_ref, out_ref = refs[count:]
    prior, fault = all_columns(chunk_refs, fault_ref, 0)
    columns = prior.shape[0]
    value = jnp.dot(turn_ref[:, :columns], prior, preferred_element_type=jnp.float32)
    value = value + jnp.dot(turn_ref[:, columns:], fault, preferred_element_type=jnp.float32)
    out_ref[...] = value.astype(jnp.bfloat16).reshape(out_ref.shape)


def by_part(chunks, parts):
    return [c.reshape((parts, c.shape[0] // parts) + c.shape[1:]) for c in chunks]


def rotate_fields(first, fields, chunks, fault, turn, parts):
    width = chunks[0].shape[-1]
    each = chunks[0].shape[0] // parts
    kept = turn.shape[0]
    noise = fault.shape[2]
    modes = kept // parts
    views = by_part(chunks, parts)
    return pl.pallas_call(
        functools.partial(rotate_kernel, len(views)),
        grid=(fields, each),
        out_shape=jax.ShapeDtypeStruct((parts, fields, each, modes, width), jnp.bfloat16),
        in_specs=[
            pl.BlockSpec((parts, 1, 1, v.shape[3], width), lambda f, j: (0, j, first + f, 0, 0))
            for v in views
        ] + [
            pl.BlockSpec((1, 1, noise, width), lambda f, j: (first + f, j, 0, 0)),
            pl.BlockSpec(turn.shape, lambda f, j: (0, 0)),
        ],
        out_specs=pl.BlockSpec((parts, 1, 1, modes, width), lambda f, j: (0, f, j, 0, 0)),
        compiler_params=pltpu.CompilerParams(vmem_limit_bytes=VMEM_BYTES),
        cost_estimate=pl.CostEstimate(
            flops=2 * fields * each * width * kept * turn.shape[1],
            bytes_accessed=2 * fields * each * width * (kept + turn.shape[1]),
            transcendentals=0,
        ),
        name="rotate",
    )(*views, fault, turn)


def gram_kernel(count, each, *refs):
    chunk_refs = refs[:count]
    fault_ref, turn_ref, out_ref, trace_ref = refs[count:]
    pairs = [all_columns(chunk_refs, fault_ref, j) for j in range(each)]
    columns = jnp.concatenate(
        [jnp.concatenate([prior, fault], axis=0) for prior, fault in pairs], axis=1
    )
    value = lax.dot_general(
        columns, columns, (((1,), (1,)), ((), ())), preferred_element_type=jnp.float32
    )
    step = pl.program_id(0)

    @pl.when(step == 0)
    def _():
        out_ref[...] = value

    @pl.when(step > 0)
    def _():
        out_ref[...] += value

    @pl.when(step == pl.num_programs(0) - 1)
    def _():
        gram = out_ref[...]
        size = gram.shape[0]
        row = lax.broadcasted_iota(jnp.int32, gram.shape, 0)
        column = lax.broadcasted_iota(jnp.int32, gram.shape, 1)
        diagonal = jnp.where(row == column, gram, 0.0)
        trace_ref[0] = jnp.sum(diagonal.reshape(-1, 8, size), axis=0)
        turn = turn_ref[...]
        turned = 0.0
        for _ in range(3):
            piece = gram.astype(jnp.bfloat16)
            turned = turned + jnp.dot(turn, piece, preferred_element_type=jnp.float32)
            gram = gram - piece.astype(jnp.float32)
        kept = turned * turn.astype(jnp.float32)
        trace_ref[1] = jnp.sum(kept.reshape(-1, 8, size), axis=0)


def local_gram(chunks, fault, turn, parts):
    width = chunks[0].shape[-1]
    each = chunks[0].shape[0] // parts
    noise = fault.shape[2]
    columns = turn.shape[1]
    views = by_part(chunks, parts)
    return pl.pallas_call(
        functools.partial(gram_kernel, len(views), each),
        grid=(3,),
        out_shape=(
            jax.ShapeDtypeStruct((columns, columns), jnp.float32),
            jax.ShapeDtypeStruct((2, 8, columns), jnp.float32),
        ),
        in_specs=[
            pl.BlockSpec((parts, each, 1, v.shape[3], width), lambda f: (0, 0, f, 0, 0))
            for v in views
        ] + [
            pl.BlockSpec((1, each, noise, width), lambda f: (f, 0, 0, 0)),
            pl.BlockSpec(turn.shape, lambda f: (0, 0)),
        ],
        out_specs=(
            pl.BlockSpec((columns, columns), lambda f: (0, 0)),
            pl.BlockSpec((2, 8, columns), lambda f: (0, 0, 0)),
        ),
        compiler_params=pltpu.CompilerParams(vmem_limit_bytes=VMEM_BYTES),
        cost_estimate=pl.CostEstimate(
            flops=2 * 3 * each * width * columns * columns,
            bytes_accessed=2 * 3 * each * width * columns,
            transcendentals=0,
        ),
        name="gram",
    )(*views, fault, turn)


def finish_kernel(aliased, scale_ref, x_ref, *refs):
    out_ref, cells = refs[aliased:]
    parts, _, each, _, width = x_ref.shape
    rows = parts * each
    tiles = width // LANES
    pitch = odd(rows)

    def spread(i, carry):
        value = x_ref[i // each, 0, i % each].astype(jnp.float32)
        for t in range(tiles):
            cells[t, pl.ds(i, GROUP, stride=pitch)] = value[:, t * LANES:(t + 1) * LANES]
        return carry

    lax.fori_loop(0, rows, spread, 0, unroll=2)
    scale = scale_ref[0, 0]

    def gather(m, carry):
        for t in range(tiles):
            value = cells[t, pl.ds(m * pitch, rows)] * scale
            out_ref[m, 0, :, t * LANES:(t + 1) * LANES] = value.astype(jnp.bfloat16)
        return carry

    lax.fori_loop(0, GROUP, gather, 0, unroll=2)


def finish_field(field, arrived, place, scale, previous):
    parts, _, each, modes, width = arrived.shape
    rows = parts * each
    operands = [scale.reshape(1, 1), arrived]
    specs = [
        pl.BlockSpec(memory_space=pltpu.SMEM),
        pl.BlockSpec((parts, 1, each, GROUP, width), lambda m: (0, place, 0, m, 0)),
    ]
    aliases = {}
    if previous is not None:
        operands.append(previous)
        specs.append(pl.BlockSpec(memory_space=pl.ANY))
        aliases = {2: 0}
    return pl.pallas_call(
        functools.partial(finish_kernel, len(aliases)),
        grid=(modes // GROUP,),
        out_shape=jax.ShapeDtypeStruct((modes, 3, rows, width), jnp.bfloat16),
        in_specs=specs,
        out_specs=pl.BlockSpec((GROUP, 1, rows, width), lambda m: (m, field, 0, 0)),
        scratch_shapes=[pltpu.VMEM((width // LANES, GROUP * odd(rows), LANES), jnp.float32)],
        input_output_aliases=aliases,
        compiler_params=pltpu.CompilerParams(vmem_limit_bytes=VMEM_BYTES),
        cost_estimate=pl.CostEstimate(
            flops=modes * rows * width,
            bytes_accessed=4 * modes * rows * width,
            transcendentals=0,
        ),
        name="finish",
    )(*operands)


def total_over(value, axis):
    count = lax.axis_size(axis)
    step = 1
    if count & (count - 1):
        return lax.psum(value, axis)
    while step < count:
        value = value + lax.ppermute(value, axis, [(i, i ^ step) for i in range(count)])
        step *= 2
    return value


def edges(block, dim):
    count = lax.axis_size("space")
    forward = [(i, i + 1) for i in range(count - 1)]
    backward = [(target, source) for source, target in forward]
    size = block.shape[dim]
    low = lax.ppermute(lax.slice_in_dim(block, size - HALO, size, axis=dim), "space", forward)
    high = lax.ppermute(lax.slice_in_dim(block, 0, HALO, axis=dim), "space", backward)
    return low, high


def shards(sqrt_factors, model_error, water_depth, sea_mask, givens_transform):
    modes, fields, rows, width = sqrt_factors.shape
    parts = lax.axis_size("mode")
    count = modes // GROUP

    static = jnp.stack([flux_coef * water_depth, sea_mask.astype(jnp.float32)])
    static_low, static_high = edges(static, 1)
    static = jnp.concatenate([static_low, static, static_high], axis=1)[:, :, None]
    head = edges(sqrt_factors[:GROUP], 2)
    tail = edges(sqrt_factors[GROUP:], 2)

    swap = functools.partial(
        lax.all_to_all, axis_name="mode", split_axis=0, concat_axis=0, tiled=True
    )
    chunks = [
        swap(forecast_groups(0, 1, sqrt_factors, *head, static[0], static[1])),
        swap(forecast_groups(1, count - 1, sqrt_factors, *tail, static[0], static[1])),
    ]

    fault = model_error.transpose(1, 2, 0, 3)
    turn = givens_transform.T
    arrived = [
        swap(rotate_fields(first, span, chunks, fault, turn, parts)) for first, span in ((0, 1), (1, 2))
    ]
    gram, traces = local_gram(chunks, fault, turn, parts)
    traces = jnp.sum(traces, axis=(1, 2))
    traces = total_over(total_over(traces, "space"), "mode")
    inflation = jnp.sqrt(traces[0] / traces[1])
    cell_count = float(fields * rows * lax.axis_size("space") * width)

    gram = lax.psum_scatter(gram, "space", scatter_dimension=0, tiled=True)
    gram = lax.psum_scatter(gram, "mode", scatter_dimension=0, tiled=True) / cell_count

    reduced = None
    for field in range(fields):
        reduced = finish_field(field, arrived[min(field, 1)], max(field - 1, 0), inflation, reduced)
    return (reduced, gram, inflation)


def solution(mesh):
    in_specs = (
        P("mode", None, "space", None),
        P(None, None, ("space", "mode"), None),
        P("space", None),
        P("space", None),
        P(),
    )
    out_specs = (P("mode", None, "space", None), P(("space", "mode"), None), P())
    return jax.shard_map(shards, mesh=mesh, in_specs=in_specs, out_specs=out_specs, check_vma=False)
```

```python
import functools

import jax
import jax.numpy as jnp
import numpy as np
from jax import lax
from jax.experimental import pallas as pl
from jax.experimental.pallas import tpu as pltpu
from jax.sharding import PartitionSpec as P

flux_coef = 0.2
slope_coef = 0.2
turn_coef = 0.1
keep_coef = 0.95

GROUP = 16
HALO = 4
LANES = 128
VMEM_BYTES = 48 * 1024 * 1024


def column_diff(tiles):
    lane = lax.broadcasted_iota(jnp.int32, tiles[0].shape, 1)
    from_left = [pltpu.roll(tile, 1, 1) for tile in tiles]
    from_right = [pltpu.roll(tile, LANES - 1, 1) for tile in tiles]
    zero = jnp.zeros_like(tiles[0])
    out = []
    for t in range(len(tiles)):
        left = from_left[t - 1] if t > 0 else zero
        right = from_right[t + 1] if t + 1 < len(tiles) else zero
        previous = jnp.where(lane == 0, left, from_left[t])
        following = jnp.where(lane == LANES - 1, right, from_right[t])
        out.append(following - previous)
    return out


def swap_matrix(inner, outer):
    place = np.arange(inner * outer).reshape(outer, inner).T.reshape(-1)
    matrix = np.zeros((inner * outer, inner * outer), np.float32)
    matrix[np.arange(inner * outer), place] = 1.0
    return jnp.asarray(matrix, jnp.bfloat16)


def split_pieces(value):
    pieces = []
    for _ in range(3):
        piece = lax.reduce_precision(value, 8, 7)
        pieces.append(piece.astype(jnp.bfloat16))
        value = value - piece
    return pieces


def block_of(count):
    return max(size for size in range(1, 7) if count % size == 0)


def forecast_kernel(x_ref, low_ref, high_ref, low_static, high_static, depth_ref, mask_ref,
                    swap_ref, swap_ends_ref, out_ref,
                    cells, ends, depth, wet, surf1, east1, north1, surf2):
    _, fields, rows, width = x_ref.shape
    tiles = width // LANES
    spots = [slice(t * LANES, (t + 1) * LANES) for t in range(tiles)]

    ends[:, :HALO] = low_ref[...].astype(jnp.float32)
    ends[:, HALO:] = high_ref[...].astype(jnp.float32)
    for field in range(fields):
        for top in range(0, rows, GROUP):
            block = x_ref[:, field, top:top + GROUP, :].reshape(GROUP * GROUP, width)
            block = jnp.dot(swap_ref[...], block, preferred_element_type=jnp.float32)
            cells[field, HALO + top:HALO + top + GROUP] = block.reshape(GROUP, GROUP, width)
        block = jnp.concatenate([ends[m * fields + field] for m in range(GROUP)], axis=0)
        block = jnp.dot(
            swap_ends_ref[...], block.astype(jnp.bfloat16), preferred_element_type=jnp.float32
        ).reshape(2 * HALO, GROUP, width)
        cells[field, :HALO] = block[:HALO]
        cells[field, HALO + rows:] = block[HALO:]

    def place_static(place, depth_row, wet_row):
        depth[place] = jnp.broadcast_to(flux_coef * depth_row, (8, width))
        wet[place] = jnp.broadcast_to(wet_row, (8, width))

    for static, first in ((low_static, 0), (high_static, HALO + rows)):
        value = static[...].astype(jnp.float32)
        level = value[0] + value[1] + value[2]
        for j in range(HALO):
            place_static(first + j, level[j:j + 1], value[3, j:j + 1])
    for top in range(0, rows, 8):
        level = depth_ref[top:top + 8]
        sea = mask_ref[top:top + 8].astype(jnp.float32)
        for j in range(8):
            place_static(HALO + top + j, level[j:j + 1], sea[j:j + 1])

    def get(ref, i):
        return [ref[i, :, spot] for spot in spots]

    def get_field(field, i):
        return [cells[field, i + HALO, :, spot] for spot in spots]

    def get_static(ref, i):
        parts = [ref[i + HALO, :, spot] for spot in spots]
        return [jnp.concatenate([part] * (GROUP // 8), axis=0) for part in parts]

    def put(ref, i, values):
        for spot, value in zip(spots, values):
            ref[i, :, spot] = value

    def times(one, other):
        return [a * b for a, b in zip(one, other)]

    def over_rows(first, last, body):
        size = block_of(last - first)

        def block(k, carry):
            body(first + k * size, size)
            return carry

        lax.fori_loop(0, (last - first) // size, block, 0)

    def surfaces(i, size, surface_at, east_at, north_at, put_at):
        flux = {j: times(get_static(depth, i + j), north_at(i + j)) for j in (-1, 0)}
        for j in range(size):
            flux[j + 1] = times(get_static(depth, i + j + 1), north_at(i + j + 1))
            sides = column_diff(times(get_static(depth, i + j), east_at(i + j)))
            sea, surface = get_static(wet, i + j), surface_at(i + j)
            put_at(i + j, [
                sea[t] * (surface[t] - (sides[t] + (flux[j + 1][t] - flux[j - 1][t])))
                for t in range(tiles)
            ])

    def flows(i, size, surface_at, east_at, north_at, put_at):
        surface = {j: surface_at(i + j) for j in (-1, 0)}
        for j in range(size):
            surface[j + 1] = surface_at(i + j + 1)
            sides = column_diff(surface[j])
            sea, east, north = get_static(wet, i + j), east_at(i + j), north_at(i + j)
            put_at(i + j, surface[j], [
                sea[t] * (keep_coef * east[t] + turn_coef * north[t] - slope_coef * sides[t])
                for t in range(tiles)
            ], [
                sea[t] * (keep_coef * north[t] - turn_coef * east[t]
                          - slope_coef * (surface[j + 1][t] - surface[j - 1][t]))
                for t in range(tiles)
            ])

    def first_surface(i, size):
        surfaces(
            i, size, lambda r: get_field(0, r), lambda r: get_field(1, r),
            lambda r: get_field(2, r), lambda r, value: put(surf1, r + 3, value),
        )

    def first_flow(i, size):
        def put_flow(r, surface, east, north):
            put(east1, r + 2, east)
            put(north1, r + 2, north)

        flows(
            i, size, lambda r: get(surf1, r + 3), lambda r: get_field(1, r),
            lambda r: get_field(2, r), put_flow,
        )

    def second_surface(i, size):
        surfaces(
            i, size, lambda r: get(surf1, r + 3), lambda r: get(east1, r + 2),
            lambda r: get(north1, r + 2), lambda r, value: put(surf2, r + 1, value),
        )

    def second_flow(i, size):
        def put_out(r, surface, east, north):
            for field, values in enumerate((surface, east, north)):
                for spot, value in zip(spots, values):
                    out_ref[r, field, :, spot] = value.astype(jnp.bfloat16)

        flows(
            i, size, lambda r: get(surf2, r + 1), lambda r: get(east1, r + 2),
            lambda r: get(north1, r + 2), put_out,
        )

    over_rows(-3, rows + 3, first_surface)
    over_rows(-2, rows + 2, first_flow)
    over_rows(-1, rows + 1, second_surface)
    over_rows(0, rows, second_flow)


def forecast_groups(first, count, factors, low, high, static_low, static_high, depth, mask):
    modes, fields, rows, width = factors.shape
    padded = rows + 2 * HALO
    edge = GROUP * fields
    swap, swap_ends = swap_matrix(GROUP, GROUP), swap_matrix(2 * HALO, GROUP)

    def rows_of(count):
        return pltpu.VMEM((count, GROUP, width), jnp.float32)

    def whole(value):
        return pl.BlockSpec(value.shape, lambda i: (0,) * value.ndim)

    return pl.pallas_call(
        forecast_kernel,
        grid=(count,),
        out_shape=jax.ShapeDtypeStruct((rows, fields, count * GROUP, width), jnp.bfloat16),
        in_specs=[
            pl.BlockSpec((GROUP, fields, rows, width), lambda i: (first + i, 0, 0, 0)),
            pl.BlockSpec((edge, HALO, width), lambda i: (i, 0, 0)),
            pl.BlockSpec((edge, HALO, width), lambda i: (i, 0, 0)),
            pl.BlockSpec((4, HALO, width), lambda i: (edge // 4, 0, 0)),
            pl.BlockSpec((4, HALO, width), lambda i: (edge // 4, 0, 0)),
            whole(depth),
            whole(mask),
            whole(swap),
            whole(swap_ends),
        ],
        out_specs=pl.BlockSpec((rows, fields, GROUP, width), lambda i: (0, 0, i, 0)),
        scratch_shapes=[
            pltpu.VMEM((fields, padded, GROUP, width), jnp.float32),
            pltpu.VMEM((edge, 2 * HALO, width), jnp.float32),
            pltpu.VMEM((padded, 8, width), jnp.float32),
            pltpu.VMEM((padded, 8, width), jnp.float32),
            rows_of(rows + 6),
            rows_of(rows + 4),
            rows_of(rows + 4),
            rows_of(rows + 2),
        ],
        compiler_params=pltpu.CompilerParams(vmem_limit_bytes=VMEM_BYTES),
        cost_estimate=pl.CostEstimate(
            flops=60 * count * GROUP * rows * width,
            bytes_accessed=2 * 2 * count * GROUP * fields * rows * width,
            transcendentals=0,
        ),
        name="forecast",
    )(factors, low, high, static_low, static_high, depth, mask, swap, swap_ends)


def all_columns(chunk_refs, fault_ref, j):
    own = [ref[:, j, 0] for ref in chunk_refs]
    joined = jnp.concatenate(own, axis=1)
    return joined.reshape(-1, joined.shape[-1]), fault_ref[0, j]


def rotate_kernel(count, *refs):
    chunk_refs = refs[:count]
    fault_ref, turn_ref, out_ref = refs[count:]
    columns = jnp.concatenate(all_columns(chunk_refs, fault_ref, 0), axis=0)
    value = jnp.dot(turn_ref[...], columns, preferred_element_type=jnp.float32)
    out_ref[...] = value.astype(jnp.bfloat16).reshape(out_ref.shape)


def by_part(chunks, parts):
    return [c.reshape((parts, c.shape[0] // parts) + c.shape[1:]) for c in chunks]


def rotate_fields(first, fields, chunks, fault, turn, parts):
    width = chunks[0].shape[-1]
    each = chunks[0].shape[0] // parts
    kept = turn.shape[0]
    noise = fault.shape[2]
    modes = kept // parts
    views = by_part(chunks, parts)
    return pl.pallas_call(
        functools.partial(rotate_kernel, len(views)),
        grid=(fields, each),
        out_shape=jax.ShapeDtypeStruct((parts, fields, each, modes, width), jnp.bfloat16),
        in_specs=[
            pl.BlockSpec((parts, 1, 1, v.shape[3], width), lambda f, j: (0, j, first + f, 0, 0))
            for v in views
        ] + [
            pl.BlockSpec((1, 1, noise, width), lambda f, j: (first + f, j, 0, 0)),
            pl.BlockSpec(turn.shape, lambda f, j: (0, 0)),
        ],
        out_specs=pl.BlockSpec((parts, 1, 1, modes, width), lambda f, j: (0, f, j, 0, 0)),
        compiler_params=pltpu.CompilerParams(vmem_limit_bytes=VMEM_BYTES),
        cost_estimate=pl.CostEstimate(
            flops=2 * fields * each * width * kept * turn.shape[1],
            bytes_accessed=2 * fields * each * width * (kept + turn.shape[1]),
            transcendentals=0,
        ),
        name="rotate",
    )(*views, fault, turn)


def gram_kernel(count, each, *refs):
    chunk_refs = refs[:count]
    fault_ref, turn_ref, out_ref, trace_ref = refs[count:]
    pairs = [all_columns(chunk_refs, fault_ref, j) for j in range(each)]
    columns = jnp.concatenate(
        [jnp.concatenate([prior, fault], axis=0) for prior, fault in pairs], axis=1
    )
    value = lax.dot_general(
        columns, columns, (((1,), (1,)), ((), ())), preferred_element_type=jnp.float32
    )
    step = pl.program_id(0)

    @pl.when(step == 0)
    def _():
        out_ref[...] = value

    @pl.when(step > 0)
    def _():
        out_ref[...] += value

    @pl.when(step == pl.num_programs(0) - 1)
    def _():
        gram = out_ref[...]
        size = gram.shape[0]
        row = lax.broadcasted_iota(jnp.int32, gram.shape, 0)
        column = lax.broadcasted_iota(jnp.int32, gram.shape, 1)
        diagonal = jnp.where(row == column, gram, 0.0)
        trace_ref[0] = jnp.sum(diagonal.reshape(-1, 8, size), axis=0)
        turn = turn_ref[...]
        turned = 0.0
        for _ in range(3):
            piece = gram.astype(jnp.bfloat16)
            turned = turned + jnp.dot(turn, piece, preferred_element_type=jnp.float32)
            gram = gram - piece.astype(jnp.float32)
        kept = turned * turn.astype(jnp.float32)
        trace_ref[1] = jnp.sum(kept.reshape(-1, 8, size), axis=0)


def local_gram(chunks, fault, turn, parts):
    width = chunks[0].shape[-1]
    each = chunks[0].shape[0] // parts
    noise = fault.shape[2]
    columns = turn.shape[1]
    views = by_part(chunks, parts)
    return pl.pallas_call(
        functools.partial(gram_kernel, len(views), each),
        grid=(3,),
        out_shape=(
            jax.ShapeDtypeStruct((columns, columns), jnp.float32),
            jax.ShapeDtypeStruct((2, 8, columns), jnp.float32),
        ),
        in_specs=[
            pl.BlockSpec((parts, each, 1, v.shape[3], width), lambda f: (0, 0, f, 0, 0))
            for v in views
        ] + [
            pl.BlockSpec((1, each, noise, width), lambda f: (f, 0, 0, 0)),
            pl.BlockSpec(turn.shape, lambda f: (0, 0)),
        ],
        out_specs=(
            pl.BlockSpec((columns, columns), lambda f: (0, 0)),
            pl.BlockSpec((2, 8, columns), lambda f: (0, 0, 0)),
        ),
        compiler_params=pltpu.CompilerParams(vmem_limit_bytes=VMEM_BYTES),
        cost_estimate=pl.CostEstimate(
            flops=2 * 3 * each * width * columns * columns,
            bytes_accessed=2 * 3 * each * width * columns,
            transcendentals=0,
        ),
        name="gram",
    )(*views, fault, turn)


def finish_kernel(aliased, scale_ref, swap_ref, x_ref, *refs):
    out_ref = refs[aliased]
    parts, _, each, _, width = x_ref.shape
    rows = parts * each
    scale = scale_ref[0, 0]
    value = x_ref[...].reshape(rows * GROUP, width)
    for top in range(0, rows, GROUP):
        block = value[top * GROUP:(top + GROUP) * GROUP]
        block = scale * jnp.dot(swap_ref[...], block, preferred_element_type=jnp.float32)
        out_ref[:, 0, top:top + GROUP, :] = block.astype(jnp.bfloat16).reshape(GROUP, GROUP, width)


def finish_field(field, arrived, place, scale, previous):
    parts, _, each, modes, width = arrived.shape
    rows = parts * each
    swap = swap_matrix(GROUP, GROUP)
    operands = [scale.reshape(1, 1), swap, arrived]
    specs = [
        pl.BlockSpec(memory_space=pltpu.SMEM),
        pl.BlockSpec(swap.shape, lambda m: (0, 0)),
        pl.BlockSpec((parts, 1, each, GROUP, width), lambda m: (0, place, 0, m, 0)),
    ]
    aliases = {}
    if previous is not None:
        operands.append(previous)
        specs.append(pl.BlockSpec(memory_space=pl.ANY))
        aliases = {3: 0}
    return pl.pallas_call(
        functools.partial(finish_kernel, len(aliases)),
        grid=(modes // GROUP,),
        out_shape=jax.ShapeDtypeStruct((modes, 3, rows, width), jnp.bfloat16),
        in_specs=specs,
        out_specs=pl.BlockSpec((GROUP, 1, rows, width), lambda m: (m, field, 0, 0)),
        input_output_aliases=aliases,
        compiler_params=pltpu.CompilerParams(vmem_limit_bytes=VMEM_BYTES),
        cost_estimate=pl.CostEstimate(
            flops=modes * rows * width,
            bytes_accessed=4 * modes * rows * width,
            transcendentals=0,
        ),
        name="finish",
    )(*operands)


def total_over(value, axis, paired):
    count = lax.axis_size(axis)
    if count & (count - 1):
        return lax.psum(value, axis)
    step = 1
    while step < count and paired:
        value = value + lax.ppermute(value, axis, [(i, i ^ step) for i in range(count)])
        step, paired = 2 * step, paired - 1
    others = [
        lax.ppermute(value, axis, [(i, i ^ k) for i in range(count)])
        for k in range(step, count, step)
    ]
    return value + sum(others) if others else value


def edges(blocks):
    count = lax.axis_size("space")
    forward = [(i, i + 1) for i in range(count - 1)]
    backward = [(target, source) for source, target in forward]
    last = jnp.concatenate([block[:, -HALO:] for block in blocks])
    first = jnp.concatenate([block[:, :HALO] for block in blocks])
    return lax.ppermute(last, "space", forward), lax.ppermute(first, "space", backward)


def shards(sqrt_factors, model_error, water_depth, sea_mask, givens_transform):
    modes, fields, rows, width = sqrt_factors.shape
    parts = lax.axis_size("mode")
    count = modes // GROUP
    flat = sqrt_factors.reshape(modes * fields, rows, width)
    edge = GROUP * fields
    static = jnp.stack(split_pieces(water_depth) + [sea_mask.astype(jnp.bfloat16)])
    head = edges([flat[:edge], static])
    tail = edges([flat[edge:]])
    static = (*head, water_depth, sea_mask)

    swap = functools.partial(
        lax.all_to_all, axis_name="mode", split_axis=0, concat_axis=0, tiled=True
    )
    chunks = [
        swap(forecast_groups(0, 1, sqrt_factors, *head, *static)),
        swap(forecast_groups(1, count - 1, sqrt_factors, *tail, *static)),
    ]

    fault = model_error.transpose(1, 2, 0, 3)
    turn = givens_transform.T
    head_field = rotate_fields(0, 1, chunks, fault, turn, parts)
    arrived = [swap(head_field)]
    gram, traces = local_gram(chunks, fault, turn, parts)
    traces = jnp.sum(traces, axis=(1, 2))
    traces = total_over(total_over(traces, "space", 0), "mode", 1)
    other_fields = rotate_fields(1, 2, chunks, fault, turn, parts)
    other_fields, traces = lax.optimization_barrier((other_fields, traces))
    arrived.append(swap(other_fields))
    inflation = jnp.sqrt(traces[0] / traces[1])
    cell_count = float(fields * rows * lax.axis_size("space") * width)

    gram = lax.psum_scatter(gram, "space", scatter_dimension=0, tiled=True)
    gram = lax.psum_scatter(gram, "mode", scatter_dimension=0, tiled=True) / cell_count

    reduced = None
    for field in range(fields):
        reduced = finish_field(field, arrived[min(field, 1)], max(field - 1, 0), inflation, reduced)
    return (reduced, gram, inflation)


def solution(mesh):
    in_specs = (
        P("mode", None, "space", None),
        P(None, None, ("space", "mode"), None),
        P("space", None),
        P("space", None),
        P(),
    )
    out_specs = (P("mode", None, "space", None), P(("space", "mode"), None), P())
    return jax.shard_map(shards, mesh=mesh, in_specs=in_specs, out_specs=out_specs, check_vma=False)
```

```python
import functools

import jax
import jax.numpy as jnp
import numpy as np
from jax import lax
from jax.experimental import pallas as pl
from jax.experimental.pallas import tpu as pltpu
from jax.sharding import PartitionSpec as P

flux_coef = 0.2
slope_coef = 0.2
turn_coef = 0.1
keep_coef = 0.95

GROUP = 16
HALO = 4
LANES = 128
VMEM_BYTES = 48 * 1024 * 1024


def column_diff(tiles):
    lane = lax.broadcasted_iota(jnp.int32, tiles[0].shape, 1)
    from_left = [pltpu.roll(tile, 1, 1) for tile in tiles]
    from_right = [pltpu.roll(tile, LANES - 1, 1) for tile in tiles]
    zero = jnp.zeros_like(tiles[0])
    out = []
    for t in range(len(tiles)):
        left = from_left[t - 1] if t > 0 else zero
        right = from_right[t + 1] if t + 1 < len(tiles) else zero
        previous = jnp.where(lane == 0, left, from_left[t])
        following = jnp.where(lane == LANES - 1, right, from_right[t])
        out.append(following - previous)
    return out


def partner(me, k):
    return jnp.bitwise_xor(me, k)


def swap_matrix(inner, outer):
    place = np.arange(inner * outer).reshape(outer, inner).T.reshape(-1)
    matrix = np.zeros((inner * outer, inner * outer), np.float32)
    matrix[np.arange(inner * outer), place] = 1.0
    return jnp.asarray(matrix, jnp.bfloat16)


def split_pieces(value):
    pieces = []
    for _ in range(3):
        piece = lax.reduce_precision(value, 8, 7)
        pieces.append(piece.astype(jnp.bfloat16))
        value = value - piece
    return pieces


def block_of(count):
    return max(size for size in range(1, 7) if count % size == 0)


def forecast_kernel(parts, me_ref, x_ref, low_ref, high_ref, low_static, high_static, depth_ref,
                    mask_ref, swap_ref, swap_ends_ref, *refs):
    out_refs = refs[:parts]
    cells, ends, depth, wet, surf1, east1, north1, surf2 = refs[parts:]
    _, fields, rows, width = x_ref.shape
    tiles = width // LANES
    spots = [slice(t * LANES, (t + 1) * LANES) for t in range(tiles)]

    ends[:, :HALO] = low_ref[...].astype(jnp.float32)
    ends[:, HALO:] = high_ref[...].astype(jnp.float32)
    for field in range(fields):
        for top in range(0, rows, GROUP):
            block = x_ref[:, field, top:top + GROUP, :].reshape(GROUP * GROUP, width)
            block = jnp.dot(swap_ref[...], block, preferred_element_type=jnp.float32)
            cells[field, HALO + top:HALO + top + GROUP] = block.reshape(GROUP, GROUP, width)
        block = jnp.concatenate([ends[m * fields + field] for m in range(GROUP)], axis=0)
        block = jnp.dot(
            swap_ends_ref[...], block.astype(jnp.bfloat16), preferred_element_type=jnp.float32
        ).reshape(2 * HALO, GROUP, width)
        cells[field, :HALO] = block[:HALO]
        cells[field, HALO + rows:] = block[HALO:]

    def place_static(place, depth_row, wet_row):
        depth[place] = jnp.broadcast_to(flux_coef * depth_row, (8, width))
        wet[place] = jnp.broadcast_to(wet_row, (8, width))

    for static, first in ((low_static, 0), (high_static, HALO + rows)):
        value = static[...].astype(jnp.float32)
        level = value[0] + value[1] + value[2]
        for j in range(HALO):
            place_static(first + j, level[j:j + 1], value[3, j:j + 1])
    for top in range(0, rows, 8):
        level = depth_ref[top:top + 8]
        sea = mask_ref[top:top + 8].astype(jnp.float32)
        for j in range(8):
            place_static(HALO + top + j, level[j:j + 1], sea[j:j + 1])

    def get(ref, i):
        return [ref[i, :, spot] for spot in spots]

    def get_field(field, i):
        return [cells[field, i + HALO, :, spot] for spot in spots]

    def get_static(ref, i):
        parts = [ref[i + HALO, :, spot] for spot in spots]
        return [jnp.concatenate([part] * (GROUP // 8), axis=0) for part in parts]

    def put(ref, i, values):
        for spot, value in zip(spots, values):
            ref[i, :, spot] = value

    def times(one, other):
        return [a * b for a, b in zip(one, other)]

    def over_rows(first, last, body):
        size = block_of(last - first)

        def block(k, carry):
            body(first + k * size, size)
            return carry

        lax.fori_loop(0, (last - first) // size, block, 0)

    def surfaces(i, size, surface_at, east_at, north_at, put_at):
        flux = {j: times(get_static(depth, i + j), north_at(i + j)) for j in (-1, 0)}
        for j in range(size):
            flux[j + 1] = times(get_static(depth, i + j + 1), north_at(i + j + 1))
            sides = column_diff(times(get_static(depth, i + j), east_at(i + j)))
            sea, surface = get_static(wet, i + j), surface_at(i + j)
            put_at(i + j, [
                sea[t] * (surface[t] - (sides[t] + (flux[j + 1][t] - flux[j - 1][t])))
                for t in range(tiles)
            ])

    def flows(i, size, surface_at, east_at, north_at, put_at):
        surface = {j: surface_at(i + j) for j in (-1, 0)}
        for j in range(size):
            surface[j + 1] = surface_at(i + j + 1)
            sides = column_diff(surface[j])
            sea, east, north = get_static(wet, i + j), east_at(i + j), north_at(i + j)
            put_at(i + j, surface[j], [
                sea[t] * (keep_coef * east[t] + turn_coef * north[t] - slope_coef * sides[t])
                for t in range(tiles)
            ], [
                sea[t] * (keep_coef * north[t] - turn_coef * east[t]
                          - slope_coef * (surface[j + 1][t] - surface[j - 1][t]))
                for t in range(tiles)
            ])

    def first_surface(i, size):
        surfaces(
            i, size, lambda r: get_field(0, r), lambda r: get_field(1, r),
            lambda r: get_field(2, r), lambda r, value: put(surf1, r + 3, value),
        )

    def first_flow(i, size):
        def put_flow(r, surface, east, north):
            put(east1, r + 2, east)
            put(north1, r + 2, north)

        flows(
            i, size, lambda r: get(surf1, r + 3), lambda r: get_field(1, r),
            lambda r: get_field(2, r), put_flow,
        )

    def second_surface(i, size):
        surfaces(
            i, size, lambda r: get(surf1, r + 3), lambda r: get(east1, r + 2),
            lambda r: get(north1, r + 2), lambda r, value: put(surf2, r + 1, value),
        )

    over_rows(-3, rows + 3, first_surface)
    over_rows(-2, rows + 2, first_flow)
    over_rows(-1, rows + 1, second_surface)

    each = rows // parts
    for k in range(parts):
        start = partner(me_ref[0, 0], k) * each

        def put_out(r, surface, east, north):
            for field, values in enumerate((surface, east, north)):
                for spot, value in zip(spots, values):
                    out_refs[k][r - start, field, :, spot] = value.astype(jnp.bfloat16)

        size = block_of(each)
        for first in range(0, each, size):
            flows(
                start + first, size, lambda r: get(surf2, r + 1), lambda r: get(east1, r + 2),
                lambda r: get(north1, r + 2), put_out,
            )


def forecast_groups(first, count, parts, me, factors, low, high, skip, static_low, static_high, depth, mask):
    modes, fields, rows, width = factors.shape
    padded = rows + 2 * HALO
    edge = GROUP * fields
    swap, swap_ends = swap_matrix(GROUP, GROUP), swap_matrix(2 * HALO, GROUP)

    def rows_of(count):
        return pltpu.VMEM((count, GROUP, width), jnp.float32)

    def whole(value):
        return pl.BlockSpec(value.shape, lambda i: (0,) * value.ndim)

    return pl.pallas_call(
        functools.partial(forecast_kernel, parts),
        grid=(count,),
        out_shape=[
            jax.ShapeDtypeStruct((rows // parts, fields, count * GROUP, width), jnp.bfloat16)
            for _ in range(parts)
        ],
        in_specs=[
            pl.BlockSpec(memory_space=pltpu.SMEM),
            pl.BlockSpec((GROUP, fields, rows, width), lambda i: (first + i, 0, 0, 0)),
            pl.BlockSpec((edge, HALO, width), lambda i: (skip + i, 0, 0)),
            pl.BlockSpec((edge, HALO, width), lambda i: (skip + i, 0, 0)),
            pl.BlockSpec((4, HALO, width), lambda i: (edge // 4, 0, 0)),
            pl.BlockSpec((4, HALO, width), lambda i: (edge // 4, 0, 0)),
            whole(depth),
            whole(mask),
            whole(swap),
            whole(swap_ends),
        ],
        out_specs=[
            pl.BlockSpec((rows // parts, fields, GROUP, width), lambda i: (0, 0, i, 0))
            for _ in range(parts)
        ],
        scratch_shapes=[
            pltpu.VMEM((fields, padded, GROUP, width), jnp.float32),
            pltpu.VMEM((edge, 2 * HALO, width), jnp.float32),
            pltpu.VMEM((padded, 8, width), jnp.float32),
            pltpu.VMEM((padded, 8, width), jnp.float32),
            rows_of(rows + 6),
            rows_of(rows + 4),
            rows_of(rows + 4),
            rows_of(rows + 2),
        ],
        compiler_params=pltpu.CompilerParams(vmem_limit_bytes=VMEM_BYTES),
        cost_estimate=pl.CostEstimate(
            flops=60 * count * GROUP * rows * width,
            bytes_accessed=2 * 2 * count * GROUP * fields * rows * width,
            transcendentals=0,
        ),
        name="forecast",
    )(me, factors, low, high, static_low, static_high, depth, mask, swap, swap_ends)


def rotate_kernel(parts, count, *refs):
    block_refs = refs[:parts * count]
    fault_ref, turn_ref = refs[parts * count:parts * count + 2]
    out_refs = refs[parts * count + 2:]
    columns = jnp.concatenate([ref[0, 0] for ref in block_refs] + [fault_ref[0, 0]], axis=0)
    value = jnp.dot(turn_ref[...], columns, preferred_element_type=jnp.float32)
    value = value.astype(jnp.bfloat16)
    modes = value.shape[0] // parts
    for k in range(parts):
        out_refs[k][0] = value[k * modes:(k + 1) * modes]


def rotate_field(field, chunks, fault, turn):
    parts = len(chunks[0])
    each, _, _, width = chunks[0][0].shape
    kept = turn.shape[0]
    noise = fault.shape[2]
    modes = kept // parts
    views = [chunk[k] for k in range(parts) for chunk in chunks]
    return pl.pallas_call(
        functools.partial(rotate_kernel, parts, len(chunks)),
        grid=(each,),
        out_shape=[
            jax.ShapeDtypeStruct((each, modes, width), jnp.bfloat16) for _ in range(parts)
        ],
        in_specs=[
            pl.BlockSpec((1, 1, v.shape[2], width), lambda j: (j, field, 0, 0)) for v in views
        ] + [
            pl.BlockSpec((1, 1, noise, width), lambda j: (field, j, 0, 0)),
            pl.BlockSpec(turn.shape, lambda j: (0, 0)),
        ],
        out_specs=[
            pl.BlockSpec((1, modes, width), lambda j: (j, 0, 0)) for _ in range(parts)
        ],
        compiler_params=pltpu.CompilerParams(vmem_limit_bytes=VMEM_BYTES),
        cost_estimate=pl.CostEstimate(
            flops=2 * each * width * kept * turn.shape[1],
            bytes_accessed=2 * each * width * (kept + turn.shape[1]),
            transcendentals=0,
        ),
        name="rotate",
    )(*views, fault, turn)


def gram_kernel(parts, count, me_ref, *refs):
    block_refs = refs[:parts * count]
    fault_ref, turn_ref, out_ref, trace_ref, columns = refs[parts * count:]
    each, width = block_refs[0].shape[0], block_refs[0].shape[-1]
    modes = sum(ref.shape[2] for ref in block_refs[:count])
    for j in range(each):
        spot = slice(j * width, (j + 1) * width)
        for k in range(parts):
            block = jnp.concatenate([ref[j, 0] for ref in block_refs[k * count:(k + 1) * count]], axis=0)
            first = pl.multiple_of(partner(me_ref[0, 0], k) * modes, GROUP)
            columns[pl.ds(first, modes), spot] = block
        columns[parts * modes:, spot] = fault_ref[0, j]
    value = lax.dot_general(
        columns[...], columns[...], (((1,), (1,)), ((), ())), preferred_element_type=jnp.float32
    )
    step = pl.program_id(0)

    @pl.when(step == 0)
    def _():
        out_ref[...] = value

    @pl.when(step > 0)
    def _():
        out_ref[...] += value

    @pl.when(step == pl.num_programs(0) - 1)
    def _():
        gram = out_ref[...]
        size = gram.shape[0]
        row = lax.broadcasted_iota(jnp.int32, gram.shape, 0)
        column = lax.broadcasted_iota(jnp.int32, gram.shape, 1)
        diagonal = jnp.where(row == column, gram, 0.0)
        trace_ref[0] = jnp.sum(diagonal.reshape(-1, 8, size), axis=0)
        turn = turn_ref[...]
        turned = 0.0
        for _ in range(3):
            piece = gram.astype(jnp.bfloat16)
            turned = turned + jnp.dot(turn, piece, preferred_element_type=jnp.float32)
            gram = gram - piece.astype(jnp.float32)
        kept = turned * turn.astype(jnp.float32)
        trace_ref[1] = jnp.sum(kept.reshape(-1, 8, size), axis=0)


def local_gram(chunks, fault, turn, me):
    parts = len(chunks[0])
    each, fields, _, width = chunks[0][0].shape
    noise = fault.shape[2]
    columns = turn.shape[1]
    views = [chunk[k] for k in range(parts) for chunk in chunks]
    return pl.pallas_call(
        functools.partial(gram_kernel, parts, len(chunks)),
        grid=(fields,),
        out_shape=(
            jax.ShapeDtypeStruct((columns, columns), jnp.float32),
            jax.ShapeDtypeStruct((2, 8, columns), jnp.float32),
        ),
        in_specs=[pl.BlockSpec(memory_space=pltpu.SMEM)] + [
            pl.BlockSpec((each, 1, v.shape[2], width), lambda f: (0, f, 0, 0)) for v in views
        ] + [
            pl.BlockSpec((1, each, noise, width), lambda f: (f, 0, 0, 0)),
            pl.BlockSpec(turn.shape, lambda f: (0, 0)),
        ],
        out_specs=(
            pl.BlockSpec((columns, columns), lambda f: (0, 0)),
            pl.BlockSpec((2, 8, columns), lambda f: (0, 0, 0)),
        ),
        scratch_shapes=[pltpu.VMEM((columns, each * width), jnp.bfloat16)],
        compiler_params=pltpu.CompilerParams(vmem_limit_bytes=VMEM_BYTES),
        cost_estimate=pl.CostEstimate(
            flops=2 * fields * each * width * columns * columns,
            bytes_accessed=2 * fields * each * width * columns,
            transcendentals=0,
        ),
        name="gram",
    )(me, *views, fault, turn)


def finish_kernel(parts, aliased, me_ref, scale_ref, swap_ref, *refs):
    block_refs = refs[:parts]
    out_ref, cells = refs[parts + aliased:]
    each, _, width = block_refs[0].shape
    rows = parts * each
    for k in range(parts):
        first = pl.multiple_of(partner(me_ref[0, 0], k) * (each * GROUP), GROUP)
        cells[pl.ds(first, each * GROUP)] = block_refs[k][...].reshape(each * GROUP, width)
    scale = scale_ref[0, 0]
    for top in range(0, rows, GROUP):
        block = cells[top * GROUP:(top + GROUP) * GROUP]
        block = scale * jnp.dot(swap_ref[...], block, preferred_element_type=jnp.float32)
        out_ref[:, 0, top:top + GROUP, :] = block.astype(jnp.bfloat16).reshape(GROUP, GROUP, width)


def finish_field(field, fields, arrived, me, scale, previous):
    parts = len(arrived)
    each, modes, width = arrived[0].shape
    rows = parts * each
    swap = swap_matrix(GROUP, GROUP)
    operands = [me, scale.reshape(1, 1), swap, *arrived]
    specs = [
        pl.BlockSpec(memory_space=pltpu.SMEM),
        pl.BlockSpec(memory_space=pltpu.SMEM),
        pl.BlockSpec(swap.shape, lambda m: (0, 0)),
    ] + [pl.BlockSpec((each, GROUP, width), lambda m: (0, m, 0)) for _ in arrived]
    aliases = {}
    if previous is not None:
        aliases = {len(operands): 0}
        operands.append(previous)
        specs.append(pl.BlockSpec(memory_space=pl.ANY))
    return pl.pallas_call(
        functools.partial(finish_kernel, parts, len(aliases)),
        grid=(modes // GROUP,),
        out_shape=jax.ShapeDtypeStruct((modes, fields, rows, width), jnp.bfloat16),
        in_specs=specs,
        out_specs=pl.BlockSpec((GROUP, 1, rows, width), lambda m: (m, field, 0, 0)),
        scratch_shapes=[pltpu.VMEM((rows * GROUP, width), jnp.bfloat16)],
        input_output_aliases=aliases,
        compiler_params=pltpu.CompilerParams(vmem_limit_bytes=VMEM_BYTES),
        cost_estimate=pl.CostEstimate(
            flops=modes * rows * width,
            bytes_accessed=4 * modes * rows * width,
            transcendentals=0,
        ),
        name="finish",
    )(*operands)


def exchange(blocks):
    parts = len(blocks)
    arrived = {0: blocks[0]}
    for k in sorted(range(1, parts), reverse=True):
        arrived[k] = lax.ppermute(blocks[k], "mode", [(i, i ^ k) for i in range(parts)])
    return [arrived[k] for k in range(parts)]


def in_partner_order(value, me, parts, size):
    blocks = [
        lax.dynamic_slice_in_dim(value, partner(me, k) * size, size, axis=0) for k in range(parts)
    ]
    return jnp.concatenate(blocks + [value[parts * size:]], axis=0)


def total_over(value, axis, paired):
    count = lax.axis_size(axis)
    if count & (count - 1):
        return lax.psum(value, axis)
    step = 1
    while step < count and paired:
        value = value + lax.ppermute(value, axis, [(i, i ^ step) for i in range(count)])
        step, paired = 2 * step, paired - 1
    others = [
        lax.ppermute(value, axis, [(i, i ^ k) for i in range(count)])
        for k in range(step, count, step)
    ]
    return value + sum(others) if others else value


def edges(blocks):
    count = lax.axis_size("space")
    forward = [(i, i + 1) for i in range(count - 1)]
    backward = [(target, source) for source, target in forward]
    last = jnp.concatenate([block[:, -HALO:] for block in blocks])
    first = jnp.concatenate([block[:, :HALO] for block in blocks])
    return lax.ppermute(last, "space", forward), lax.ppermute(first, "space", backward)


def shards(sqrt_factors, model_error, water_depth, sea_mask, givens_transform):
    modes, fields, rows, width = sqrt_factors.shape
    parts = lax.axis_size("mode")
    count = modes // GROUP
    flat = sqrt_factors.reshape(modes * fields, rows, width)
    edge = GROUP * fields
    static = jnp.stack(split_pieces(water_depth) + [sea_mask.astype(jnp.bfloat16)])
    head = edges([flat[:edge], static])
    tail = edges([flat[edge:]])
    static = (*head, water_depth, sea_mask)
    index = lax.axis_index("mode")
    me = index.reshape(1, 1)

    chunks, first = [], 0
    for size in (1, 1, count - 2):
        if size > 0:
            low_high = (*head, 0) if first == 0 else (*tail, first - 1)
            chunks.append(exchange(
                forecast_groups(first, size, parts, me, sqrt_factors, *low_high, *static)
            ))
            first += size

    fault = model_error.transpose(1, 2, 0, 3)
    turn = givens_transform.T
    ordered = in_partner_order(givens_transform, index, parts, modes).T
    ordered = in_partner_order(ordered, index, parts, modes)
    arrived = [exchange(rotate_field(f, chunks, fault, ordered)) for f in range(fields - 1)]
    gram, traces = local_gram(chunks, fault, turn, me)
    traces = jnp.sum(traces, axis=(1, 2))
    traces = total_over(total_over(traces, "space", 0), "mode", 1)
    last = rotate_field(fields - 1, chunks, fault, ordered)
    *last, traces = lax.optimization_barrier((*last, traces))
    arrived.append(exchange(last))
    inflation = jnp.sqrt(traces[0] / traces[1])
    cell_count = float(fields * rows * lax.axis_size("space") * width)

    gram = lax.psum_scatter(gram, "space", scatter_dimension=0, tiled=True)
    gram = lax.psum_scatter(gram, "mode", scatter_dimension=0, tiled=True) / cell_count

    reduced = None
    for field in range(fields):
        reduced = finish_field(field, fields, arrived[field], me, inflation, reduced)
    return (reduced, gram, inflation)


def solution(mesh):
    in_specs = (
        P("mode", None, "space", None),
        P(None, None, ("space", "mode"), None),
        P("space", None),
        P("space", None),
        P(),
    )
    out_specs = (P("mode", None, "space", None), P(("space", "mode"), None), P())
    return jax.shard_map(shards, mesh=mesh, in_specs=in_specs, out_specs=out_specs, check_vma=False)
```

```python
import functools

import jax
import jax.numpy as jnp
import numpy as np
from jax import lax
from jax.experimental import pallas as pl
from jax.experimental.pallas import tpu as pltpu
from jax.sharding import PartitionSpec as P

flux_coef = 0.2
slope_coef = 0.2
turn_coef = 0.1
keep_coef = 0.95

GROUP = 16
HALO = 4
LANES = 128
VMEM_BYTES = 48 * 1024 * 1024


def column_diff(tiles):
    lane = lax.broadcasted_iota(jnp.int32, tiles[0].shape, 1)
    from_left = [pltpu.roll(tile, 1, 1) for tile in tiles]
    from_right = [pltpu.roll(tile, LANES - 1, 1) for tile in tiles]
    zero = jnp.zeros_like(tiles[0])
    out = []
    for t in range(len(tiles)):
        left = from_left[t - 1] if t > 0 else zero
        right = from_right[t + 1] if t + 1 < len(tiles) else zero
        previous = jnp.where(lane == 0, left, from_left[t])
        following = jnp.where(lane == LANES - 1, right, from_right[t])
        out.append(following - previous)
    return out


def swap_matrix(inner, outer):
    place = np.arange(inner * outer).reshape(outer, inner).T.reshape(-1)
    matrix = np.zeros((inner * outer, inner * outer), np.float32)
    matrix[np.arange(inner * outer), place] = 1.0
    return jnp.asarray(matrix, jnp.bfloat16)


def in_hbm(shape, dtype):
    return pltpu.HBM(shape, dtype)


def cut_edges_kernel(fixed, *refs):
    first_ref, last_ref = refs[:2]
    out_first, out_last = refs[-2:]
    group, fields = first_ref.shape[:2]
    for ref, out, low in ((first_ref, out_first, 0), (last_ref, out_last, GROUP - HALO)):
        for m in range(group):
            for field in range(fields):
                edge = ref[m, field].astype(jnp.float32)[low:low + HALO]
                out[m * fields + field] = edge.astype(jnp.bfloat16)
    if fixed:
        depth_ref, mask_ref = refs[2:4]
        for out, low in ((out_first, 0), (out_last, depth_ref.shape[0] - HALO)):
            rest = depth_ref[low:low + HALO]
            for piece in range(3):
                part = rest.astype(jnp.bfloat16)
                out[group * fields + piece] = part
                rest = rest - part.astype(jnp.float32)
            out[group * fields + 3] = mask_ref[low:low + HALO].astype(jnp.float32).astype(jnp.bfloat16)


def cut_edges(first, groups, factors, fixed):
    _, fields, rows, width = factors.shape
    size = GROUP * groups if fixed else GROUP
    steps = 1 if fixed else groups
    count = size * steps * fields + (4 if fixed else 0)
    block = size * fields + (4 if fixed else 0)
    out = jax.ShapeDtypeStruct((count, HALO, width), jnp.bfloat16)
    return pl.pallas_call(
        functools.partial(cut_edges_kernel, bool(fixed)),
        grid=(steps,),
        out_shape=(out, out),
        in_specs=[
            pl.BlockSpec((size, fields, GROUP, width), lambda i: (first // (size // GROUP) + i, 0, 0, 0)),
            pl.BlockSpec((size, fields, GROUP, width),
                         lambda i: (first // (size // GROUP) + i, 0, rows // GROUP - 1, 0)),
        ] + [pl.BlockSpec(value.shape, lambda i: (0, 0)) for value in fixed],
        out_specs=[pl.BlockSpec((block, HALO, width), lambda i: (i, 0, 0))] * 2,
        compiler_params=pltpu.CompilerParams(vmem_limit_bytes=VMEM_BYTES),
        cost_estimate=pl.CostEstimate(
            flops=0, bytes_accessed=5 * count * HALO * width * 2, transcendentals=0
        ),
        name="cut_edges",
    )(factors, factors, *fixed)


def block_of(count):
    return max(size for size in range(1, 7) if count % size == 0)


def forecast_kernel(x_ref, low_ref, high_ref, low_static, high_static, depth_ref, mask_ref,
                    swap_ref, swap_ends_ref, *refs):
    out_ref, cells, ends, depth, wet, surf1, east1, north1, surf2 = refs[-9:]
    _, fields, rows, width = x_ref.shape
    tiles = width // LANES
    spots = [slice(t * LANES, (t + 1) * LANES) for t in range(tiles)]

    ends[:, :HALO] = low_ref[...].astype(jnp.float32)
    ends[:, HALO:] = high_ref[...].astype(jnp.float32)
    for field in range(fields):
        for top in range(0, rows, GROUP):
            block = x_ref[:, field, top:top + GROUP, :].reshape(GROUP * GROUP, width)
            block = jnp.dot(swap_ref[...], block, preferred_element_type=jnp.float32)
            cells[field, HALO + top:HALO + top + GROUP] = block.reshape(GROUP, GROUP, width)
        block = jnp.concatenate([ends[m * fields + field] for m in range(GROUP)], axis=0)
        block = jnp.dot(
            swap_ends_ref[...], block.astype(jnp.bfloat16), preferred_element_type=jnp.float32
        ).reshape(2 * HALO, GROUP, width)
        cells[field, :HALO] = block[:HALO]
        cells[field, HALO + rows:] = block[HALO:]

    def place_static(place, depth_row, wet_row):
        depth[place] = jnp.broadcast_to(flux_coef * depth_row, (8, width))
        wet[place] = jnp.broadcast_to(wet_row, (8, width))

    for static, first in ((low_static, 0), (high_static, HALO + rows)):
        value = static[...].astype(jnp.float32)
        level = value[0] + value[1] + value[2]
        for j in range(HALO):
            place_static(first + j, level[j:j + 1], value[3, j:j + 1])
    for top in range(0, rows, 8):
        level = depth_ref[top:top + 8]
        sea = mask_ref[top:top + 8].astype(jnp.float32)
        for j in range(8):
            place_static(HALO + top + j, level[j:j + 1], sea[j:j + 1])

    def get(ref, i):
        return [ref[i, :, spot] for spot in spots]

    def get_field(field, i):
        return [cells[field, i + HALO, :, spot] for spot in spots]

    def get_static(ref, i):
        parts = [ref[i + HALO, :, spot] for spot in spots]
        return [jnp.concatenate([part] * (GROUP // 8), axis=0) for part in parts]

    def put(ref, i, values):
        for spot, value in zip(spots, values):
            ref[i, :, spot] = value

    def times(one, other):
        return [a * b for a, b in zip(one, other)]

    def over_rows(first, last, body):
        size = block_of(last - first)

        def block(k, carry):
            body(first + k * size, size)
            return carry

        lax.fori_loop(0, (last - first) // size, block, 0)

    def surfaces(i, size, surface_at, east_at, north_at, put_at):
        flux = {j: times(get_static(depth, i + j), north_at(i + j)) for j in (-1, 0)}
        for j in range(size):
            flux[j + 1] = times(get_static(depth, i + j + 1), north_at(i + j + 1))
            sides = column_diff(times(get_static(depth, i + j), east_at(i + j)))
            sea, surface = get_static(wet, i + j), surface_at(i + j)
            put_at(i + j, [
                sea[t] * (surface[t] - (sides[t] + (flux[j + 1][t] - flux[j - 1][t])))
                for t in range(tiles)
            ])

    def flows(i, size, surface_at, east_at, north_at, put_at):
        surface = {j: surface_at(i + j) for j in (-1, 0)}
        for j in range(size):
            surface[j + 1] = surface_at(i + j + 1)
            sides = column_diff(surface[j])
            sea, east, north = get_static(wet, i + j), east_at(i + j), north_at(i + j)
            put_at(i + j, surface[j], [
                sea[t] * (keep_coef * east[t] + turn_coef * north[t] - slope_coef * sides[t])
                for t in range(tiles)
            ], [
                sea[t] * (keep_coef * north[t] - turn_coef * east[t]
                          - slope_coef * (surface[j + 1][t] - surface[j - 1][t]))
                for t in range(tiles)
            ])

    def first_surface(i, size):
        surfaces(
            i, size, lambda r: get_field(0, r), lambda r: get_field(1, r),
            lambda r: get_field(2, r), lambda r, value: put(surf1, r + 3, value),
        )

    def first_flow(i, size):
        def put_flow(r, surface, east, north):
            put(east1, r + 2, east)
            put(north1, r + 2, north)

        flows(
            i, size, lambda r: get(surf1, r + 3), lambda r: get_field(1, r),
            lambda r: get_field(2, r), put_flow,
        )

    def second_surface(i, size):
        surfaces(
            i, size, lambda r: get(surf1, r + 3), lambda r: get(east1, r + 2),
            lambda r: get(north1, r + 2), lambda r, value: put(surf2, r + 1, value),
        )

    def second_flow(i, size):
        def put_out(r, surface, east, north):
            for field, values in enumerate((surface, east, north)):
                for spot, value in zip(spots, values):
                    out_ref[r, field, :, spot] = value.astype(jnp.bfloat16)

        flows(
            i, size, lambda r: get(surf2, r + 1), lambda r: get(east1, r + 2),
            lambda r: get(north1, r + 2), put_out,
        )

    over_rows(-3, rows + 3, first_surface)
    over_rows(-2, rows + 2, first_flow)
    over_rows(-1, rows + 1, second_surface)
    over_rows(0, rows, second_flow)


def forecast_groups(first, count, skip, place, whole_count, previous, factors, low, high,
                    static_low, static_high, depth, mask):
    modes, fields, rows, width = factors.shape
    padded = rows + 2 * HALO
    edge = GROUP * fields
    last = static_low.shape[0] // 4 - 1
    swap, swap_ends = swap_matrix(GROUP, GROUP), swap_matrix(2 * HALO, GROUP)

    def rows_of(count):
        return pltpu.VMEM((count, GROUP, width), jnp.float32)

    def whole(value):
        return pl.BlockSpec(value.shape, lambda i: (0,) * value.ndim)

    return pl.pallas_call(
        forecast_kernel,
        grid=(count,),
        out_shape=in_hbm((rows, fields, whole_count * GROUP, width), jnp.bfloat16),
        in_specs=[
            pl.BlockSpec((GROUP, fields, rows, width), lambda i: (first + i, 0, 0, 0)),
            pl.BlockSpec((edge, HALO, width), lambda i: (skip + i, 0, 0)),
            pl.BlockSpec((edge, HALO, width), lambda i: (skip + i, 0, 0)),
            pl.BlockSpec((4, HALO, width), lambda i: (last, 0, 0)),
            pl.BlockSpec((4, HALO, width), lambda i: (last, 0, 0)),
            whole(depth),
            whole(mask),
            whole(swap),
            whole(swap_ends),
        ] + [pl.BlockSpec(memory_space=pl.ANY) for _ in previous],
        out_specs=pl.BlockSpec((rows, fields, GROUP, width), lambda i: (0, 0, place + i, 0)),
        input_output_aliases={9: 0} if previous else {},
        scratch_shapes=[
            pltpu.VMEM((fields, padded, GROUP, width), jnp.float32),
            pltpu.VMEM((edge, 2 * HALO, width), jnp.float32),
            pltpu.VMEM((padded, 8, width), jnp.float32),
            pltpu.VMEM((padded, 8, width), jnp.float32),
            rows_of(rows + 6),
            rows_of(rows + 4),
            rows_of(rows + 4),
            rows_of(rows + 2),
        ],
        compiler_params=pltpu.CompilerParams(vmem_limit_bytes=VMEM_BYTES),
        cost_estimate=pl.CostEstimate(
            flops=60 * count * GROUP * rows * width,
            bytes_accessed=2 * 2 * count * GROUP * fields * rows * width,
            transcendentals=0,
        ),
        name="forecast",
    )(factors, low, high, static_low, static_high, depth, mask, swap, swap_ends, *previous)


def all_columns(chunk_refs, fault_ref, j):
    own = [ref[:, j, 0] for ref in chunk_refs]
    joined = jnp.concatenate(own, axis=1)
    return joined.reshape(-1, joined.shape[-1]), fault_ref[0, j]


def rotate_kernel(count, *refs):
    chunk_refs = refs[:count]
    fault_ref, turn_ref, out_ref = refs[count:]
    parts, _, size, modes, width = out_ref.shape
    for j in range(size):
        columns = jnp.concatenate(all_columns(chunk_refs, fault_ref, j), axis=0)
        value = jnp.dot(turn_ref[...], columns, preferred_element_type=jnp.float32)
        out_ref[:, 0, j] = value.astype(jnp.bfloat16).reshape(parts, modes, width)


def by_part(chunks, parts):
    return [c.reshape((parts, c.shape[0] // parts) + c.shape[1:]) for c in chunks]


def rotate_fields(first, fields, chunks, fault, turn, parts):
    width = chunks[0].shape[-1]
    each = chunks[0].shape[0] // parts
    kept = turn.shape[0]
    noise = fault.shape[2]
    modes = kept // parts
    size = 3 if each % 3 == 0 else 1
    views = by_part(chunks, parts)
    return pl.pallas_call(
        functools.partial(rotate_kernel, len(views)),
        grid=(fields, each // size),
        out_shape=in_hbm((parts, fields, each, modes, width), jnp.bfloat16),
        in_specs=[
            pl.BlockSpec((parts, size, 1, v.shape[3], width), lambda f, j: (0, j, first + f, 0, 0))
            for v in views
        ] + [
            pl.BlockSpec((1, size, noise, width), lambda f, j: (first + f, j, 0, 0)),
            pl.BlockSpec(turn.shape, lambda f, j: (0, 0)),
        ],
        out_specs=pl.BlockSpec((parts, 1, size, modes, width), lambda f, j: (0, f, j, 0, 0)),
        compiler_params=pltpu.CompilerParams(vmem_limit_bytes=VMEM_BYTES),
        cost_estimate=pl.CostEstimate(
            flops=2 * fields * each * width * kept * turn.shape[1],
            bytes_accessed=2 * fields * each * width * (kept + turn.shape[1]),
            transcendentals=0,
        ),
        name="rotate",
    )(*views, fault, turn)


def gram_kernel(count, each, devices, *refs):
    chunk_refs = refs[:count]
    fault_ref, turn_ref, half_ref, keep_ref, send_ref, gram_ref = refs[count:]
    pairs = [all_columns(chunk_refs, fault_ref, j) for j in range(each)]
    columns = jnp.concatenate(
        [jnp.concatenate([prior, fault], axis=0) for prior, fault in pairs], axis=1
    )
    value = lax.dot_general(
        columns, columns, (((1,), (1,)), ((), ())), preferred_element_type=jnp.float32
    )
    step = pl.program_id(0)

    @pl.when(step == 0)
    def _():
        gram_ref[...] = value

    @pl.when(step > 0)
    def _():
        gram_ref[...] += value

    @pl.when(step == pl.num_programs(0) - 1)
    def _():
        gram = gram_ref[...]
        size = gram.shape[0]
        row = lax.broadcasted_iota(jnp.int32, gram.shape, 0)
        column = lax.broadcasted_iota(jnp.int32, gram.shape, 1)
        full = jnp.sum(jnp.where(row == column, gram, 0.0))
        turn = turn_ref[...]
        turned = 0.0
        for _ in range(3):
            piece = gram.astype(jnp.bfloat16)
            turned = turned + jnp.dot(turn, piece, preferred_element_type=jnp.float32)
            gram = gram - piece.astype(jnp.float32)
        kept = jnp.sum(turned * turn.astype(jnp.float32))
        own = size // devices
        slot = keep_ref.shape[0] // (devices // 2)
        lane = lax.broadcasted_iota(jnp.int32, (keep_ref.shape[0], LANES), 1)
        traces = jnp.where(lane == 0, full, jnp.where(lane == 1, kept, 0.0))
        low = half_ref[0, 0] == 0
        for out in (keep_ref, send_ref):
            if slot != own:
                out[...] = jnp.zeros_like(out)
            out[:, size:] = traces
        for q in range(devices // 2):
            even = gram_ref[2 * q * own:(2 * q + 1) * own]
            uneven = gram_ref[(2 * q + 1) * own:(2 * q + 2) * own]
            keep_ref[q * slot:q * slot + own, :size] = jnp.where(low, even, uneven)
            send_ref[q * slot:q * slot + own, :size] = jnp.where(low, uneven, even)


def local_gram(chunks, fault, turn, parts, devices, half):
    width = chunks[0].shape[-1]
    each = chunks[0].shape[0] // parts
    noise = fault.shape[2]
    columns = turn.shape[1]
    views = by_part(chunks, parts)
    slot = -(-columns // devices // 8) * 8
    slots = (devices // 2 * slot, columns + LANES)
    out = in_hbm(slots, jnp.float32)
    return pl.pallas_call(
        functools.partial(gram_kernel, len(views), each, devices),
        grid=(3,),
        out_shape=(out, out),
        in_specs=[
            pl.BlockSpec((parts, each, 1, v.shape[3], width), lambda f: (0, 0, f, 0, 0))
            for v in views
        ] + [
            pl.BlockSpec((1, each, noise, width), lambda f: (f, 0, 0, 0)),
            pl.BlockSpec(turn.shape, lambda f: (0, 0)),
            pl.BlockSpec(memory_space=pltpu.SMEM),
        ],
        out_specs=[pl.BlockSpec(slots, lambda f: (0, 0))] * 2,
        scratch_shapes=[pltpu.VMEM((columns, columns), jnp.float32)],
        compiler_params=pltpu.CompilerParams(vmem_limit_bytes=VMEM_BYTES),
        cost_estimate=pl.CostEstimate(
            flops=2 * 3 * each * width * columns * columns,
            bytes_accessed=2 * 3 * each * width * columns,
            transcendentals=0,
        ),
        name="gram",
    )(*views, fault, turn, half)


def add_kernel(count, parts, me_ref, *refs):
    total = refs[0][...]
    for ref in refs[1:count]:
        total = total + ref[...]
    total_ref = refs[-1]
    total_ref[...] = total
    rows = total.shape[0] // parts
    for k in range(parts):
        first = pl.multiple_of(jnp.bitwise_xor(me_ref[0, 0], k) * rows, 8)
        refs[count + k][...] = total_ref[pl.ds(first, rows)]


def add_and_cut(terms, me, parts):
    rows, width = terms[0].shape
    whole = pl.BlockSpec((rows, width), lambda: (0, 0))
    block = pl.BlockSpec((rows // parts, width), lambda: (0, 0))
    return pl.pallas_call(
        functools.partial(add_kernel, len(terms), parts),
        out_shape=[in_hbm((rows // parts, width), jnp.float32) for _ in range(parts)],
        in_specs=[pl.BlockSpec(memory_space=pltpu.SMEM)] + [whole for _ in terms],
        out_specs=[block for _ in range(parts)],
        scratch_shapes=[pltpu.VMEM((rows, width), jnp.float32)],
        compiler_params=pltpu.CompilerParams(vmem_limit_bytes=VMEM_BYTES),
        cost_estimate=pl.CostEstimate(
            flops=len(terms) * rows * width,
            bytes_accessed=4 * (len(terms) + 1) * rows * width,
            transcendentals=0,
        ),
        name="add",
    )(me.reshape(1, 1), *terms)


def partners(axis, distance):
    return [(i, i ^ distance) for i in range(lax.axis_size(axis))]


def reduce_gram(keep, send):
    index = lax.axis_index("mode")
    other = lax.ppermute(send, "mode", partners("mode", 1))
    count = lax.axis_size("space")
    blocks = add_and_cut([keep, other], lax.axis_index("space"), count)
    terms = [blocks[0]] + [
        lax.ppermute(blocks[k], "space", partners("space", k)) for k in range(1, count)
    ]
    count = lax.axis_size("mode") // 2
    blocks = add_and_cut(terms, index // 2, count)
    terms = [blocks[0]] + [
        lax.ppermute(blocks[k], "mode", partners("mode", 2 * k)) for k in range(1, count)
    ]
    return sum(terms)


def finish_kernel(aliased, scale_ref, swap_ref, x_ref, *refs):
    out_ref = refs[aliased]
    parts, _, each, _, width = x_ref.shape
    rows = parts * each
    scale = scale_ref[0, 0]
    value = x_ref[...].reshape(rows * GROUP, width)
    for top in range(0, rows, GROUP):
        block = value[top * GROUP:(top + GROUP) * GROUP]
        block = scale * jnp.dot(swap_ref[...], block, preferred_element_type=jnp.float32)
        out_ref[:, 0, top:top + GROUP, :] = block.astype(jnp.bfloat16).reshape(GROUP, GROUP, width)


def finish_fields(first, arrived, scale, previous):
    parts, fields, each, modes, width = arrived.shape
    rows = parts * each
    swap = swap_matrix(GROUP, GROUP)
    operands = [scale.reshape(1, 1), swap, arrived, *previous]
    return pl.pallas_call(
        functools.partial(finish_kernel, len(previous)),
        grid=(fields, modes // GROUP),
        out_shape=jax.ShapeDtypeStruct((modes, 3, rows, width), jnp.bfloat16),
        in_specs=[
            pl.BlockSpec(memory_space=pltpu.SMEM),
            pl.BlockSpec(swap.shape, lambda f, m: (0, 0)),
            pl.BlockSpec((parts, 1, each, GROUP, width), lambda f, m: (0, f, 0, m, 0)),
        ] + [pl.BlockSpec(memory_space=pl.ANY) for _ in previous],
        out_specs=pl.BlockSpec((GROUP, 1, rows, width), lambda f, m: (m, first + f, 0, 0)),
        input_output_aliases={3: 0} if previous else {},
        compiler_params=pltpu.CompilerParams(vmem_limit_bytes=VMEM_BYTES),
        cost_estimate=pl.CostEstimate(
            flops=fields * modes * rows * width,
            bytes_accessed=4 * fields * modes * rows * width,
            transcendentals=0,
        ),
        name="finish",
    )(*operands)


def send_edges(first, last):
    count = lax.axis_size("space")
    forward = [(i, i + 1) for i in range(count - 1)]
    backward = [(target, source) for source, target in forward]
    return lax.ppermute(last, "space", forward), lax.ppermute(first, "space", backward)


def shards(sqrt_factors, model_error, water_depth, sea_mask, givens_transform):
    modes, fields, rows, width = sqrt_factors.shape
    parts = lax.axis_size("mode")
    count = modes // GROUP
    swap = functools.partial(
        lax.all_to_all, axis_name="mode", split_axis=0, concat_axis=0, tiled=True
    )

    near = min(count, 2)
    head = send_edges(*cut_edges(0, near, sqrt_factors, (water_depth, sea_mask)))
    static = (*head, water_depth, sea_mask)
    chunks = [swap(forecast_groups(0, 1, 0, 0, 1, (), sqrt_factors, *head, *static))]
    rest = ()
    if near > 1:
        rest = (forecast_groups(1, 1, 1, 0, count - 1, rest, sqrt_factors, *head, *static),)
    if count > near:
        tail = send_edges(*cut_edges(near, count - near, sqrt_factors, ()))
        rest = (forecast_groups(
            near, count - near, 0, near - 1, count - 1, rest, sqrt_factors, *tail, *static
        ),)
    chunks += [swap(value) for value in rest]

    fault = model_error.transpose(1, 2, 0, 3)
    turn = givens_transform.T
    devices = lax.axis_size("space") * parts
    half = lax.rem(lax.axis_index("mode"), 2).reshape(1, 1)
    columns = turn.shape[1]
    cell_count = float(fields * rows * lax.axis_size("space") * width)

    arrived = swap(rotate_fields(0, 2, chunks, fault, turn, parts))
    total = reduce_gram(*local_gram(chunks, fault, turn, parts, devices, half))
    last = rotate_fields(2, fields - 2, chunks, fault, turn, parts)
    last, total = lax.optimization_barrier((last, total))
    last = swap(last)
    gram = total[:columns // devices, :columns] / cell_count
    inflation = jnp.sqrt(total[0, columns] / total[0, columns + 1])

    reduced = finish_fields(0, arrived, inflation, ())
    reduced = finish_fields(2, last, inflation, (reduced,))
    return (reduced, gram, inflation)


def solution(mesh):
    in_specs = (
        P("mode", None, "space", None),
        P(None, None, ("space", "mode"), None),
        P("space", None),
        P("space", None),
        P(),
    )
    out_specs = (P("mode", None, "space", None), P(("space", "mode"), None), P())
    return jax.shard_map(shards, mesh=mesh, in_specs=in_specs, out_specs=out_specs, check_vma=False)
```

```python
import functools

import jax
import jax.numpy as jnp
import numpy as np
from jax import lax
from jax.experimental import pallas as pl
from jax.experimental.pallas import tpu as pltpu
from jax.sharding import PartitionSpec as P

flux_coef = 0.2
slope_coef = 0.2
turn_coef = 0.1
keep_coef = 0.95

GROUP = 16
HALO = 4
LANES = 128
VMEM_BYTES = 48 * 1024 * 1024


def column_diff(tiles):
    lane = lax.broadcasted_iota(jnp.int32, tiles[0].shape, 1)
    from_left = [pltpu.roll(tile, 1, 1) for tile in tiles]
    from_right = [pltpu.roll(tile, LANES - 1, 1) for tile in tiles]
    zero = jnp.zeros_like(tiles[0])
    out = []
    for t in range(len(tiles)):
        left = from_left[t - 1] if t > 0 else zero
        right = from_right[t + 1] if t + 1 < len(tiles) else zero
        previous = jnp.where(lane == 0, left, from_left[t])
        following = jnp.where(lane == LANES - 1, right, from_right[t])
        out.append(following - previous)
    return out


def swap_matrix(inner, outer):
    place = np.arange(inner * outer).reshape(outer, inner).T.reshape(-1)
    matrix = np.zeros((inner * outer, inner * outer), np.float32)
    matrix[np.arange(inner * outer), place] = 1.0
    return jnp.asarray(matrix, jnp.bfloat16)


def in_hbm(shape, dtype):
    return pltpu.HBM(shape, dtype)


def cut_edges_kernel(fixed, *refs):
    first_ref, last_ref = refs[:2]
    out_first, out_last = refs[-2:]
    group, fields = first_ref.shape[:2]
    for ref, out, low in ((first_ref, out_first, 0), (last_ref, out_last, GROUP - HALO)):
        for m in range(group):
            for field in range(fields):
                edge = ref[m, field].astype(jnp.float32)[low:low + HALO]
                out[m * fields + field] = edge.astype(jnp.bfloat16)
    if fixed:
        depth_ref, mask_ref = refs[2:4]
        for out, low in ((out_first, 0), (out_last, depth_ref.shape[0] - HALO)):
            rest = depth_ref[low:low + HALO]
            for piece in range(3):
                part = rest.astype(jnp.bfloat16)
                out[group * fields + piece] = part
                rest = rest - part.astype(jnp.float32)
            out[group * fields + 3] = mask_ref[low:low + HALO].astype(jnp.float32).astype(jnp.bfloat16)


def cut_edges(first, groups, factors, fixed):
    _, fields, rows, width = factors.shape
    size = GROUP * groups if fixed else GROUP
    steps = 1 if fixed else groups
    count = size * steps * fields + (4 if fixed else 0)
    block = size * fields + (4 if fixed else 0)
    out = jax.ShapeDtypeStruct((count, HALO, width), jnp.bfloat16)
    return pl.pallas_call(
        functools.partial(cut_edges_kernel, bool(fixed)),
        grid=(steps,),
        out_shape=(out, out),
        in_specs=[
            pl.BlockSpec((size, fields, GROUP, width), lambda i: (first // (size // GROUP) + i, 0, 0, 0)),
            pl.BlockSpec((size, fields, GROUP, width),
                         lambda i: (first // (size // GROUP) + i, 0, rows // GROUP - 1, 0)),
        ] + [pl.BlockSpec(value.shape, lambda i: (0, 0)) for value in fixed],
        out_specs=[pl.BlockSpec((block, HALO, width), lambda i: (i, 0, 0))] * 2,
        compiler_params=pltpu.CompilerParams(vmem_limit_bytes=VMEM_BYTES),
        cost_estimate=pl.CostEstimate(
            flops=0, bytes_accessed=5 * count * HALO * width * 2, transcendentals=0
        ),
        name="cut_edges",
    )(factors, factors, *fixed)


def block_of(count):
    return max(size for size in range(1, 14) if count % size == 0)


def forecast_kernel(x_ref, low_ref, high_ref, low_static, high_static, depth_ref, mask_ref,
                    swap_ref, swap_ends_ref, *refs):
    out_ref, cells, ends, depth, wet, surf1, east1, north1, surf2 = refs[-9:]
    _, fields, rows, width = x_ref.shape
    tiles = width // LANES
    spots = [slice(t * LANES, (t + 1) * LANES) for t in range(tiles)]

    ends[:, :HALO] = low_ref[...].astype(jnp.float32)
    ends[:, HALO:] = high_ref[...].astype(jnp.float32)
    for field in range(fields):
        for top in range(0, rows, GROUP):
            block = x_ref[:, field, top:top + GROUP, :].reshape(GROUP * GROUP, width)
            block = jnp.dot(swap_ref[...], block, preferred_element_type=jnp.float32)
            cells[field, HALO + top:HALO + top + GROUP] = block.reshape(GROUP, GROUP, width)
        block = jnp.concatenate([ends[m * fields + field] for m in range(GROUP)], axis=0)
        block = jnp.dot(
            swap_ends_ref[...], block.astype(jnp.bfloat16), preferred_element_type=jnp.float32
        ).reshape(2 * HALO, GROUP, width)
        cells[field, :HALO] = block[:HALO]
        cells[field, HALO + rows:] = block[HALO:]

    def place_static(place, depth_row, wet_row):
        depth[place] = jnp.broadcast_to(flux_coef * depth_row, (8, width))
        wet[place] = jnp.broadcast_to(wet_row, (8, width))

    for static, first in ((low_static, 0), (high_static, HALO + rows)):
        value = static[...].astype(jnp.float32)
        level = value[0] + value[1] + value[2]
        for j in range(HALO):
            place_static(first + j, level[j:j + 1], value[3, j:j + 1])
    for top in range(0, rows, 8):
        level = depth_ref[top:top + 8]
        sea = mask_ref[top:top + 8].astype(jnp.float32)
        for j in range(8):
            place_static(HALO + top + j, level[j:j + 1], sea[j:j + 1])

    def get(ref, i):
        return [ref[i, :, spot] for spot in spots]

    def get_field(field, i):
        return [cells[field, i + HALO, :, spot] for spot in spots]

    def get_static(ref, i):
        parts = [ref[i + HALO, :, spot] for spot in spots]
        return [jnp.concatenate([part] * (GROUP // 8), axis=0) for part in parts]

    def put(ref, i, values):
        for spot, value in zip(spots, values):
            ref[i, :, spot] = value

    def times(one, other):
        return [a * b for a, b in zip(one, other)]

    def over_rows(first, last, body):
        size = block_of(last - first)

        def block(k, carry):
            body(first + k * size, size)
            return carry

        lax.fori_loop(0, (last - first) // size, block, 0)

    def surfaces(i, size, surface_at, east_at, north_at, put_at):
        flux = {j: times(get_static(depth, i + j), north_at(i + j)) for j in (-1, 0)}
        for j in range(size):
            flux[j + 1] = times(get_static(depth, i + j + 1), north_at(i + j + 1))
            sides = column_diff(times(get_static(depth, i + j), east_at(i + j)))
            sea, surface = get_static(wet, i + j), surface_at(i + j)
            put_at(i + j, [
                sea[t] * (surface[t] - (sides[t] + (flux[j + 1][t] - flux[j - 1][t])))
                for t in range(tiles)
            ])

    def flows(i, size, surface_at, east_at, north_at, put_at):
        surface = {j: surface_at(i + j) for j in (-1, 0)}
        for j in range(size):
            surface[j + 1] = surface_at(i + j + 1)
            sides = column_diff(surface[j])
            sea, east, north = get_static(wet, i + j), east_at(i + j), north_at(i + j)
            put_at(i + j, surface[j], [
                sea[t] * (keep_coef * east[t] + turn_coef * north[t] - slope_coef * sides[t])
                for t in range(tiles)
            ], [
                sea[t] * (keep_coef * north[t] - turn_coef * east[t]
                          - slope_coef * (surface[j + 1][t] - surface[j - 1][t]))
                for t in range(tiles)
            ])

    def first_surface(i, size):
        surfaces(
            i, size, lambda r: get_field(0, r), lambda r: get_field(1, r),
            lambda r: get_field(2, r), lambda r, value: put(surf1, r + 3, value),
        )

    def first_flow(i, size):
        def put_flow(r, surface, east, north):
            put(east1, r + 2, east)
            put(north1, r + 2, north)

        flows(
            i, size, lambda r: get(surf1, r + 3), lambda r: get_field(1, r),
            lambda r: get_field(2, r), put_flow,
        )

    def second_surface(i, size):
        surfaces(
            i, size, lambda r: get(surf1, r + 3), lambda r: get(east1, r + 2),
            lambda r: get(north1, r + 2), lambda r, value: put(surf2, r + 1, value),
        )

    def second_flow(i, size):
        def put_out(r, surface, east, north):
            for field, values in enumerate((surface, east, north)):
                for spot, value in zip(spots, values):
                    out_ref[r, field, :, spot] = value.astype(jnp.bfloat16)

        flows(
            i, size, lambda r: get(surf2, r + 1), lambda r: get(east1, r + 2),
            lambda r: get(north1, r + 2), put_out,
        )

    over_rows(-3, rows + 3, first_surface)
    over_rows(-2, rows + 2, first_flow)
    over_rows(-1, rows + 1, second_surface)
    over_rows(0, rows, second_flow)


def forecast_groups(first, count, skip, place, whole_count, previous, factors, low, high,
                    static_low, static_high, depth, mask):
    modes, fields, rows, width = factors.shape
    padded = rows + 2 * HALO
    edge = GROUP * fields
    last = static_low.shape[0] // 4 - 1
    swap, swap_ends = swap_matrix(GROUP, GROUP), swap_matrix(2 * HALO, GROUP)

    def rows_of(count):
        return pltpu.VMEM((count, GROUP, width), jnp.float32)

    def whole(value):
        return pl.BlockSpec(value.shape, lambda i: (0,) * value.ndim)

    return pl.pallas_call(
        forecast_kernel,
        grid=(count,),
        out_shape=in_hbm((rows, fields, whole_count * GROUP, width), jnp.bfloat16),
        in_specs=[
            pl.BlockSpec((GROUP, fields, rows, width), lambda i: (first + i, 0, 0, 0)),
            pl.BlockSpec((edge, HALO, width), lambda i: (skip + i, 0, 0)),
            pl.BlockSpec((edge, HALO, width), lambda i: (skip + i, 0, 0)),
            pl.BlockSpec((4, HALO, width), lambda i: (last, 0, 0)),
            pl.BlockSpec((4, HALO, width), lambda i: (last, 0, 0)),
            whole(depth),
            whole(mask),
            whole(swap),
            whole(swap_ends),
        ] + [pl.BlockSpec(memory_space=pl.ANY) for _ in previous],
        out_specs=pl.BlockSpec((rows, fields, GROUP, width), lambda i: (0, 0, place + i, 0)),
        input_output_aliases={9: 0} if previous else {},
        scratch_shapes=[
            pltpu.VMEM((fields, padded, GROUP, width), jnp.float32),
            pltpu.VMEM((edge, 2 * HALO, width), jnp.float32),
            pltpu.VMEM((padded, 8, width), jnp.float32),
            pltpu.VMEM((padded, 8, width), jnp.float32),
            rows_of(rows + 6),
            rows_of(rows + 4),
            rows_of(rows + 4),
            rows_of(rows + 2),
        ],
        compiler_params=pltpu.CompilerParams(vmem_limit_bytes=VMEM_BYTES),
        cost_estimate=pl.CostEstimate(
            flops=60 * count * GROUP * rows * width,
            bytes_accessed=2 * 2 * count * GROUP * fields * rows * width,
            transcendentals=0,
        ),
        name="forecast",
    )(factors, low, high, static_low, static_high, depth, mask, swap, swap_ends, *previous)


def all_columns(chunk_refs, fault_ref, j):
    own = [ref[:, j, 0] for ref in chunk_refs]
    joined = jnp.concatenate(own, axis=1)
    return joined.reshape(-1, joined.shape[-1]), fault_ref[0, j]


def rotate_kernel(count, *refs):
    chunk_refs = refs[:count]
    fault_ref, turn_ref, out_ref = refs[count:]
    parts, _, size, modes, width = out_ref.shape
    for j in range(size):
        columns = jnp.concatenate(all_columns(chunk_refs, fault_ref, j), axis=0)
        value = jnp.dot(turn_ref[...], columns, preferred_element_type=jnp.float32)
        out_ref[:, 0, j] = value.astype(jnp.bfloat16).reshape(parts, modes, width)


def by_part(chunks, parts):
    return [c.reshape((parts, c.shape[0] // parts) + c.shape[1:]) for c in chunks]


def rotate_fields(first, fields, chunks, fault, turn, parts):
    width = chunks[0].shape[-1]
    each = chunks[0].shape[0] // parts
    kept = turn.shape[0]
    noise = fault.shape[2]
    modes = kept // parts
    size = 3 if each % 3 == 0 else 1
    views = by_part(chunks, parts)
    return pl.pallas_call(
        functools.partial(rotate_kernel, len(views)),
        grid=(fields, each // size),
        out_shape=in_hbm((parts, fields, each, modes, width), jnp.bfloat16),
        in_specs=[
            pl.BlockSpec((parts, size, 1, v.shape[3], width), lambda f, j: (0, j, first + f, 0, 0))
            for v in views
        ] + [
            pl.BlockSpec((1, size, noise, width), lambda f, j: (first + f, j, 0, 0)),
            pl.BlockSpec(turn.shape, lambda f, j: (0, 0)),
        ],
        out_specs=pl.BlockSpec((parts, 1, size, modes, width), lambda f, j: (0, f, j, 0, 0)),
        compiler_params=pltpu.CompilerParams(vmem_limit_bytes=VMEM_BYTES),
        cost_estimate=pl.CostEstimate(
            flops=2 * fields * each * width * kept * turn.shape[1],
            bytes_accessed=2 * fields * each * width * (kept + turn.shape[1]),
            transcendentals=0,
        ),
        name="rotate",
    )(*views, fault, turn)


def gram_kernel(count, each, devices, *refs):
    chunk_refs = refs[:count]
    fault_ref, turn_ref, half_ref, keep_ref, send_ref, gram_ref = refs[count:]
    pairs = [all_columns(chunk_refs, fault_ref, j) for j in range(each)]
    columns = jnp.concatenate(
        [jnp.concatenate([prior, fault], axis=0) for prior, fault in pairs], axis=1
    )
    value = lax.dot_general(
        columns, columns, (((1,), (1,)), ((), ())), preferred_element_type=jnp.float32
    )
    step = pl.program_id(0)

    @pl.when(step == 0)
    def _():
        gram_ref[...] = value

    @pl.when(step > 0)
    def _():
        gram_ref[...] += value

    @pl.when(step == pl.num_programs(0) - 1)
    def _():
        gram = gram_ref[...]
        size = gram.shape[0]
        row = lax.broadcasted_iota(jnp.int32, gram.shape, 0)
        column = lax.broadcasted_iota(jnp.int32, gram.shape, 1)
        full = jnp.sum(jnp.where(row == column, gram, 0.0))
        turn = turn_ref[...]
        turned = 0.0
        for _ in range(3):
            piece = gram.astype(jnp.bfloat16)
            turned = turned + jnp.dot(turn, piece, preferred_element_type=jnp.float32)
            gram = gram - piece.astype(jnp.float32)
        kept = jnp.sum(turned * turn.astype(jnp.float32))
        own = size // devices
        slot = keep_ref.shape[0] // (devices // 2)
        lane = lax.broadcasted_iota(jnp.int32, (keep_ref.shape[0], LANES), 1)
        traces = jnp.where(lane == 0, full, jnp.where(lane == 1, kept, 0.0))
        low = half_ref[0, 0] == 0
        for out in (keep_ref, send_ref):
            if slot != own:
                out[...] = jnp.zeros_like(out)
            out[:, size:] = traces
        for q in range(devices // 2):
            even = gram_ref[2 * q * own:(2 * q + 1) * own]
            uneven = gram_ref[(2 * q + 1) * own:(2 * q + 2) * own]
            keep_ref[q * slot:q * slot + own, :size] = jnp.where(low, even, uneven)
            send_ref[q * slot:q * slot + own, :size] = jnp.where(low, uneven, even)


def local_gram(chunks, fault, turn, parts, devices, half):
    width = chunks[0].shape[-1]
    each = chunks[0].shape[0] // parts
    noise = fault.shape[2]
    columns = turn.shape[1]
    views = by_part(chunks, parts)
    slot = -(-columns // devices // 8) * 8
    slots = (devices // 2 * slot, columns + LANES)
    out = in_hbm(slots, jnp.float32)
    return pl.pallas_call(
        functools.partial(gram_kernel, len(views), each, devices),
        grid=(3,),
        out_shape=(out, out),
        in_specs=[
            pl.BlockSpec((parts, each, 1, v.shape[3], width), lambda f: (0, 0, f, 0, 0))
            for v in views
        ] + [
            pl.BlockSpec((1, each, noise, width), lambda f: (f, 0, 0, 0)),
            pl.BlockSpec(turn.shape, lambda f: (0, 0)),
            pl.BlockSpec(memory_space=pltpu.SMEM),
        ],
        out_specs=[pl.BlockSpec(slots, lambda f: (0, 0))] * 2,
        scratch_shapes=[pltpu.VMEM((columns, columns), jnp.float32)],
        compiler_params=pltpu.CompilerParams(vmem_limit_bytes=VMEM_BYTES),
        cost_estimate=pl.CostEstimate(
            flops=2 * 3 * each * width * columns * columns,
            bytes_accessed=2 * 3 * each * width * columns,
            transcendentals=0,
        ),
        name="gram",
    )(*views, fault, turn, half)


def add_kernel(count, parts, me_ref, *refs):
    total = refs[0][...]
    for ref in refs[1:count]:
        total = total + ref[...]
    total_ref = refs[-1]
    total_ref[...] = total
    rows = total.shape[0] // parts
    for k in range(parts):
        first = pl.multiple_of(jnp.bitwise_xor(me_ref[0, 0], k) * rows, 8)
        refs[count + k][...] = total_ref[pl.ds(first, rows)]


def add_and_cut(terms, me, parts):
    rows, width = terms[0].shape
    whole = pl.BlockSpec((rows, width), lambda: (0, 0))
    block = pl.BlockSpec((rows // parts, width), lambda: (0, 0))
    return pl.pallas_call(
        functools.partial(add_kernel, len(terms), parts),
        out_shape=[in_hbm((rows // parts, width), jnp.float32) for _ in range(parts)],
        in_specs=[pl.BlockSpec(memory_space=pltpu.SMEM)] + [whole for _ in terms],
        out_specs=[block for _ in range(parts)],
        scratch_shapes=[pltpu.VMEM((rows, width), jnp.float32)],
        compiler_params=pltpu.CompilerParams(vmem_limit_bytes=VMEM_BYTES),
        cost_estimate=pl.CostEstimate(
            flops=len(terms) * rows * width,
            bytes_accessed=4 * (len(terms) + 1) * rows * width,
            transcendentals=0,
        ),
        name="add",
    )(me.reshape(1, 1), *terms)


def partners(axis, distance):
    return [(i, i ^ distance) for i in range(lax.axis_size(axis))]


def sum_over_slabs(keep, send):
    other = lax.ppermute(send, "mode", partners("mode", 1))
    count = lax.axis_size("space")
    blocks = add_and_cut([keep, other], lax.axis_index("space"), count)
    terms = [blocks[0]] + [
        lax.ppermute(blocks[k], "space", partners("space", k)) for k in range(1, count)
    ]
    return add_and_cut(terms, lax.axis_index("mode") // 2, lax.axis_size("mode") // 2)


def sum_over_modes(blocks):
    return blocks[0] + sum(
        lax.ppermute(block, "mode", partners("mode", 2 * k))
        for k, block in enumerate(blocks) if k > 0
    )


def finish_kernel(aliased, scale_ref, swap_ref, x_ref, *refs):
    out_ref = refs[aliased]
    parts, _, each, _, width = x_ref.shape
    rows = parts * each
    scale = scale_ref[0, 0]
    value = x_ref[...].reshape(rows * GROUP, width)
    for top in range(0, rows, GROUP):
        block = value[top * GROUP:(top + GROUP) * GROUP]
        block = scale * jnp.dot(swap_ref[...], block, preferred_element_type=jnp.float32)
        out_ref[:, 0, top:top + GROUP, :] = block.astype(jnp.bfloat16).reshape(GROUP, GROUP, width)


def finish_fields(first, arrived, scale, previous):
    parts, fields, each, modes, width = arrived.shape
    rows = parts * each
    swap = swap_matrix(GROUP, GROUP)
    operands = [scale.reshape(1, 1), swap, arrived, *previous]
    return pl.pallas_call(
        functools.partial(finish_kernel, len(previous)),
        grid=(fields, modes // GROUP),
        out_shape=jax.ShapeDtypeStruct((modes, 3, rows, width), jnp.bfloat16),
        in_specs=[
            pl.BlockSpec(memory_space=pltpu.SMEM),
            pl.BlockSpec(swap.shape, lambda f, m: (0, 0)),
            pl.BlockSpec((parts, 1, each, GROUP, width), lambda f, m: (0, f, 0, m, 0)),
        ] + [pl.BlockSpec(memory_space=pl.ANY) for _ in previous],
        out_specs=pl.BlockSpec((GROUP, 1, rows, width), lambda f, m: (m, first + f, 0, 0)),
        input_output_aliases={3: 0} if previous else {},
        compiler_params=pltpu.CompilerParams(vmem_limit_bytes=VMEM_BYTES),
        cost_estimate=pl.CostEstimate(
            flops=fields * modes * rows * width,
            bytes_accessed=4 * fields * modes * rows * width,
            transcendentals=0,
        ),
        name="finish",
    )(*operands)


def send_edges(first, last):
    count = lax.axis_size("space")
    forward = [(i, i + 1) for i in range(count - 1)]
    backward = [(target, source) for source, target in forward]
    return lax.ppermute(last, "space", forward), lax.ppermute(first, "space", backward)


def shards(sqrt_factors, model_error, water_depth, sea_mask, givens_transform):
    modes, fields, rows, width = sqrt_factors.shape
    parts = lax.axis_size("mode")
    count = modes // GROUP
    swap = functools.partial(
        lax.all_to_all, axis_name="mode", split_axis=0, concat_axis=0, tiled=True
    )

    near = min(count, 2)
    water_depth, sea_mask = (
        pltpu.with_memory_space_constraint(value, pltpu.HBM) for value in (water_depth, sea_mask)
    )
    head = send_edges(*cut_edges(0, near, sqrt_factors, (water_depth, sea_mask)))
    static = (*head, water_depth, sea_mask)
    chunks = [swap(forecast_groups(0, 1, 0, 0, 1, (), sqrt_factors, *head, *static))]
    rest = ()
    if near > 1:
        rest = (forecast_groups(1, 1, 1, 0, count - 1, rest, sqrt_factors, *head, *static),)
    if count > near:
        tail = send_edges(*cut_edges(near, count - near, sqrt_factors, ()))
        rest = (forecast_groups(
            near, count - near, 0, near - 1, count - 1, rest, sqrt_factors, *tail, *static
        ),)
    chunks += [swap(value) for value in rest]

    fault = model_error.transpose(1, 2, 0, 3)
    turn = givens_transform.T
    devices = lax.axis_size("space") * parts
    half = lax.rem(lax.axis_index("mode"), 2).reshape(1, 1)
    columns = turn.shape[1]
    cell_count = float(fields * rows * lax.axis_size("space") * width)

    arrived = swap(rotate_fields(0, 2, chunks, fault, turn, parts))
    blocks = sum_over_slabs(*local_gram(chunks, fault, turn, parts, devices, half))
    last = rotate_fields(2, fields - 2, chunks, fault, turn, parts)
    last, *blocks = lax.optimization_barrier((last, *blocks))
    total = sum_over_modes(blocks)
    last = swap(last)
    gram = total[:columns // devices, :columns] / cell_count
    inflation = jnp.sqrt(total[0, columns] / total[0, columns + 1])

    reduced = finish_fields(0, arrived, inflation, ())
    reduced = finish_fields(2, last, inflation, (reduced,))
    return (reduced, gram, inflation)


def solution(mesh):
    in_specs = (
        P("mode", None, "space", None),
        P(None, None, ("space", "mode"), None),
        P("space", None),
        P("space", None),
        P(),
    )
    out_specs = (P("mode", None, "space", None), P(("space", "mode"), None), P())
    return jax.shard_map(shards, mesh=mesh, in_specs=in_specs, out_specs=out_specs, check_vma=False)
```

```python
import functools

import jax
import jax.numpy as jnp
import numpy as np
from jax import lax
from jax.experimental import pallas as pl
from jax.experimental.pallas import tpu as pltpu
from jax.sharding import PartitionSpec as P

flux_coef = 0.2
slope_coef = 0.2
turn_coef = 0.1
keep_coef = 0.95

GROUP = 16
HALO = 4
LANES = 128
VMEM_BYTES = 48 * 1024 * 1024


def column_diff(tiles):
    lane = lax.broadcasted_iota(jnp.int32, tiles[0].shape, 1)
    from_left = [pltpu.roll(tile, 1, 1) for tile in tiles]
    from_right = [pltpu.roll(tile, LANES - 1, 1) for tile in tiles]
    zero = jnp.zeros_like(tiles[0])
    out = []
    for t in range(len(tiles)):
        left = from_left[t - 1] if t > 0 else zero
        right = from_right[t + 1] if t + 1 < len(tiles) else zero
        previous = jnp.where(lane == 0, left, from_left[t])
        following = jnp.where(lane == LANES - 1, right, from_right[t])
        out.append(following - previous)
    return out


def swap_matrix(inner, outer):
    place = np.arange(inner * outer).reshape(outer, inner).T.reshape(-1)
    matrix = np.zeros((inner * outer, inner * outer), np.float32)
    matrix[np.arange(inner * outer), place] = 1.0
    return jnp.asarray(matrix, jnp.bfloat16)


def in_hbm(shape, dtype):
    return pltpu.HBM(shape, dtype)


def cut_edges_kernel(fixed, *refs):
    first_ref, last_ref = refs[:2]
    out_first, out_last = refs[-2:]
    group, fields = first_ref.shape[:2]
    for ref, out, low in ((first_ref, out_first, 0), (last_ref, out_last, GROUP - HALO)):
        for m in range(group):
            for field in range(fields):
                edge = ref[m, field].astype(jnp.float32)[low:low + HALO]
                out[m * fields + field] = edge.astype(jnp.bfloat16)
    if fixed:
        depth_ref, mask_ref = refs[2:4]
        for out, low in ((out_first, 0), (out_last, depth_ref.shape[0] - HALO)):
            rest = depth_ref[low:low + HALO]
            for piece in range(3):
                part = rest.astype(jnp.bfloat16)
                out[group * fields + piece] = part
                rest = rest - part.astype(jnp.float32)
            out[group * fields + 3] = mask_ref[low:low + HALO].astype(jnp.float32).astype(jnp.bfloat16)


def cut_edges(first, groups, factors, fixed):
    _, fields, rows, width = factors.shape
    size = GROUP * groups if fixed else GROUP
    steps = 1 if fixed else groups
    count = size * steps * fields + (4 if fixed else 0)
    block = size * fields + (4 if fixed else 0)
    out = jax.ShapeDtypeStruct((count, HALO, width), jnp.bfloat16)
    return pl.pallas_call(
        functools.partial(cut_edges_kernel, bool(fixed)),
        grid=(steps,),
        out_shape=(out, out),
        in_specs=[
            pl.BlockSpec((size, fields, GROUP, width), lambda i: (first // (size // GROUP) + i, 0, 0, 0)),
            pl.BlockSpec((size, fields, GROUP, width),
                         lambda i: (first // (size // GROUP) + i, 0, rows // GROUP - 1, 0)),
        ] + [pl.BlockSpec(value.shape, lambda i: (0, 0)) for value in fixed],
        out_specs=[pl.BlockSpec((block, HALO, width), lambda i: (i, 0, 0))] * 2,
        compiler_params=pltpu.CompilerParams(vmem_limit_bytes=VMEM_BYTES),
        cost_estimate=pl.CostEstimate(
            flops=0, bytes_accessed=5 * count * HALO * width * 2, transcendentals=0
        ),
        name="cut_edges",
    )(factors, factors, *fixed)


def block_of(count):
    return max(size for size in range(1, 28) if count % size == 0)


def forecast_kernel(x_ref, low_ref, high_ref, low_static, high_static, depth_ref, mask_ref,
                    swap_ref, swap_ends_ref, *refs):
    out_ref, cells, ends, depth, wet, surf1, east1, north1, surf2 = refs[-9:]
    _, fields, rows, width = x_ref.shape
    tiles = width // LANES
    spots = [slice(t * LANES, (t + 1) * LANES) for t in range(tiles)]

    ends[:, :HALO] = low_ref[...].astype(jnp.float32)
    ends[:, HALO:] = high_ref[...].astype(jnp.float32)
    for field in range(fields):
        for top in range(0, rows, GROUP):
            block = x_ref[:, field, top:top + GROUP, :].reshape(GROUP * GROUP, width)
            block = jnp.dot(swap_ref[...], block, preferred_element_type=jnp.float32)
            block = block * slope_coef if field == 0 else block
            cells[field, HALO + top:HALO + top + GROUP] = block.reshape(GROUP, GROUP, width)
        block = jnp.concatenate([ends[m * fields + field] for m in range(GROUP)], axis=0)
        block = jnp.dot(
            swap_ends_ref[...], block.astype(jnp.bfloat16), preferred_element_type=jnp.float32
        ).reshape(2 * HALO, GROUP, width)
        block = block * slope_coef if field == 0 else block
        cells[field, :HALO] = block[:HALO]
        cells[field, HALO + rows:] = block[HALO:]

    def place_static(place, depth_row, wet_row):
        depth[place] = jnp.broadcast_to(flux_coef * slope_coef * depth_row, (8, width))
        wet[place] = jnp.broadcast_to(wet_row, (8, width))

    for static, first in ((low_static, 0), (high_static, HALO + rows)):
        value = static[...].astype(jnp.float32)
        level = value[0] + value[1] + value[2]
        for j in range(HALO):
            place_static(first + j, level[j:j + 1], value[3, j:j + 1])
    for top in range(0, rows, 8):
        level = depth_ref[top:top + 8]
        sea = mask_ref[top:top + 8].astype(jnp.float32)
        for j in range(8):
            place_static(HALO + top + j, level[j:j + 1], sea[j:j + 1])

    def get(ref, i):
        return [ref[i, :, spot] for spot in spots]

    def get_field(field, i):
        return [cells[field, i + HALO, :, spot] for spot in spots]

    def get_static(ref, i):
        parts = [ref[i + HALO, :, spot] for spot in spots]
        return [jnp.concatenate([part] * (GROUP // 8), axis=0) for part in parts]

    def put(ref, i, values):
        for spot, value in zip(spots, values):
            ref[i, :, spot] = value

    def times(one, other):
        return [a * b for a, b in zip(one, other)]

    def over_rows(first, last, body):
        size = block_of(last - first)

        def block(k, carry):
            body(first + k * size, size)
            return carry

        lax.fori_loop(0, (last - first) // size, block, 0)

    def surfaces(i, size, surface_at, east_at, north_at, put_at):
        flux = {j: times(get_static(depth, i + j), north_at(i + j)) for j in (-1, 0)}
        for j in range(size):
            flux[j + 1] = times(get_static(depth, i + j + 1), north_at(i + j + 1))
            sides = column_diff(times(get_static(depth, i + j), east_at(i + j)))
            sea, surface = get_static(wet, i + j), surface_at(i + j)
            put_at(i + j, [
                sea[t] * (surface[t] - (sides[t] + (flux[j + 1][t] - flux[j - 1][t])))
                for t in range(tiles)
            ])

    def flows(i, size, surface_at, east_at, north_at, put_at):
        surface = {j: surface_at(i + j) for j in (-1, 0)}
        for j in range(size):
            surface[j + 1] = surface_at(i + j + 1)
            sides = column_diff(surface[j])
            sea, east, north = get_static(wet, i + j), east_at(i + j), north_at(i + j)
            put_at(i + j, surface[j], [
                sea[t] * (keep_coef * east[t] + turn_coef * north[t] - sides[t])
                for t in range(tiles)
            ], [
                sea[t] * (keep_coef * north[t] - turn_coef * east[t]
                          - (surface[j + 1][t] - surface[j - 1][t]))
                for t in range(tiles)
            ])

    def first_surface(i, size):
        surfaces(
            i, size, lambda r: get_field(0, r), lambda r: get_field(1, r),
            lambda r: get_field(2, r), lambda r, value: put(surf1, r + 3, value),
        )

    def first_flow(i, size):
        def put_flow(r, surface, east, north):
            put(east1, r + 2, east)
            put(north1, r + 2, north)

        flows(
            i, size, lambda r: get(surf1, r + 3), lambda r: get_field(1, r),
            lambda r: get_field(2, r), put_flow,
        )

    def second_surface(i, size):
        surfaces(
            i, size, lambda r: get(surf1, r + 3), lambda r: get(east1, r + 2),
            lambda r: get(north1, r + 2), lambda r, value: put(surf2, r + 1, value),
        )

    def second_flow(i, size):
        def put_out(r, surface, east, north):
            surface = [value * (1.0 / slope_coef) for value in surface]
            for field, values in enumerate((surface, east, north)):
                for spot, value in zip(spots, values):
                    out_ref[r, field, :, spot] = value.astype(jnp.bfloat16)

        flows(
            i, size, lambda r: get(surf2, r + 1), lambda r: get(east1, r + 2),
            lambda r: get(north1, r + 2), put_out,
        )

    over_rows(-3, rows + 3, first_surface)
    over_rows(-2, rows + 2, first_flow)
    over_rows(-1, rows + 1, second_surface)
    over_rows(0, rows, second_flow)


def forecast_groups(first, count, skip, place, whole_count, previous, factors, low, high,
                    static_low, static_high, depth, mask):
    modes, fields, rows, width = factors.shape
    padded = rows + 2 * HALO
    edge = GROUP * fields
    last = static_low.shape[0] // 4 - 1
    swap, swap_ends = swap_matrix(GROUP, GROUP), swap_matrix(2 * HALO, GROUP)

    def rows_of(count):
        return pltpu.VMEM((count, GROUP, width), jnp.float32)

    def whole(value):
        return pl.BlockSpec(value.shape, lambda i: (0,) * value.ndim)

    return pl.pallas_call(
        forecast_kernel,
        grid=(count,),
        out_shape=in_hbm((rows, fields, whole_count * GROUP, width), jnp.bfloat16),
        in_specs=[
            pl.BlockSpec((GROUP, fields, rows, width), lambda i: (first + i, 0, 0, 0)),
            pl.BlockSpec((edge, HALO, width), lambda i: (skip + i, 0, 0)),
            pl.BlockSpec((edge, HALO, width), lambda i: (skip + i, 0, 0)),
            pl.BlockSpec((4, HALO, width), lambda i: (last, 0, 0)),
            pl.BlockSpec((4, HALO, width), lambda i: (last, 0, 0)),
            whole(depth),
            whole(mask),
            whole(swap),
            whole(swap_ends),
        ] + [pl.BlockSpec(memory_space=pl.ANY) for _ in previous],
        out_specs=pl.BlockSpec((rows, fields, GROUP, width), lambda i: (0, 0, place + i, 0)),
        input_output_aliases={9: 0} if len(previous) == 1 else {},
        scratch_shapes=[
            pltpu.VMEM((fields, padded, GROUP, width), jnp.float32),
            pltpu.VMEM((edge, 2 * HALO, width), jnp.float32),
            pltpu.VMEM((padded, 8, width), jnp.float32),
            pltpu.VMEM((padded, 8, width), jnp.float32),
            rows_of(rows + 6),
            rows_of(rows + 4),
            rows_of(rows + 4),
            rows_of(rows + 2),
        ],
        compiler_params=pltpu.CompilerParams(vmem_limit_bytes=VMEM_BYTES),
        cost_estimate=pl.CostEstimate(
            flops=60 * count * GROUP * rows * width,
            bytes_accessed=2 * 2 * count * GROUP * fields * rows * width,
            transcendentals=0,
        ),
        name="forecast",
    )(factors, low, high, static_low, static_high, depth, mask, swap, swap_ends, *previous)


def all_columns(chunk_refs, fault_ref, j):
    own = [ref[:, j, 0] for ref in chunk_refs]
    joined = jnp.concatenate(own, axis=1)
    return joined.reshape(-1, joined.shape[-1]), fault_ref[0, j]


def rotate_kernel(count, *refs):
    chunk_refs = refs[:count]
    fault_ref, turn_ref, out_ref = refs[count:]
    parts, _, size, modes, width = out_ref.shape
    for j in range(size):
        columns = jnp.concatenate(all_columns(chunk_refs, fault_ref, j), axis=0)
        value = jnp.dot(turn_ref[...], columns, preferred_element_type=jnp.float32)
        out_ref[:, 0, j] = value.astype(jnp.bfloat16).reshape(parts, modes, width)


def by_part(chunks, parts):
    return [c.reshape((parts, c.shape[0] // parts) + c.shape[1:]) for c in chunks]


def rotate_fields(first, fields, chunks, fault, turn, parts):
    width = chunks[0].shape[-1]
    each = chunks[0].shape[0] // parts
    kept = turn.shape[0]
    noise = fault.shape[2]
    modes = kept // parts
    size = 3 if each % 3 == 0 else 1
    views = by_part(chunks, parts)
    return pl.pallas_call(
        functools.partial(rotate_kernel, len(views)),
        grid=(fields, each // size),
        out_shape=in_hbm((parts, fields, each, modes, width), jnp.bfloat16),
        in_specs=[
            pl.BlockSpec((parts, size, 1, v.shape[3], width), lambda f, j: (0, j, first + f, 0, 0))
            for v in views
        ] + [
            pl.BlockSpec((1, size, noise, width), lambda f, j: (first + f, j, 0, 0)),
            pl.BlockSpec(turn.shape, lambda f, j: (0, 0)),
        ],
        out_specs=pl.BlockSpec((parts, 1, size, modes, width), lambda f, j: (0, f, j, 0, 0)),
        compiler_params=pltpu.CompilerParams(vmem_limit_bytes=VMEM_BYTES),
        cost_estimate=pl.CostEstimate(
            flops=2 * fields * each * width * kept * turn.shape[1],
            bytes_accessed=2 * fields * each * width * (kept + turn.shape[1]),
            transcendentals=0,
        ),
        name="rotate",
    )(*views, fault, turn)


def gram_kernel(count, each, devices, *refs):
    chunk_refs = refs[:count]
    fault_ref, turn_ref, half_ref, keep_ref, send_ref, gram_ref = refs[count:]
    pairs = [all_columns(chunk_refs, fault_ref, j) for j in range(each)]
    columns = jnp.concatenate(
        [jnp.concatenate([prior, fault], axis=0) for prior, fault in pairs], axis=1
    )
    value = lax.dot_general(
        columns, columns, (((1,), (1,)), ((), ())), preferred_element_type=jnp.float32
    )
    step = pl.program_id(0)

    @pl.when(step == 0)
    def _():
        gram_ref[...] = value

    @pl.when(step > 0)
    def _():
        gram_ref[...] += value

    @pl.when(step == pl.num_programs(0) - 1)
    def _():
        gram = gram_ref[...]
        size = gram.shape[0]
        row = lax.broadcasted_iota(jnp.int32, gram.shape, 0)
        column = lax.broadcasted_iota(jnp.int32, gram.shape, 1)
        full = jnp.sum(jnp.where(row == column, gram, 0.0))
        turn = turn_ref[...]
        turned = 0.0
        for _ in range(3):
            piece = gram.astype(jnp.bfloat16)
            turned = turned + jnp.dot(turn, piece, preferred_element_type=jnp.float32)
            gram = gram - piece.astype(jnp.float32)
        kept = jnp.sum(turned * turn.astype(jnp.float32))
        own = size // devices
        slot = keep_ref.shape[0] // (devices // 2)
        lane = lax.broadcasted_iota(jnp.int32, (keep_ref.shape[0], LANES), 1)
        traces = jnp.where(lane == 0, full, jnp.where(lane == 1, kept, 0.0))
        low = half_ref[0, 0] == 0
        for out in (keep_ref, send_ref):
            if slot != own:
                out[...] = jnp.zeros_like(out)
            out[:, size:] = traces
        for q in range(devices // 2):
            even = gram_ref[2 * q * own:(2 * q + 1) * own]
            uneven = gram_ref[(2 * q + 1) * own:(2 * q + 2) * own]
            keep_ref[q * slot:q * slot + own, :size] = jnp.where(low, even, uneven)
            send_ref[q * slot:q * slot + own, :size] = jnp.where(low, uneven, even)


def local_gram(chunks, fault, turn, parts, devices, half):
    width = chunks[0].shape[-1]
    each = chunks[0].shape[0] // parts
    noise = fault.shape[2]
    columns = turn.shape[1]
    views = by_part(chunks, parts)
    slot = -(-columns // devices // 8) * 8
    slots = (devices // 2 * slot, columns + LANES)
    out = in_hbm(slots, jnp.float32)
    return pl.pallas_call(
        functools.partial(gram_kernel, len(views), each, devices),
        grid=(3,),
        out_shape=(out, out),
        in_specs=[
            pl.BlockSpec((parts, each, 1, v.shape[3], width), lambda f: (0, 0, f, 0, 0))
            for v in views
        ] + [
            pl.BlockSpec((1, each, noise, width), lambda f: (f, 0, 0, 0)),
            pl.BlockSpec(turn.shape, lambda f: (0, 0)),
            pl.BlockSpec(memory_space=pltpu.SMEM),
        ],
        out_specs=[pl.BlockSpec(slots, lambda f: (0, 0))] * 2,
        scratch_shapes=[pltpu.VMEM((columns, columns), jnp.float32)],
        compiler_params=pltpu.CompilerParams(vmem_limit_bytes=VMEM_BYTES),
        cost_estimate=pl.CostEstimate(
            flops=2 * 3 * each * width * columns * columns,
            bytes_accessed=2 * 3 * each * width * columns,
            transcendentals=0,
        ),
        name="gram",
    )(*views, fault, turn, half)


def add_kernel(count, parts, me_ref, *refs):
    total = refs[0][...]
    for ref in refs[1:count]:
        total = total + ref[...]
    total_ref = refs[-1]
    total_ref[...] = total
    rows = total.shape[0] // parts
    for k in range(parts):
        first = pl.multiple_of(jnp.bitwise_xor(me_ref[0, 0], k) * rows, 8)
        refs[count + k][...] = total_ref[pl.ds(first, rows)]


def add_and_cut(terms, me, parts):
    rows, width = terms[0].shape
    whole = pl.BlockSpec((rows, width), lambda: (0, 0))
    block = pl.BlockSpec((rows // parts, width), lambda: (0, 0))
    return pl.pallas_call(
        functools.partial(add_kernel, len(terms), parts),
        out_shape=[in_hbm((rows // parts, width), jnp.float32) for _ in range(parts)],
        in_specs=[pl.BlockSpec(memory_space=pltpu.SMEM)] + [whole for _ in terms],
        out_specs=[block for _ in range(parts)],
        scratch_shapes=[pltpu.VMEM((rows, width), jnp.float32)],
        compiler_params=pltpu.CompilerParams(vmem_limit_bytes=VMEM_BYTES),
        cost_estimate=pl.CostEstimate(
            flops=len(terms) * rows * width,
            bytes_accessed=4 * (len(terms) + 1) * rows * width,
            transcendentals=0,
        ),
        name="add",
    )(me.reshape(1, 1), *terms)


def partners(axis, distance):
    return [(i, i ^ distance) for i in range(lax.axis_size(axis))]


def sum_over_slabs(keep, send):
    other = lax.ppermute(send, "mode", partners("mode", 1))
    count = lax.axis_size("space")
    blocks = add_and_cut([keep, other], lax.axis_index("space"), count)
    terms = [blocks[0]] + [
        lax.ppermute(blocks[k], "space", partners("space", k)) for k in range(1, count)
    ]
    return add_and_cut(terms, lax.axis_index("mode") // 2, lax.axis_size("mode") // 2)


def sum_over_modes(blocks):
    return blocks[0] + sum(
        lax.ppermute(block, "mode", partners("mode", 2 * k))
        for k, block in enumerate(blocks) if k > 0
    )


def finish_kernel(aliased, scale_ref, swap_ref, x_ref, *refs):
    out_ref = refs[aliased]
    parts, _, each, _, width = x_ref.shape
    rows = parts * each
    scale = scale_ref[0, 0]
    value = x_ref[...].reshape(rows * GROUP, width)
    for top in range(0, rows, GROUP):
        block = value[top * GROUP:(top + GROUP) * GROUP]
        block = scale * jnp.dot(swap_ref[...], block, preferred_element_type=jnp.float32)
        out_ref[:, 0, top:top + GROUP, :] = block.astype(jnp.bfloat16).reshape(GROUP, GROUP, width)


def finish_fields(first, arrived, scale, previous):
    parts, fields, each, modes, width = arrived.shape
    rows = parts * each
    swap = swap_matrix(GROUP, GROUP)
    operands = [scale.reshape(1, 1), swap, arrived, *previous]
    return pl.pallas_call(
        functools.partial(finish_kernel, len(previous)),
        grid=(fields, modes // GROUP),
        out_shape=jax.ShapeDtypeStruct((modes, 3, rows, width), jnp.bfloat16),
        in_specs=[
            pl.BlockSpec(memory_space=pltpu.SMEM),
            pl.BlockSpec(swap.shape, lambda f, m: (0, 0)),
            pl.BlockSpec((parts, 1, each, GROUP, width), lambda f, m: (0, f, 0, m, 0)),
        ] + [pl.BlockSpec(memory_space=pl.ANY) for _ in previous],
        out_specs=pl.BlockSpec((GROUP, 1, rows, width), lambda f, m: (m, first + f, 0, 0)),
        input_output_aliases={3: 0} if previous else {},
        compiler_params=pltpu.CompilerParams(vmem_limit_bytes=VMEM_BYTES),
        cost_estimate=pl.CostEstimate(
            flops=fields * modes * rows * width,
            bytes_accessed=4 * fields * modes * rows * width,
            transcendentals=0,
        ),
        name="finish",
    )(*operands)


def send_edges(first, last):
    count = lax.axis_size("space")
    forward = [(i, i + 1) for i in range(count - 1)]
    backward = [(target, source) for source, target in forward]
    return lax.ppermute(last, "space", forward), lax.ppermute(first, "space", backward)


def shards(sqrt_factors, model_error, water_depth, sea_mask, givens_transform):
    modes, fields, rows, width = sqrt_factors.shape
    parts = lax.axis_size("mode")
    count = modes // GROUP
    swap = functools.partial(
        lax.all_to_all, axis_name="mode", split_axis=0, concat_axis=0, tiled=True
    )

    near = min(count, 2)
    water_depth, sea_mask = (
        pltpu.with_memory_space_constraint(value, pltpu.HBM) for value in (water_depth, sea_mask)
    )
    head = send_edges(*cut_edges(0, near, sqrt_factors, (water_depth, sea_mask)))
    static = (*head, water_depth, sea_mask)
    cut = cut_edges(near, count - near, sqrt_factors, ()) if count > near else ()
    chunks = [swap(forecast_groups(0, 1, 0, 0, 1, cut, sqrt_factors, *head, *static))]
    rest = ()
    if near > 1:
        rest = (forecast_groups(1, 1, 1, 0, count - 1, rest, sqrt_factors, *head, *static),)
    if count > near:
        tail = send_edges(*cut)
        rest = (forecast_groups(
            near, count - near, 0, near - 1, count - 1, rest, sqrt_factors, *tail, *static
        ),)
    chunks += [swap(value) for value in rest]

    fault = model_error.transpose(1, 2, 0, 3)
    turn = givens_transform.T
    devices = lax.axis_size("space") * parts
    half = lax.rem(lax.axis_index("mode"), 2).reshape(1, 1)
    columns = turn.shape[1]
    cell_count = float(fields * rows * lax.axis_size("space") * width)

    arrived = swap(rotate_fields(0, 2, chunks, fault, turn, parts))
    blocks = sum_over_slabs(*local_gram(chunks, fault, turn, parts, devices, half))
    last = rotate_fields(2, fields - 2, chunks, fault, turn, parts)
    last, total = lax.optimization_barrier((last, sum_over_modes(blocks)))
    last = swap(last)
    gram = total[:columns // devices, :columns] / cell_count
    inflation = jnp.sqrt(total[0, columns] / total[0, columns + 1])

    reduced = finish_fields(0, arrived, inflation, ())
    reduced = finish_fields(2, last, inflation, (reduced,))
    return (reduced, gram, inflation)


def solution(mesh):
    in_specs = (
        P("mode", None, "space", None),
        P(None, None, ("space", "mode"), None),
        P("space", None),
        P("space", None),
        P(),
    )
    out_specs = (P("mode", None, "space", None), P(("space", "mode"), None), P())
    return jax.shard_map(shards, mesh=mesh, in_specs=in_specs, out_specs=out_specs, check_vma=False)
```

```python
import functools

import jax
import jax.numpy as jnp
import numpy as np
from jax import lax
from jax.experimental import pallas as pl
from jax.experimental.pallas import tpu as pltpu
from jax.sharding import PartitionSpec as P

flux_coef = 0.2
slope_coef = 0.2
turn_coef = 0.1
keep_coef = 0.95

GROUP = 16
HALO = 4
LANES = 128
MIB = 1024 * 1024


def column_diff(tiles):
    lane = lax.broadcasted_iota(jnp.int32, tiles[0].shape, 1)
    from_left = [pltpu.roll(tile, 1, 1) for tile in tiles]
    from_right = [pltpu.roll(tile, LANES - 1, 1) for tile in tiles]
    zero = jnp.zeros_like(tiles[0])
    out = []
    for t in range(len(tiles)):
        left = from_left[t - 1] if t > 0 else zero
        right = from_right[t + 1] if t + 1 < len(tiles) else zero
        previous = jnp.where(lane == 0, left, from_left[t])
        following = jnp.where(lane == LANES - 1, right, from_right[t])
        out.append(following - previous)
    return out


def swap_matrix(inner, outer):
    place = np.arange(inner * outer).reshape(outer, inner).T.reshape(-1)
    matrix = np.zeros((inner * outer, inner * outer), np.float32)
    matrix[np.arange(inner * outer), place] = 1.0
    return jnp.asarray(matrix, jnp.bfloat16)


def in_hbm(shape, dtype):
    return pltpu.HBM(shape, dtype)


def cut_edges_kernel(fixed, *refs):
    first_ref, last_ref = refs[:2]
    out_first, out_last = refs[-2:]
    group, fields = first_ref.shape[:2]
    for ref, out, low in ((first_ref, out_first, 0), (last_ref, out_last, GROUP - HALO)):
        for m in range(group):
            for field in range(fields):
                edge = ref[m, field].astype(jnp.float32)[low:low + HALO]
                out[m * fields + field] = edge.astype(jnp.bfloat16)
    if fixed:
        depth_ref, mask_ref = refs[2:4]
        for out, low in ((out_first, 0), (out_last, depth_ref.shape[0] - HALO)):
            rest = depth_ref[low:low + HALO]
            for piece in range(3):
                part = rest.astype(jnp.bfloat16)
                out[group * fields + piece] = part
                rest = rest - part.astype(jnp.float32)
            out[group * fields + 3] = mask_ref[low:low + HALO].astype(jnp.float32).astype(jnp.bfloat16)


def cut_edges(first, groups, factors, fixed):
    _, fields, rows, width = factors.shape
    size = GROUP * groups if fixed else GROUP
    steps = 1 if fixed else groups
    count = size * steps * fields + (4 if fixed else 0)
    block = size * fields + (4 if fixed else 0)
    out = in_hbm((count, HALO, width), jnp.bfloat16)
    return pl.pallas_call(
        functools.partial(cut_edges_kernel, bool(fixed)),
        grid=(steps,),
        out_shape=(out, out),
        in_specs=[
            pl.BlockSpec((size, fields, GROUP, width), lambda i: (first // (size // GROUP) + i, 0, 0, 0)),
            pl.BlockSpec((size, fields, GROUP, width),
                         lambda i: (first // (size // GROUP) + i, 0, rows // GROUP - 1, 0)),
        ] + [pl.BlockSpec(value.shape, lambda i: (0, 0)) for value in fixed],
        out_specs=[pl.BlockSpec((block, HALO, width), lambda i: (i, 0, 0))] * 2,
        compiler_params=pltpu.CompilerParams(vmem_limit_bytes=8 * MIB),
        cost_estimate=pl.CostEstimate(
            flops=0, bytes_accessed=5 * count * HALO * width * 2, transcendentals=0
        ),
        name="cut_edges",
    )(factors, factors, *fixed)


def block_of(count):
    return max(size for size in range(1, 55) if count % size == 0)


def forecast_kernel(x_ref, low_ref, high_ref, low_static, high_static, depth_ref, mask_ref,
                    swap_ref, swap_ends_ref, *refs):
    out_ref, cells, ends, depth, wet, surf1, east1, north1, surf2 = refs[-9:]
    _, fields, rows, width = x_ref.shape
    tiles = width // LANES
    spots = [slice(t * LANES, (t + 1) * LANES) for t in range(tiles)]

    ends[:, :HALO] = low_ref[...].astype(jnp.float32)
    ends[:, HALO:] = high_ref[...].astype(jnp.float32)
    for field in range(fields):
        for top in range(0, rows, GROUP):
            block = x_ref[:, field, top:top + GROUP, :].reshape(GROUP * GROUP, width)
            block = jnp.dot(swap_ref[...], block, preferred_element_type=jnp.float32)
            block = block * slope_coef if field == 0 else block
            cells[field, HALO + top:HALO + top + GROUP] = block.reshape(GROUP, GROUP, width)
        block = jnp.concatenate([ends[m * fields + field] for m in range(GROUP)], axis=0)
        block = jnp.dot(
            swap_ends_ref[...], block.astype(jnp.bfloat16), preferred_element_type=jnp.float32
        ).reshape(2 * HALO, GROUP, width)
        block = block * slope_coef if field == 0 else block
        cells[field, :HALO] = block[:HALO]
        cells[field, HALO + rows:] = block[HALO:]

    def place_static(place, depth_row, wet_row):
        depth[place] = jnp.broadcast_to(flux_coef * slope_coef * depth_row, (8, width))
        wet[place] = jnp.broadcast_to(wet_row, (8, width))

    for static, first in ((low_static, 0), (high_static, HALO + rows)):
        value = static[...].astype(jnp.float32)
        level = value[0] + value[1] + value[2]
        for j in range(HALO):
            place_static(first + j, level[j:j + 1], value[3, j:j + 1])
    for top in range(0, rows, 8):
        level = depth_ref[top:top + 8]
        sea = mask_ref[top:top + 8].astype(jnp.float32)
        for j in range(8):
            place_static(HALO + top + j, level[j:j + 1], sea[j:j + 1])

    def get(ref, i):
        return [ref[i, :, spot] for spot in spots]

    def get_field(field, i):
        return [cells[field, i + HALO, :, spot] for spot in spots]

    def get_static(ref, i):
        parts = [ref[i + HALO, :, spot] for spot in spots]
        return [jnp.concatenate([part] * (GROUP // 8), axis=0) for part in parts]

    def put(ref, i, values):
        for spot, value in zip(spots, values):
            ref[i, :, spot] = value

    def times(one, other):
        return [a * b for a, b in zip(one, other)]

    def over_rows(first, last, body):
        size = block_of(last - first)

        def block(k, carry):
            body(first + k * size, size)
            return carry

        lax.fori_loop(0, (last - first) // size, block, 0)

    def surfaces(i, size, surface_at, east_at, north_at, put_at):
        flux = {j: times(get_static(depth, i + j), north_at(i + j)) for j in (-1, 0)}
        for j in range(size):
            flux[j + 1] = times(get_static(depth, i + j + 1), north_at(i + j + 1))
            sides = column_diff(times(get_static(depth, i + j), east_at(i + j)))
            sea, surface = get_static(wet, i + j), surface_at(i + j)
            put_at(i + j, [
                sea[t] * (surface[t] - (sides[t] + (flux[j + 1][t] - flux[j - 1][t])))
                for t in range(tiles)
            ])

    def flows(i, size, surface_at, east_at, north_at, put_at):
        surface = {j: surface_at(i + j) for j in (-1, 0)}
        for j in range(size):
            surface[j + 1] = surface_at(i + j + 1)
            sides = column_diff(surface[j])
            sea, east, north = get_static(wet, i + j), east_at(i + j), north_at(i + j)
            put_at(i + j, surface[j], [
                sea[t] * (keep_coef * east[t] + turn_coef * north[t] - sides[t])
                for t in range(tiles)
            ], [
                sea[t] * (keep_coef * north[t] - turn_coef * east[t]
                          - (surface[j + 1][t] - surface[j - 1][t]))
                for t in range(tiles)
            ])

    def first_surface(i, size):
        surfaces(
            i, size, lambda r: get_field(0, r), lambda r: get_field(1, r),
            lambda r: get_field(2, r), lambda r, value: put(surf1, r + 3, value),
        )

    def first_flow(i, size):
        def put_flow(r, surface, east, north):
            put(east1, r + 2, east)
            put(north1, r + 2, north)

        flows(
            i, size, lambda r: get(surf1, r + 3), lambda r: get_field(1, r),
            lambda r: get_field(2, r), put_flow,
        )

    def second_surface(i, size):
        surfaces(
            i, size, lambda r: get(surf1, r + 3), lambda r: get(east1, r + 2),
            lambda r: get(north1, r + 2), lambda r, value: put(surf2, r + 1, value),
        )

    def second_flow(i, size):
        def put_out(r, surface, east, north):
            surface = [value * (1.0 / slope_coef) for value in surface]
            for field, values in enumerate((surface, east, north)):
                for spot, value in zip(spots, values):
                    out_ref[r, field, :, spot] = value.astype(jnp.bfloat16)

        flows(
            i, size, lambda r: get(surf2, r + 1), lambda r: get(east1, r + 2),
            lambda r: get(north1, r + 2), put_out,
        )

    over_rows(-3, rows + 3, first_surface)
    over_rows(-2, rows + 2, first_flow)
    over_rows(-1, rows + 1, second_surface)
    over_rows(0, rows, second_flow)


def forecast_groups(first, count, skip, place, whole_count, previous, factors, low, high,
                    static_low, static_high, depth, mask):
    modes, fields, rows, width = factors.shape
    padded = rows + 2 * HALO
    edge = GROUP * fields
    last = static_low.shape[0] // 4 - 1
    swap, swap_ends = swap_matrix(GROUP, GROUP), swap_matrix(2 * HALO, GROUP)

    def rows_of(count):
        return pltpu.VMEM((count, GROUP, width), jnp.float32)

    def whole(value):
        return pl.BlockSpec(value.shape, lambda i: (0,) * value.ndim)

    return pl.pallas_call(
        forecast_kernel,
        grid=(count,),
        out_shape=in_hbm((rows, fields, whole_count * GROUP, width), jnp.bfloat16),
        in_specs=[
            pl.BlockSpec((GROUP, fields, rows, width), lambda i: (first + i, 0, 0, 0)),
            pl.BlockSpec((edge, HALO, width), lambda i: (skip + i, 0, 0)),
            pl.BlockSpec((edge, HALO, width), lambda i: (skip + i, 0, 0)),
            pl.BlockSpec((4, HALO, width), lambda i: (last, 0, 0)),
            pl.BlockSpec((4, HALO, width), lambda i: (last, 0, 0)),
            whole(depth),
            whole(mask),
            whole(swap),
            whole(swap_ends),
        ] + [pl.BlockSpec(memory_space=pltpu.HBM) for _ in previous],
        out_specs=pl.BlockSpec((rows, fields, GROUP, width), lambda i: (0, 0, place + i, 0)),
        input_output_aliases={9: 0} if len(previous) == 1 else {},
        scratch_shapes=[
            pltpu.VMEM((fields, padded, GROUP, width), jnp.float32),
            pltpu.VMEM((edge, 2 * HALO, width), jnp.float32),
            pltpu.VMEM((padded, 8, width), jnp.float32),
            pltpu.VMEM((padded, 8, width), jnp.float32),
            rows_of(rows + 6),
            rows_of(rows + 4),
            rows_of(rows + 4),
            rows_of(rows + 2),
        ],
        compiler_params=pltpu.CompilerParams(vmem_limit_bytes=30 * MIB),
        cost_estimate=pl.CostEstimate(
            flops=60 * count * GROUP * rows * width,
            bytes_accessed=2 * 2 * count * GROUP * fields * rows * width,
            transcendentals=0,
        ),
        name="forecast",
    )(factors, low, high, static_low, static_high, depth, mask, swap, swap_ends, *previous)


def all_columns(chunk_refs, fault_ref, j):
    own = [ref[:, j, 0] for ref in chunk_refs]
    joined = jnp.concatenate(own, axis=1)
    return joined.reshape(-1, joined.shape[-1]), fault_ref[0, j]


def rotate_kernel(count, *refs):
    chunk_refs = refs[:count]
    fault_ref, turn_ref, out_ref = refs[count:]
    parts, _, size, modes, width = out_ref.shape
    for j in range(size):
        columns = jnp.concatenate(all_columns(chunk_refs, fault_ref, j), axis=0)
        value = jnp.dot(turn_ref[...], columns, preferred_element_type=jnp.float32)
        out_ref[:, 0, j] = value.astype(jnp.bfloat16).reshape(parts, modes, width)


def by_part(chunks, parts):
    return [c.reshape((parts, c.shape[0] // parts) + c.shape[1:]) for c in chunks]


def rotate_fields(first, fields, chunks, fault, turn, parts):
    width = chunks[0].shape[-1]
    each = chunks[0].shape[0] // parts
    kept = turn.shape[0]
    noise = fault.shape[2]
    modes = kept // parts
    size = 3 if each % 3 == 0 else 1
    views = by_part(chunks, parts)
    return pl.pallas_call(
        functools.partial(rotate_kernel, len(views)),
        grid=(fields, each // size),
        out_shape=in_hbm((parts, fields, each, modes, width), jnp.bfloat16),
        in_specs=[
            pl.BlockSpec((parts, size, 1, v.shape[3], width), lambda f, j: (0, j, first + f, 0, 0))
            for v in views
        ] + [
            pl.BlockSpec((1, size, noise, width), lambda f, j: (first + f, j, 0, 0)),
            pl.BlockSpec(turn.shape, lambda f, j: (0, 0)),
        ],
        out_specs=pl.BlockSpec((parts, 1, size, modes, width), lambda f, j: (0, f, j, 0, 0)),
        compiler_params=pltpu.CompilerParams(vmem_limit_bytes=16 * MIB),
        cost_estimate=pl.CostEstimate(
            flops=2 * fields * each * width * kept * turn.shape[1],
            bytes_accessed=2 * fields * each * width * (kept + turn.shape[1]),
            transcendentals=0,
        ),
        name="rotate",
    )(*views, fault, turn)


def gram_kernel(count, each, devices, *refs):
    chunk_refs = refs[:count]
    fault_ref, turn_ref, half_ref, keep_ref, send_ref, gram_ref = refs[count:]
    pairs = [all_columns(chunk_refs, fault_ref, j) for j in range(each)]
    columns = jnp.concatenate(
        [jnp.concatenate([prior, fault], axis=0) for prior, fault in pairs], axis=1
    )
    value = lax.dot_general(
        columns, columns, (((1,), (1,)), ((), ())), preferred_element_type=jnp.float32
    )
    step = pl.program_id(0)

    @pl.when(step == 0)
    def _():
        gram_ref[...] = value

    @pl.when(step > 0)
    def _():
        gram_ref[...] += value

    @pl.when(step == pl.num_programs(0) - 1)
    def _():
        gram = gram_ref[...]
        size = gram.shape[0]
        row = lax.broadcasted_iota(jnp.int32, gram.shape, 0)
        column = lax.broadcasted_iota(jnp.int32, gram.shape, 1)
        full = jnp.sum(jnp.where(row == column, gram, 0.0))
        turn = turn_ref[...]
        turned = 0.0
        for _ in range(3):
            piece = gram.astype(jnp.bfloat16)
            turned = turned + jnp.dot(turn, piece, preferred_element_type=jnp.float32)
            gram = gram - piece.astype(jnp.float32)
        kept = jnp.sum(turned * turn.astype(jnp.float32))
        own = size // devices
        slot = keep_ref.shape[0] // (devices // 2)
        lane = lax.broadcasted_iota(jnp.int32, (keep_ref.shape[0], LANES), 1)
        traces = jnp.where(lane == 0, full, jnp.where(lane == 1, kept, 0.0))
        low = half_ref[0, 0] == 0
        for out in (keep_ref, send_ref):
            if slot != own:
                out[...] = jnp.zeros_like(out)
            out[:, size:] = traces
        for q in range(devices // 2):
            even = gram_ref[2 * q * own:(2 * q + 1) * own]
            uneven = gram_ref[(2 * q + 1) * own:(2 * q + 2) * own]
            keep_ref[q * slot:q * slot + own, :size] = jnp.where(low, even, uneven)
            send_ref[q * slot:q * slot + own, :size] = jnp.where(low, uneven, even)


def local_gram(chunks, fault, turn, parts, devices, half):
    width = chunks[0].shape[-1]
    each = chunks[0].shape[0] // parts
    noise = fault.shape[2]
    columns = turn.shape[1]
    views = by_part(chunks, parts)
    slot = -(-columns // devices // 8) * 8
    slots = (devices // 2 * slot, columns + LANES)
    out = in_hbm(slots, jnp.float32)
    return pl.pallas_call(
        functools.partial(gram_kernel, len(views), each, devices),
        grid=(3,),
        out_shape=(out, out),
        in_specs=[
            pl.BlockSpec((parts, each, 1, v.shape[3], width), lambda f: (0, 0, f, 0, 0))
            for v in views
        ] + [
            pl.BlockSpec((1, each, noise, width), lambda f: (f, 0, 0, 0)),
            pl.BlockSpec(turn.shape, lambda f: (0, 0)),
            pl.BlockSpec(memory_space=pltpu.SMEM),
        ],
        out_specs=[pl.BlockSpec(slots, lambda f: (0, 0))] * 2,
        scratch_shapes=[pltpu.VMEM((columns, columns), jnp.float32)],
        compiler_params=pltpu.CompilerParams(vmem_limit_bytes=30 * MIB),
        cost_estimate=pl.CostEstimate(
            flops=2 * 3 * each * width * columns * columns,
            bytes_accessed=2 * 3 * each * width * columns,
            transcendentals=0,
        ),
        name="gram",
    )(*views, fault, turn, half)


def add_kernel(count, parts, me_ref, *refs):
    total = refs[0][...]
    for ref in refs[1:count]:
        total = total + ref[...]
    total_ref = refs[-1]
    total_ref[...] = total
    rows = total.shape[0] // parts
    for k in range(parts):
        first = pl.multiple_of(jnp.bitwise_xor(me_ref[0, 0], k) * rows, 8)
        refs[count + k][...] = total_ref[pl.ds(first, rows)]


def add_and_cut(terms, me, parts):
    rows, width = terms[0].shape
    whole = pl.BlockSpec((rows, width), lambda: (0, 0))
    block = pl.BlockSpec((rows // parts, width), lambda: (0, 0))
    return pl.pallas_call(
        functools.partial(add_kernel, len(terms), parts),
        out_shape=[in_hbm((rows // parts, width), jnp.float32) for _ in range(parts)],
        in_specs=[pl.BlockSpec(memory_space=pltpu.SMEM)] + [whole for _ in terms],
        out_specs=[block for _ in range(parts)],
        scratch_shapes=[pltpu.VMEM((rows, width), jnp.float32)],
        compiler_params=pltpu.CompilerParams(vmem_limit_bytes=8 * MIB),
        cost_estimate=pl.CostEstimate(
            flops=len(terms) * rows * width,
            bytes_accessed=4 * (len(terms) + 1) * rows * width,
            transcendentals=0,
        ),
        name="add",
    )(me.reshape(1, 1), *terms)


def partners(axis, distance):
    return [(i, i ^ distance) for i in range(lax.axis_size(axis))]


def sum_over_slabs(keep, send):
    other = lax.ppermute(send, "mode", partners("mode", 1))
    count = lax.axis_size("space")
    blocks = add_and_cut([keep, other], lax.axis_index("space"), count)
    terms = [blocks[0]] + [
        lax.ppermute(blocks[k], "space", partners("space", k)) for k in range(1, count)
    ]
    return add_and_cut(terms, lax.axis_index("mode") // 2, lax.axis_size("mode") // 2)


def sum_over_modes(blocks):
    return blocks[0] + sum(
        lax.ppermute(block, "mode", partners("mode", 2 * k))
        for k, block in enumerate(blocks) if k > 0
    )


def finish_kernel(aliased, scale_ref, swap_ref, x_ref, *refs):
    out_ref = refs[aliased]
    parts, _, each, _, width = x_ref.shape
    rows = parts * each
    scale = scale_ref[0, 0]
    value = x_ref[...].reshape(rows * GROUP, width)
    for top in range(0, rows, GROUP):
        block = value[top * GROUP:(top + GROUP) * GROUP]
        block = scale * jnp.dot(swap_ref[...], block, preferred_element_type=jnp.float32)
        out_ref[:, 0, top:top + GROUP, :] = block.astype(jnp.bfloat16).reshape(GROUP, GROUP, width)


def finish_fields(first, arrived, scale, previous):
    parts, fields, each, modes, width = arrived.shape
    rows = parts * each
    swap = swap_matrix(GROUP, GROUP)
    operands = [scale.reshape(1, 1), swap, arrived, *previous]
    return pl.pallas_call(
        functools.partial(finish_kernel, len(previous)),
        grid=(fields, modes // GROUP),
        out_shape=jax.ShapeDtypeStruct((modes, 3, rows, width), jnp.bfloat16),
        in_specs=[
            pl.BlockSpec(memory_space=pltpu.SMEM),
            pl.BlockSpec(swap.shape, lambda f, m: (0, 0)),
            pl.BlockSpec((parts, 1, each, GROUP, width), lambda f, m: (0, f, 0, m, 0)),
        ] + [pl.BlockSpec(memory_space=pltpu.HBM) for _ in previous],
        out_specs=pl.BlockSpec((GROUP, 1, rows, width), lambda f, m: (m, first + f, 0, 0)),
        input_output_aliases={3: 0} if previous else {},
        compiler_params=pltpu.CompilerParams(vmem_limit_bytes=10 * MIB),
        cost_estimate=pl.CostEstimate(
            flops=fields * modes * rows * width,
            bytes_accessed=4 * fields * modes * rows * width,
            transcendentals=0,
        ),
        name="finish",
    )(*operands)


def send_edges(first, last):
    count = lax.axis_size("space")
    forward = [(i, i + 1) for i in range(count - 1)]
    backward = [(target, source) for source, target in forward]
    return lax.ppermute(last, "space", forward), lax.ppermute(first, "space", backward)


def shards(sqrt_factors, model_error, water_depth, sea_mask, givens_transform):
    modes, fields, rows, width = sqrt_factors.shape
    parts = lax.axis_size("mode")
    count = modes // GROUP
    swap = functools.partial(
        lax.all_to_all, axis_name="mode", split_axis=0, concat_axis=0, tiled=True
    )

    near = min(count, 2)
    water_depth, sea_mask = (
        pltpu.with_memory_space_constraint(value, pltpu.HBM) for value in (water_depth, sea_mask)
    )
    factors = pltpu.with_memory_space_constraint(sqrt_factors, pltpu.HBM)
    head = send_edges(*cut_edges(0, near, factors, (water_depth, sea_mask)))
    static = (*head, water_depth, sea_mask)
    cut = cut_edges(near, count - near, factors, ()) if count > near else ()
    chunks = [swap(forecast_groups(0, 1, 0, 0, 1, cut, sqrt_factors, *head, *static))]
    rest = ()
    if near > 1:
        rest = (forecast_groups(1, 1, 1, 0, count - 1, rest, sqrt_factors, *head, *static),)
    if count > near:
        tail = send_edges(*cut)
        rest = (forecast_groups(
            near, count - near, 0, near - 1, count - 1, rest, sqrt_factors, *tail, *static
        ),)
    chunks += [swap(value) for value in rest]

    fault = model_error.transpose(1, 2, 0, 3)
    turn = givens_transform.T
    devices = lax.axis_size("space") * parts
    half = lax.rem(lax.axis_index("mode"), 2).reshape(1, 1)
    columns = turn.shape[1]
    cell_count = float(fields * rows * lax.axis_size("space") * width)

    arrived = swap(rotate_fields(0, 2, chunks, fault, turn, parts))
    blocks = sum_over_slabs(*local_gram(chunks, fault, turn, parts, devices, half))
    last = rotate_fields(2, fields - 2, chunks, fault, turn, parts)
    last, total = lax.optimization_barrier((last, sum_over_modes(blocks)))
    last = swap(last)
    gram = total[:columns // devices, :columns] / cell_count
    inflation = jnp.sqrt(total[0, columns] / total[0, columns + 1])

    reduced = finish_fields(0, arrived, inflation, ())
    reduced = finish_fields(2, last, inflation, (reduced,))
    return (reduced, gram, inflation)


def solution(mesh):
    in_specs = (
        P("mode", None, "space", None),
        P(None, None, ("space", "mode"), None),
        P("space", None),
        P("space", None),
        P(),
    )
    out_specs = (P("mode", None, "space", None), P(("space", "mode"), None), P())
    return jax.shard_map(shards, mesh=mesh, in_specs=in_specs, out_specs=out_specs, check_vma=False)
```

```python
import functools

import jax
import jax.numpy as jnp
import numpy as np
from jax import lax
from jax.experimental import pallas as pl
from jax.experimental.pallas import tpu as pltpu
from jax.sharding import PartitionSpec as P

flux_coef = 0.2
slope_coef = 0.2
turn_coef = 0.1
keep_coef = 0.95

GROUP = 16
HALO = 4
LANES = 128
VMEM_BYTES = 48 * 1024 * 1024


def column_diff(tiles):
    lane = lax.broadcasted_iota(jnp.int32, tiles[0].shape, 1)
    from_left = [pltpu.roll(tile, 1, 1) for tile in tiles]
    from_right = [pltpu.roll(tile, LANES - 1, 1) for tile in tiles]
    zero = jnp.zeros_like(tiles[0])
    out = []
    for t in range(len(tiles)):
        left = from_left[t - 1] if t > 0 else zero
        right = from_right[t + 1] if t + 1 < len(tiles) else zero
        previous = jnp.where(lane == 0, left, from_left[t])
        following = jnp.where(lane == LANES - 1, right, from_right[t])
        out.append(following - previous)
    return out


def swap_matrix(inner, outer):
    place = np.arange(inner * outer).reshape(outer, inner).T.reshape(-1)
    matrix = np.zeros((inner * outer, inner * outer), np.float32)
    matrix[np.arange(inner * outer), place] = 1.0
    return jnp.asarray(matrix, jnp.bfloat16)


def in_hbm(shape, dtype):
    return pltpu.HBM(shape, dtype)


def cut_edges_kernel(fixed, *refs):
    first_ref, last_ref = refs[:2]
    out_first, out_last = refs[-2:]
    group, fields = first_ref.shape[:2]
    for ref, out, low in ((first_ref, out_first, 0), (last_ref, out_last, GROUP - HALO)):
        for m in range(group):
            for field in range(fields):
                edge = ref[m, field].astype(jnp.float32)[low:low + HALO]
                out[m * fields + field] = edge.astype(jnp.bfloat16)
    if fixed:
        depth_ref, mask_ref = refs[2:4]
        for out, low in ((out_first, 0), (out_last, depth_ref.shape[0] - HALO)):
            rest = depth_ref[low:low + HALO]
            for piece in range(3):
                part = rest.astype(jnp.bfloat16)
                out[group * fields + piece] = part
                rest = rest - part.astype(jnp.float32)
            out[group * fields + 3] = mask_ref[low:low + HALO].astype(jnp.float32).astype(jnp.bfloat16)


def cut_edges(first, groups, factors, fixed):
    _, fields, rows, width = factors.shape
    size = GROUP * groups if fixed else GROUP
    steps = 1 if fixed else groups
    count = size * steps * fields + (4 if fixed else 0)
    block = size * fields + (4 if fixed else 0)
    out = in_hbm((count, HALO, width), jnp.bfloat16)
    return pl.pallas_call(
        functools.partial(cut_edges_kernel, bool(fixed)),
        grid=(steps,),
        out_shape=(out, out),
        in_specs=[
            pl.BlockSpec((size, fields, GROUP, width), lambda i: (first // (size // GROUP) + i, 0, 0, 0)),
            pl.BlockSpec((size, fields, GROUP, width),
                         lambda i: (first // (size // GROUP) + i, 0, rows // GROUP - 1, 0)),
        ] + [pl.BlockSpec(value.shape, lambda i: (0, 0)) for value in fixed],
        out_specs=[pl.BlockSpec((block, HALO, width), lambda i: (i, 0, 0))] * 2,
        compiler_params=pltpu.CompilerParams(vmem_limit_bytes=VMEM_BYTES),
        cost_estimate=pl.CostEstimate(
            flops=0, bytes_accessed=5 * count * HALO * width * 2, transcendentals=0
        ),
        name="cut_edges",
    )(factors, factors, *fixed)


def block_of(count):
    return max(size for size in range(1, 55) if count % size == 0)


def forecast_kernel(x_ref, low_ref, high_ref, low_static, high_static, depth_ref, mask_ref,
                    swap_ref, swap_ends_ref, *refs):
    out_ref, cells, ends, depth, wet, surf1, east1, north1, surf2 = refs[-9:]
    _, fields, rows, width = x_ref.shape
    tiles = width // LANES
    spots = [slice(t * LANES, (t + 1) * LANES) for t in range(tiles)]

    ends[:, :HALO] = low_ref[...].astype(jnp.float32)
    ends[:, HALO:] = high_ref[...].astype(jnp.float32)
    for field in range(fields):
        for top in range(0, rows, GROUP):
            block = x_ref[:, field, top:top + GROUP, :].reshape(GROUP * GROUP, width)
            block = jnp.dot(swap_ref[...], block, preferred_element_type=jnp.float32)
            block = block * slope_coef if field == 0 else block
            cells[field, HALO + top:HALO + top + GROUP] = block.reshape(GROUP, GROUP, width)
        block = jnp.concatenate([ends[m * fields + field] for m in range(GROUP)], axis=0)
        block = jnp.dot(
            swap_ends_ref[...], block.astype(jnp.bfloat16), preferred_element_type=jnp.float32
        ).reshape(2 * HALO, GROUP, width)
        block = block * slope_coef if field == 0 else block
        cells[field, :HALO] = block[:HALO]
        cells[field, HALO + rows:] = block[HALO:]

    def place_static(place, depth_row, wet_row):
        depth[place] = jnp.broadcast_to(flux_coef * slope_coef * depth_row, (8, width))
        wet[place] = jnp.broadcast_to(wet_row, (8, width))

    for static, first in ((low_static, 0), (high_static, HALO + rows)):
        value = static[...].astype(jnp.float32)
        level = value[0] + value[1] + value[2]
        for j in range(HALO):
            place_static(first + j, level[j:j + 1], value[3, j:j + 1])
    for top in range(0, rows, 8):
        level = depth_ref[top:top + 8]
        sea = mask_ref[top:top + 8].astype(jnp.float32)
        for j in range(8):
            place_static(HALO + top + j, level[j:j + 1], sea[j:j + 1])

    def get(ref, i):
        return [ref[i, :, spot] for spot in spots]

    def get_field(field, i):
        return [cells[field, i + HALO, :, spot] for spot in spots]

    def get_static(ref, i):
        parts = [ref[i + HALO, :, spot] for spot in spots]
        return [jnp.concatenate([part] * (GROUP // 8), axis=0) for part in parts]

    def put(ref, i, values):
        for spot, value in zip(spots, values):
            ref[i, :, spot] = value

    def times(one, other):
        return [a * b for a, b in zip(one, other)]

    def over_rows(first, last, body):
        size = block_of(last - first)

        def block(k, carry):
            body(first + k * size, size)
            return carry

        lax.fori_loop(0, (last - first) // size, block, 0)

    def surfaces(i, size, surface_at, east_at, north_at, put_at):
        flux = {j: times(get_static(depth, i + j), north_at(i + j)) for j in (-1, 0)}
        for j in range(size):
            flux[j + 1] = times(get_static(depth, i + j + 1), north_at(i + j + 1))
            sides = column_diff(times(get_static(depth, i + j), east_at(i + j)))
            sea, surface = get_static(wet, i + j), surface_at(i + j)
            put_at(i + j, [
                sea[t] * (surface[t] - (sides[t] + (flux[j + 1][t] - flux[j - 1][t])))
                for t in range(tiles)
            ])

    def flows(i, size, surface_at, east_at, north_at, put_at):
        surface = {j: surface_at(i + j) for j in (-1, 0)}
        for j in range(size):
            surface[j + 1] = surface_at(i + j + 1)
            sides = column_diff(surface[j])
            sea, east, north = get_static(wet, i + j), east_at(i + j), north_at(i + j)
            put_at(i + j, surface[j], [
                sea[t] * (keep_coef * east[t] + turn_coef * north[t] - sides[t])
                for t in range(tiles)
            ], [
                sea[t] * (keep_coef * north[t] - turn_coef * east[t]
                          - (surface[j + 1][t] - surface[j - 1][t]))
                for t in range(tiles)
            ])

    def first_surface(i, size):
        surfaces(
            i, size, lambda r: get_field(0, r), lambda r: get_field(1, r),
            lambda r: get_field(2, r), lambda r, value: put(surf1, r + 3, value),
        )

    def first_flow(i, size):
        def put_flow(r, surface, east, north):
            put(east1, r + 2, east)
            put(north1, r + 2, north)

        flows(
            i, size, lambda r: get(surf1, r + 3), lambda r: get_field(1, r),
            lambda r: get_field(2, r), put_flow,
        )

    def second_surface(i, size):
        surfaces(
            i, size, lambda r: get(surf1, r + 3), lambda r: get(east1, r + 2),
            lambda r: get(north1, r + 2), lambda r, value: put(surf2, r + 1, value),
        )

    def second_flow(i, size):
        def put_out(r, surface, east, north):
            surface = [value * (1.0 / slope_coef) for value in surface]
            for field, values in enumerate((surface, east, north)):
                for spot, value in zip(spots, values):
                    out_ref[r, field, :, spot] = value.astype(jnp.bfloat16)

        flows(
            i, size, lambda r: get(surf2, r + 1), lambda r: get(east1, r + 2),
            lambda r: get(north1, r + 2), put_out,
        )

    over_rows(-3, rows + 3, first_surface)
    over_rows(-2, rows + 2, first_flow)
    over_rows(-1, rows + 1, second_surface)
    over_rows(0, rows, second_flow)


def forecast_groups(first, count, skip, place, whole_count, previous, factors, low, high,
                    static_low, static_high, depth, mask):
    modes, fields, rows, width = factors.shape
    padded = rows + 2 * HALO
    edge = GROUP * fields
    last = static_low.shape[0] // 4 - 1
    swap, swap_ends = swap_matrix(GROUP, GROUP), swap_matrix(2 * HALO, GROUP)

    def rows_of(count):
        return pltpu.VMEM((count, GROUP, width), jnp.float32)

    def whole(value):
        return pl.BlockSpec(value.shape, lambda i: (0,) * value.ndim)

    return pl.pallas_call(
        forecast_kernel,
        grid=(count,),
        out_shape=in_hbm((rows, fields, whole_count * GROUP, width), jnp.bfloat16),
        in_specs=[
            pl.BlockSpec((GROUP, fields, rows, width), lambda i: (first + i, 0, 0, 0)),
            pl.BlockSpec((edge, HALO, width), lambda i: (skip + i, 0, 0)),
            pl.BlockSpec((edge, HALO, width), lambda i: (skip + i, 0, 0)),
            pl.BlockSpec((4, HALO, width), lambda i: (last, 0, 0)),
            pl.BlockSpec((4, HALO, width), lambda i: (last, 0, 0)),
            whole(depth),
            whole(mask),
            whole(swap),
            whole(swap_ends),
        ] + [pl.BlockSpec(memory_space=pltpu.HBM) for _ in previous],
        out_specs=pl.BlockSpec((rows, fields, GROUP, width), lambda i: (0, 0, place + i, 0)),
        input_output_aliases={9: 0} if previous else {},
        scratch_shapes=[
            pltpu.VMEM((fields, padded, GROUP, width), jnp.float32),
            pltpu.VMEM((edge, 2 * HALO, width), jnp.float32),
            pltpu.VMEM((padded, 8, width), jnp.float32),
            pltpu.VMEM((padded, 8, width), jnp.float32),
            rows_of(rows + 6),
            rows_of(rows + 4),
            rows_of(rows + 4),
            rows_of(rows + 2),
        ],
        compiler_params=pltpu.CompilerParams(vmem_limit_bytes=VMEM_BYTES),
        cost_estimate=pl.CostEstimate(
            flops=60 * count * GROUP * rows * width,
            bytes_accessed=2 * 2 * count * GROUP * fields * rows * width,
            transcendentals=0,
        ),
        name="forecast",
    )(factors, low, high, static_low, static_high, depth, mask, swap, swap_ends, *previous)


def all_columns(chunk_refs, fault_ref, j):
    own = [ref[:, j, 0] for ref in chunk_refs]
    joined = jnp.concatenate(own, axis=1)
    return joined.reshape(-1, joined.shape[-1]), fault_ref[0, j]


def rotate_kernel(count, *refs):
    chunk_refs = refs[:count]
    fault_ref, turn_ref, out_ref = refs[count:]
    parts, _, size, modes, width = out_ref.shape
    for j in range(size):
        columns = jnp.concatenate(all_columns(chunk_refs, fault_ref, j), axis=0)
        value = jnp.dot(turn_ref[...], columns, preferred_element_type=jnp.float32)
        out_ref[:, 0, j] = value.astype(jnp.bfloat16).reshape(parts, modes, width)


def by_part(chunks, parts):
    return [c.reshape((parts, c.shape[0] // parts) + c.shape[1:]) for c in chunks]


def rotate_fields(first, fields, chunks, fault, turn, parts):
    width = chunks[0].shape[-1]
    each = chunks[0].shape[0] // parts
    kept = turn.shape[0]
    noise = fault.shape[2]
    modes = kept // parts
    size = 3 if each % 3 == 0 else 1
    views = by_part(chunks, parts)
    return pl.pallas_call(
        functools.partial(rotate_kernel, len(views)),
        grid=(fields, each // size),
        out_shape=in_hbm((parts, fields, each, modes, width), jnp.bfloat16),
        in_specs=[
            pl.BlockSpec((parts, size, 1, v.shape[3], width), lambda f, j: (0, j, first + f, 0, 0))
            for v in views
        ] + [
            pl.BlockSpec((1, size, noise, width), lambda f, j: (first + f, j, 0, 0)),
            pl.BlockSpec(turn.shape, lambda f, j: (0, 0)),
        ],
        out_specs=pl.BlockSpec((parts, 1, size, modes, width), lambda f, j: (0, f, j, 0, 0)),
        compiler_params=pltpu.CompilerParams(vmem_limit_bytes=VMEM_BYTES),
        cost_estimate=pl.CostEstimate(
            flops=2 * fields * each * width * kept * turn.shape[1],
            bytes_accessed=2 * fields * each * width * (kept + turn.shape[1]),
            transcendentals=0,
        ),
        name="rotate",
    )(*views, fault, turn)


def rotate_blocks_kernel(parts, count, me_ref, *refs):
    chunk_refs = refs[:count]
    fault_ref, turn_ref = refs[count:count + 2]
    out_refs, turned = refs[count + 2:-1], refs[-1]
    size, modes, _ = out_refs[0].shape
    for j in range(size):
        columns = jnp.concatenate(all_columns(chunk_refs, fault_ref, j), axis=0)
        value = jnp.dot(turn_ref[...], columns, preferred_element_type=jnp.float32)
        turned[j] = value.astype(jnp.bfloat16)
        for k in range(parts):
            first = pl.multiple_of(jnp.bitwise_xor(me_ref[0, 0], k) * modes, GROUP)
            out_refs[k][j] = turned[j, pl.ds(first, modes)]


def rotate_blocks(field, chunks, fault, turn, parts, me):
    width = chunks[0].shape[-1]
    each = chunks[0].shape[0] // parts
    kept = turn.shape[0]
    noise = fault.shape[2]
    modes = kept // parts
    size = 3 if each % 3 == 0 else 1
    views = by_part(chunks, parts)
    return pl.pallas_call(
        functools.partial(rotate_blocks_kernel, parts, len(views)),
        grid=(each // size,),
        out_shape=[in_hbm((each, modes, width), jnp.bfloat16) for _ in range(parts)],
        in_specs=[pl.BlockSpec(memory_space=pltpu.SMEM)] + [
            pl.BlockSpec((parts, size, 1, v.shape[3], width), lambda j: (0, j, field, 0, 0))
            for v in views
        ] + [
            pl.BlockSpec((1, size, noise, width), lambda j: (field, j, 0, 0)),
            pl.BlockSpec(turn.shape, lambda j: (0, 0)),
        ],
        out_specs=[pl.BlockSpec((size, modes, width), lambda j: (j, 0, 0)) for _ in range(parts)],
        scratch_shapes=[pltpu.VMEM((size, kept, width), jnp.bfloat16)],
        compiler_params=pltpu.CompilerParams(vmem_limit_bytes=VMEM_BYTES),
        cost_estimate=pl.CostEstimate(
            flops=2 * each * width * kept * turn.shape[1],
            bytes_accessed=2 * each * width * (kept + turn.shape[1]),
            transcendentals=0,
        ),
        name="rotate_blocks",
    )(me, *views, fault, turn)


def gram_kernel(count, each, devices, *refs):
    chunk_refs = refs[:count]
    fault_ref, turn_ref, half_ref, keep_ref, send_ref, gram_ref = refs[count:]
    pairs = [all_columns(chunk_refs, fault_ref, j) for j in range(each)]
    columns = jnp.concatenate(
        [jnp.concatenate([prior, fault], axis=0) for prior, fault in pairs], axis=1
    )
    value = lax.dot_general(
        columns, columns, (((1,), (1,)), ((), ())), preferred_element_type=jnp.float32
    )
    step = pl.program_id(0)

    @pl.when(step == 0)
    def _():
        gram_ref[...] = value

    @pl.when(step > 0)
    def _():
        gram_ref[...] += value

    @pl.when(step == pl.num_programs(0) - 1)
    def _():
        gram = gram_ref[...]
        size = gram.shape[0]
        row = lax.broadcasted_iota(jnp.int32, gram.shape, 0)
        column = lax.broadcasted_iota(jnp.int32, gram.shape, 1)
        full = jnp.sum(jnp.where(row == column, gram, 0.0))
        turn = turn_ref[...]
        turned = 0.0
        for _ in range(3):
            piece = gram.astype(jnp.bfloat16)
            turned = turned + jnp.dot(turn, piece, preferred_element_type=jnp.float32)
            gram = gram - piece.astype(jnp.float32)
        kept = jnp.sum(turned * turn.astype(jnp.float32))
        own = size // devices
        slot = keep_ref.shape[0] // (devices // 2)
        lane = lax.broadcasted_iota(jnp.int32, (keep_ref.shape[0], LANES), 1)
        traces = jnp.where(lane == 0, full, jnp.where(lane == 1, kept, 0.0))
        low = half_ref[0, 0] == 0
        for out in (keep_ref, send_ref):
            if slot != own:
                out[...] = jnp.zeros_like(out)
            out[:, size:] = traces
        for q in range(devices // 2):
            even = gram_ref[2 * q * own:(2 * q + 1) * own]
            uneven = gram_ref[(2 * q + 1) * own:(2 * q + 2) * own]
            keep_ref[q * slot:q * slot + own, :size] = jnp.where(low, even, uneven)
            send_ref[q * slot:q * slot + own, :size] = jnp.where(low, uneven, even)


def local_gram(chunks, fault, turn, parts, devices, half):
    width = chunks[0].shape[-1]
    each = chunks[0].shape[0] // parts
    noise = fault.shape[2]
    columns = turn.shape[1]
    views = by_part(chunks, parts)
    slot = -(-columns // devices // 8) * 8
    slots = (devices // 2 * slot, columns + LANES)
    out = in_hbm(slots, jnp.float32)
    return pl.pallas_call(
        functools.partial(gram_kernel, len(views), each, devices),
        grid=(3,),
        out_shape=(out, out),
        in_specs=[
            pl.BlockSpec((parts, each, 1, v.shape[3], width), lambda f: (0, 0, f, 0, 0))
            for v in views
        ] + [
            pl.BlockSpec((1, each, noise, width), lambda f: (f, 0, 0, 0)),
            pl.BlockSpec(turn.shape, lambda f: (0, 0)),
            pl.BlockSpec(memory_space=pltpu.SMEM),
        ],
        out_specs=[pl.BlockSpec(slots, lambda f: (0, 0))] * 2,
        scratch_shapes=[pltpu.VMEM((columns, columns), jnp.float32)],
        compiler_params=pltpu.CompilerParams(vmem_limit_bytes=VMEM_BYTES),
        cost_estimate=pl.CostEstimate(
            flops=2 * 3 * each * width * columns * columns,
            bytes_accessed=2 * 3 * each * width * columns,
            transcendentals=0,
        ),
        name="gram",
    )(*views, fault, turn, half)


def add_kernel(count, parts, me_ref, *refs):
    total = refs[0][...]
    for ref in refs[1:count]:
        total = total + ref[...]
    total_ref = refs[-1]
    total_ref[...] = total
    rows = total.shape[0] // parts
    for k in range(parts):
        first = pl.multiple_of(jnp.bitwise_xor(me_ref[0, 0], k) * rows, 8)
        refs[count + k][...] = total_ref[pl.ds(first, rows)]


def add_and_cut(terms, me, parts):
    rows, width = terms[0].shape
    whole = pl.BlockSpec((rows, width), lambda: (0, 0))
    block = pl.BlockSpec((rows // parts, width), lambda: (0, 0))
    return pl.pallas_call(
        functools.partial(add_kernel, len(terms), parts),
        out_shape=[in_hbm((rows // parts, width), jnp.float32) for _ in range(parts)],
        in_specs=[pl.BlockSpec(memory_space=pltpu.SMEM)] + [whole for _ in terms],
        out_specs=[block for _ in range(parts)],
        scratch_shapes=[pltpu.VMEM((rows, width), jnp.float32)],
        compiler_params=pltpu.CompilerParams(vmem_limit_bytes=VMEM_BYTES),
        cost_estimate=pl.CostEstimate(
            flops=len(terms) * rows * width,
            bytes_accessed=4 * (len(terms) + 1) * rows * width,
            transcendentals=0,
        ),
        name="add",
    )(me.reshape(1, 1), *terms)


def partners(axis, distance):
    return [(i, i ^ distance) for i in range(lax.axis_size(axis))]


def sum_over_slabs(keep, send):
    other = lax.ppermute(send, "mode", partners("mode", 1))
    count = lax.axis_size("space")
    blocks = add_and_cut([keep, other], lax.axis_index("space"), count)
    terms = [blocks[0]] + [
        lax.ppermute(blocks[k], "space", partners("space", k)) for k in range(1, count)
    ]
    return add_and_cut(terms, lax.axis_index("mode") // 2, lax.axis_size("mode") // 2)


def sum_over_modes(blocks):
    return blocks[0] + sum(
        lax.ppermute(block, "mode", partners("mode", 2 * k))
        for k, block in enumerate(blocks) if k > 0
    )


def finish_kernel(aliased, scale_ref, swap_ref, x_ref, *refs):
    out_ref = refs[aliased]
    parts, _, each, _, width = x_ref.shape
    rows = parts * each
    scale = scale_ref[0, 0]
    value = x_ref[...].reshape(rows * GROUP, width)
    for top in range(0, rows, GROUP):
        block = value[top * GROUP:(top + GROUP) * GROUP]
        block = scale * jnp.dot(swap_ref[...], block, preferred_element_type=jnp.float32)
        out_ref[:, 0, top:top + GROUP, :] = block.astype(jnp.bfloat16).reshape(GROUP, GROUP, width)


def finish_blocks_kernel(parts, me_ref, scale_ref, swap_ref, *refs):
    block_refs = refs[:parts]
    out_ref, cells = refs[-2:]
    each, _, width = block_refs[0].shape
    rows = parts * each
    for k in range(parts):
        first = pl.multiple_of(jnp.bitwise_xor(me_ref[0, 0], k) * (each * GROUP), GROUP)
        cells[pl.ds(first, each * GROUP)] = block_refs[k][...].reshape(each * GROUP, width)
    scale = scale_ref[0, 0]
    for top in range(0, rows, GROUP):
        block = cells[top * GROUP:(top + GROUP) * GROUP]
        block = scale * jnp.dot(swap_ref[...], block, preferred_element_type=jnp.float32)
        out_ref[:, 0, top:top + GROUP, :] = block.astype(jnp.bfloat16).reshape(GROUP, GROUP, width)


def finish_blocks(field, arrived, me, scale, previous):
    parts = len(arrived)
    each, modes, width = arrived[0].shape
    rows = parts * each
    swap = swap_matrix(GROUP, GROUP)
    return pl.pallas_call(
        functools.partial(finish_blocks_kernel, parts),
        grid=(modes // GROUP,),
        out_shape=jax.ShapeDtypeStruct((modes, 3, rows, width), jnp.bfloat16),
        in_specs=[
            pl.BlockSpec(memory_space=pltpu.SMEM),
            pl.BlockSpec(memory_space=pltpu.SMEM),
            pl.BlockSpec(swap.shape, lambda m: (0, 0)),
        ] + [pl.BlockSpec((each, GROUP, width), lambda m: (0, m, 0)) for _ in arrived] + [
            pl.BlockSpec(memory_space=pltpu.HBM)
        ],
        out_specs=pl.BlockSpec((GROUP, 1, rows, width), lambda m: (m, field, 0, 0)),
        scratch_shapes=[pltpu.VMEM((rows * GROUP, width), jnp.bfloat16)],
        input_output_aliases={3 + parts: 0},
        compiler_params=pltpu.CompilerParams(vmem_limit_bytes=VMEM_BYTES),
        cost_estimate=pl.CostEstimate(
            flops=modes * rows * width,
            bytes_accessed=4 * modes * rows * width,
            transcendentals=0,
        ),
        name="finish_blocks",
    )(me, scale.reshape(1, 1), swap, *arrived, previous)


def exchange(blocks):
    arrived = {0: blocks[0]}
    for k in reversed(range(1, len(blocks))):
        arrived[k] = lax.ppermute(blocks[k], "mode", partners("mode", k))
    return [arrived[k] for k in range(len(blocks))]


def finish_fields(first, arrived, scale, previous):
    parts, fields, each, modes, width = arrived.shape
    rows = parts * each
    swap = swap_matrix(GROUP, GROUP)
    operands = [scale.reshape(1, 1), swap, arrived, *previous]
    return pl.pallas_call(
        functools.partial(finish_kernel, len(previous)),
        grid=(fields, modes // GROUP),
        out_shape=jax.ShapeDtypeStruct((modes, 3, rows, width), jnp.bfloat16),
        in_specs=[
            pl.BlockSpec(memory_space=pltpu.SMEM),
            pl.BlockSpec(swap.shape, lambda f, m: (0, 0)),
            pl.BlockSpec((parts, 1, each, GROUP, width), lambda f, m: (0, f, 0, m, 0)),
        ] + [pl.BlockSpec(memory_space=pltpu.HBM) for _ in previous],
        out_specs=pl.BlockSpec((GROUP, 1, rows, width), lambda f, m: (m, first + f, 0, 0)),
        input_output_aliases={3: 0} if previous else {},
        compiler_params=pltpu.CompilerParams(vmem_limit_bytes=VMEM_BYTES),
        cost_estimate=pl.CostEstimate(
            flops=fields * modes * rows * width,
            bytes_accessed=4 * fields * modes * rows * width,
            transcendentals=0,
        ),
        name="finish",
    )(*operands)


def send_edges(first, last):
    count = lax.axis_size("space")
    forward = [(i, i + 1) for i in range(count - 1)]
    backward = [(target, source) for source, target in forward]
    return lax.ppermute(last, "space", forward), lax.ppermute(first, "space", backward)


def shards(sqrt_factors, model_error, water_depth, sea_mask, givens_transform):
    modes, fields, rows, width = sqrt_factors.shape
    parts = lax.axis_size("mode")
    count = modes // GROUP
    swap = functools.partial(
        lax.all_to_all, axis_name="mode", split_axis=0, concat_axis=0, tiled=True
    )

    near = min(count, 2)
    water_depth, sea_mask = (
        pltpu.with_memory_space_constraint(value, pltpu.HBM) for value in (water_depth, sea_mask)
    )
    factors = pltpu.with_memory_space_constraint(sqrt_factors, pltpu.HBM)
    head = send_edges(*cut_edges(0, near, factors, (water_depth, sea_mask)))
    cut = cut_edges(near, count - near, factors, ()) if count > near else ()
    *head, = lax.optimization_barrier((*head, *cut))
    head, cut = head[:2], head[2:]
    static = (*head, water_depth, sea_mask)
    chunks = [swap(forecast_groups(0, 1, 0, 0, 1, (), sqrt_factors, *head, *static))]
    rest = ()
    if near > 1:
        rest = (forecast_groups(1, 1, 1, 0, count - 1, rest, sqrt_factors, *head, *static),)
    if count > near:
        tail = send_edges(*cut)
        rest = (forecast_groups(
            near, count - near, 0, near - 1, count - 1, rest, sqrt_factors, *tail, *static
        ),)
    chunks += [swap(value) for value in rest]

    fault = model_error.transpose(1, 2, 0, 3)
    turn = givens_transform.T
    devices = lax.axis_size("space") * parts
    half = lax.rem(lax.axis_index("mode"), 2).reshape(1, 1)
    columns = turn.shape[1]
    cell_count = float(fields * rows * lax.axis_size("space") * width)

    arrived = swap(rotate_fields(0, 2, chunks, fault, turn, parts))
    keep, send = local_gram(chunks, fault, turn, parts, devices, half)
    turn, keep, send = lax.optimization_barrier((turn, keep, send))
    blocks = sum_over_slabs(keep, send)
    me = lax.axis_index("mode").reshape(1, 1)
    last = exchange(rotate_blocks(fields - 1, chunks, fault, turn, parts, me))
    total = sum_over_modes(blocks)
    gram = total[:columns // devices, :columns] / cell_count
    inflation = jnp.sqrt(total[0, columns] / total[0, columns + 1])

    reduced = finish_fields(0, arrived, inflation, ())
    reduced = finish_blocks(fields - 1, last, me, inflation, reduced)
    return (reduced, gram, inflation)


def solution(mesh):
    in_specs = (
        P("mode", None, "space", None),
        P(None, None, ("space", "mode"), None),
        P("space", None),
        P("space", None),
        P(),
    )
    out_specs = (P("mode", None, "space", None), P(("space", "mode"), None), P())
    return jax.shard_map(shards, mesh=mesh, in_specs=in_specs, out_specs=out_specs, check_vma=False)
```

```python
import functools

import jax
import jax.numpy as jnp
import numpy as np
from jax import lax
from jax.experimental import pallas as pl
from jax.experimental.pallas import tpu as pltpu
from jax.sharding import PartitionSpec as P

flux_coef = 0.2
slope_coef = 0.2
turn_coef = 0.1
keep_coef = 0.95

GROUP = 16
HALO = 4
LANES = 128
VMEM_BYTES = 48 * 1024 * 1024


def column_diff(tiles):
    lane = lax.broadcasted_iota(jnp.int32, tiles[0].shape, 1)
    from_left = [pltpu.roll(tile, 1, 1) for tile in tiles]
    from_right = [pltpu.roll(tile, LANES - 1, 1) for tile in tiles]
    zero = jnp.zeros_like(tiles[0])
    out = []
    for t in range(len(tiles)):
        left = from_left[t - 1] if t > 0 else zero
        right = from_right[t + 1] if t + 1 < len(tiles) else zero
        previous = jnp.where(lane == 0, left, from_left[t])
        following = jnp.where(lane == LANES - 1, right, from_right[t])
        out.append(following - previous)
    return out


def swap_matrix(inner, outer):
    place = np.arange(inner * outer).reshape(outer, inner).T.reshape(-1)
    matrix = np.zeros((inner * outer, inner * outer), np.float32)
    matrix[np.arange(inner * outer), place] = 1.0
    return jnp.asarray(matrix, jnp.bfloat16)


def in_hbm(shape, dtype):
    return pltpu.HBM(shape, dtype)


def cut_edges_kernel(fixed, *refs):
    first_ref, last_ref = refs[:2]
    out_first, out_last = refs[-2:]
    group, fields = first_ref.shape[:2]
    for ref, out, low in ((first_ref, out_first, 0), (last_ref, out_last, GROUP - HALO)):
        for m in range(group):
            for field in range(fields):
                edge = ref[m, field].astype(jnp.float32)[low:low + HALO]
                out[m * fields + field] = edge.astype(jnp.bfloat16)
    if fixed:
        depth_ref, mask_ref = refs[2:4]
        for out, low in ((out_first, 0), (out_last, depth_ref.shape[0] - HALO)):
            rest = depth_ref[low:low + HALO]
            for piece in range(3):
                part = rest.astype(jnp.bfloat16)
                out[group * fields + piece] = part
                rest = rest - part.astype(jnp.float32)
            out[group * fields + 3] = mask_ref[low:low + HALO].astype(jnp.float32).astype(jnp.bfloat16)


def cut_edges(first, groups, factors, fixed):
    _, fields, rows, width = factors.shape
    size = GROUP * groups if fixed else GROUP
    steps = 1 if fixed else groups
    count = size * steps * fields + (4 if fixed else 0)
    block = size * fields + (4 if fixed else 0)
    place = jax.ShapeDtypeStruct if fixed else in_hbm
    out = place((count, HALO, width), jnp.bfloat16)
    return pl.pallas_call(
        functools.partial(cut_edges_kernel, bool(fixed)),
        grid=(steps,),
        out_shape=(out, out),
        in_specs=[
            pl.BlockSpec((size, fields, GROUP, width), lambda i: (first // (size // GROUP) + i, 0, 0, 0)),
            pl.BlockSpec((size, fields, GROUP, width),
                         lambda i: (first // (size // GROUP) + i, 0, rows // GROUP - 1, 0)),
        ] + [pl.BlockSpec(value.shape, lambda i: (0, 0)) for value in fixed],
        out_specs=[pl.BlockSpec((block, HALO, width), lambda i: (i, 0, 0))] * 2,
        compiler_params=pltpu.CompilerParams(vmem_limit_bytes=VMEM_BYTES),
        cost_estimate=pl.CostEstimate(
            flops=0, bytes_accessed=5 * count * HALO * width * 2, transcendentals=0
        ),
        name="cut_edges",
    )(factors, factors, *fixed)


def block_of(count):
    return max(size for size in range(1, 55) if count % size == 0)


def forecast_kernel(x_ref, low_ref, high_ref, low_static, high_static, depth_ref, mask_ref,
                    swap_ref, swap_ends_ref, *refs):
    out_ref, cells, ends, depth, wet, surf1, east1, north1, surf2 = refs[-9:]
    _, fields, rows, width = x_ref.shape
    tiles = width // LANES
    spots = [slice(t * LANES, (t + 1) * LANES) for t in range(tiles)]

    ends[:, :HALO] = low_ref[...].astype(jnp.float32)
    ends[:, HALO:] = high_ref[...].astype(jnp.float32)
    for field in range(fields):
        for top in range(0, rows, GROUP):
            block = x_ref[:, field, top:top + GROUP, :].reshape(GROUP * GROUP, width)
            block = jnp.dot(swap_ref[...], block, preferred_element_type=jnp.float32)
            block = block * slope_coef if field == 0 else block
            cells[field, HALO + top:HALO + top + GROUP] = block.reshape(GROUP, GROUP, width)
        block = jnp.concatenate([ends[m * fields + field] for m in range(GROUP)], axis=0)
        block = jnp.dot(
            swap_ends_ref[...], block.astype(jnp.bfloat16), preferred_element_type=jnp.float32
        ).reshape(2 * HALO, GROUP, width)
        block = block * slope_coef if field == 0 else block
        cells[field, :HALO] = block[:HALO]
        cells[field, HALO + rows:] = block[HALO:]

    def place_static(place, depth_row, wet_row):
        depth[place] = jnp.broadcast_to(flux_coef * slope_coef * depth_row, (8, width))
        wet[place] = jnp.broadcast_to(wet_row, (8, width))

    for static, first in ((low_static, 0), (high_static, HALO + rows)):
        value = static[...].astype(jnp.float32)
        level = value[0] + value[1] + value[2]
        for j in range(HALO):
            place_static(first + j, level[j:j + 1], value[3, j:j + 1])
    for top in range(0, rows, 8):
        level = depth_ref[top:top + 8]
        sea = mask_ref[top:top + 8].astype(jnp.float32)
        for j in range(8):
            place_static(HALO + top + j, level[j:j + 1], sea[j:j + 1])

    def get(ref, i):
        return [ref[i, :, spot] for spot in spots]

    def get_field(field, i):
        return [cells[field, i + HALO, :, spot] for spot in spots]

    def get_static(ref, i):
        parts = [ref[i + HALO, :, spot] for spot in spots]
        return [jnp.concatenate([part] * (GROUP // 8), axis=0) for part in parts]

    def put(ref, i, values):
        for spot, value in zip(spots, values):
            ref[i, :, spot] = value

    def times(one, other):
        return [a * b for a, b in zip(one, other)]

    def over_rows(first, last, body):
        size = block_of(last - first)

        def block(k, carry):
            body(first + k * size, size)
            return carry

        lax.fori_loop(0, (last - first) // size, block, 0)

    def surfaces(i, size, surface_at, east_at, north_at, put_at):
        flux = {j: times(get_static(depth, i + j), north_at(i + j)) for j in (-1, 0)}
        for j in range(size):
            flux[j + 1] = times(get_static(depth, i + j + 1), north_at(i + j + 1))
            sides = column_diff(times(get_static(depth, i + j), east_at(i + j)))
            sea, surface = get_static(wet, i + j), surface_at(i + j)
            put_at(i + j, [
                sea[t] * (surface[t] - (sides[t] + (flux[j + 1][t] - flux[j - 1][t])))
                for t in range(tiles)
            ])

    def flows(i, size, surface_at, east_at, north_at, put_at):
        surface = {j: surface_at(i + j) for j in (-1, 0)}
        for j in range(size):
            surface[j + 1] = surface_at(i + j + 1)
            sides = column_diff(surface[j])
            sea, east, north = get_static(wet, i + j), east_at(i + j), north_at(i + j)
            put_at(i + j, surface[j], [
                sea[t] * (keep_coef * east[t] + turn_coef * north[t] - sides[t])
                for t in range(tiles)
            ], [
                sea[t] * (keep_coef * north[t] - turn_coef * east[t]
                          - (surface[j + 1][t] - surface[j - 1][t]))
                for t in range(tiles)
            ])

    def first_surface(i, size):
        surfaces(
            i, size, lambda r: get_field(0, r), lambda r: get_field(1, r),
            lambda r: get_field(2, r), lambda r, value: put(surf1, r + 3, value),
        )

    def first_flow(i, size):
        def put_flow(r, surface, east, north):
            put(east1, r + 2, east)
            put(north1, r + 2, north)

        flows(
            i, size, lambda r: get(surf1, r + 3), lambda r: get_field(1, r),
            lambda r: get_field(2, r), put_flow,
        )

    def second_surface(i, size):
        surfaces(
            i, size, lambda r: get(surf1, r + 3), lambda r: get(east1, r + 2),
            lambda r: get(north1, r + 2), lambda r, value: put(surf2, r + 1, value),
        )

    def second_flow(i, size):
        def put_out(r, surface, east, north):
            surface = [value * (1.0 / slope_coef) for value in surface]
            for field, values in enumerate((surface, east, north)):
                for spot, value in zip(spots, values):
                    out_ref[r, field, :, spot] = value.astype(jnp.bfloat16)

        flows(
            i, size, lambda r: get(surf2, r + 1), lambda r: get(east1, r + 2),
            lambda r: get(north1, r + 2), put_out,
        )

    over_rows(-3, rows + 3, first_surface)
    over_rows(-2, rows + 2, first_flow)
    over_rows(-1, rows + 1, second_surface)
    over_rows(0, rows, second_flow)


def forecast_groups(first, count, skip, place, whole_count, previous, factors, low, high,
                    static_low, static_high, depth, mask):
    modes, fields, rows, width = factors.shape
    padded = rows + 2 * HALO
    edge = GROUP * fields
    last = static_low.shape[0] // 4 - 1
    swap, swap_ends = swap_matrix(GROUP, GROUP), swap_matrix(2 * HALO, GROUP)

    def rows_of(count):
        return pltpu.VMEM((count, GROUP, width), jnp.float32)

    def whole(value):
        return pl.BlockSpec(value.shape, lambda i: (0,) * value.ndim)

    return pl.pallas_call(
        forecast_kernel,
        grid=(count,),
        out_shape=in_hbm((rows, fields, whole_count * GROUP, width), jnp.bfloat16),
        in_specs=[
            pl.BlockSpec((GROUP, fields, rows, width), lambda i: (first + i, 0, 0, 0)),
            pl.BlockSpec((edge, HALO, width), lambda i: (skip + i, 0, 0)),
            pl.BlockSpec((edge, HALO, width), lambda i: (skip + i, 0, 0)),
            pl.BlockSpec((4, HALO, width), lambda i: (last, 0, 0)),
            pl.BlockSpec((4, HALO, width), lambda i: (last, 0, 0)),
            whole(depth),
            whole(mask),
            whole(swap),
            whole(swap_ends),
        ] + [pl.BlockSpec(memory_space=pltpu.HBM) for _ in previous],
        out_specs=pl.BlockSpec((rows, fields, GROUP, width), lambda i: (0, 0, place + i, 0)),
        input_output_aliases={9: 0} if previous else {},
        scratch_shapes=[
            pltpu.VMEM((fields, padded, GROUP, width), jnp.float32),
            pltpu.VMEM((edge, 2 * HALO, width), jnp.float32),
            pltpu.VMEM((padded, 8, width), jnp.float32),
            pltpu.VMEM((padded, 8, width), jnp.float32),
            rows_of(rows + 6),
            rows_of(rows + 4),
            rows_of(rows + 4),
            rows_of(rows + 2),
        ],
        compiler_params=pltpu.CompilerParams(vmem_limit_bytes=VMEM_BYTES),
        cost_estimate=pl.CostEstimate(
            flops=60 * count * GROUP * rows * width,
            bytes_accessed=2 * 2 * count * GROUP * fields * rows * width,
            transcendentals=0,
        ),
        name="forecast",
    )(factors, low, high, static_low, static_high, depth, mask, swap, swap_ends, *previous)


def all_columns(chunk_refs, fault_ref, j):
    own = [ref[:, j, 0] for ref in chunk_refs]
    joined = jnp.concatenate(own, axis=1)
    return joined.reshape(-1, joined.shape[-1]), fault_ref[0, j]


def rotate_kernel(count, *refs):
    chunk_refs = refs[:count]
    fault_ref, turn_ref, out_ref = refs[count:]
    parts, _, size, modes, width = out_ref.shape
    for j in range(size):
        columns = jnp.concatenate(all_columns(chunk_refs, fault_ref, j), axis=0)
        value = jnp.dot(turn_ref[...], columns, preferred_element_type=jnp.float32)
        out_ref[:, 0, j] = value.astype(jnp.bfloat16).reshape(parts, modes, width)


def by_part(chunks, parts):
    return [c.reshape((parts, c.shape[0] // parts) + c.shape[1:]) for c in chunks]


def rotate_fields(first, fields, chunks, fault, turn, parts):
    width = chunks[0].shape[-1]
    each = chunks[0].shape[0] // parts
    kept = turn.shape[0]
    noise = fault.shape[2]
    modes = kept // parts
    size = 3 if each % 3 == 0 else 1
    views = by_part(chunks, parts)
    return pl.pallas_call(
        functools.partial(rotate_kernel, len(views)),
        grid=(fields, each // size),
        out_shape=in_hbm((parts, fields, each, modes, width), jnp.bfloat16),
        in_specs=[
            pl.BlockSpec((parts, size, 1, v.shape[3], width), lambda f, j: (0, j, first + f, 0, 0))
            for v in views
        ] + [
            pl.BlockSpec((1, size, noise, width), lambda f, j: (first + f, j, 0, 0)),
            pl.BlockSpec(turn.shape, lambda f, j: (0, 0)),
        ],
        out_specs=pl.BlockSpec((parts, 1, size, modes, width), lambda f, j: (0, f, j, 0, 0)),
        compiler_params=pltpu.CompilerParams(vmem_limit_bytes=VMEM_BYTES),
        cost_estimate=pl.CostEstimate(
            flops=2 * fields * each * width * kept * turn.shape[1],
            bytes_accessed=2 * fields * each * width * (kept + turn.shape[1]),
            transcendentals=0,
        ),
        name="rotate",
    )(*views, fault, turn)


def gram_kernel(count, each, devices, *refs):
    chunk_refs = refs[:count]
    fault_ref, turn_ref, half_ref, keep_ref, send_ref, gram_ref = refs[count:]
    pairs = [all_columns(chunk_refs, fault_ref, j) for j in range(each)]
    columns = jnp.concatenate(
        [jnp.concatenate([prior, fault], axis=0) for prior, fault in pairs], axis=1
    )
    value = lax.dot_general(
        columns, columns, (((1,), (1,)), ((), ())), preferred_element_type=jnp.float32
    )
    step = pl.program_id(0)

    @pl.when(step == 0)
    def _():
        gram_ref[...] = value

    @pl.when(step > 0)
    def _():
        gram_ref[...] += value

    @pl.when(step == pl.num_programs(0) - 1)
    def _():
        gram = gram_ref[...]
        size = gram.shape[0]
        row = lax.broadcasted_iota(jnp.int32, gram.shape, 0)
        column = lax.broadcasted_iota(jnp.int32, gram.shape, 1)
        full = jnp.sum(jnp.where(row == column, gram, 0.0))
        turn = turn_ref[...]
        turned = 0.0
        for _ in range(3):
            piece = gram.astype(jnp.bfloat16)
            turned = turned + jnp.dot(turn, piece, preferred_element_type=jnp.float32)
            gram = gram - piece.astype(jnp.float32)
        kept = jnp.sum(turned * turn.astype(jnp.float32))
        own = size // devices
        slot = keep_ref.shape[0] // (devices // 2)
        lane = lax.broadcasted_iota(jnp.int32, (keep_ref.shape[0], LANES), 1)
        traces = jnp.where(lane == 0, full, jnp.where(lane == 1, kept, 0.0))
        low = half_ref[0, 0] == 0
        for out in (keep_ref, send_ref):
            if slot != own:
                out[...] = jnp.zeros_like(out)
            out[:, size:] = traces
        for q in range(devices // 2):
            even = gram_ref[2 * q * own:(2 * q + 1) * own]
            uneven = gram_ref[(2 * q + 1) * own:(2 * q + 2) * own]
            keep_ref[q * slot:q * slot + own, :size] = jnp.where(low, even, uneven)
            send_ref[q * slot:q * slot + own, :size] = jnp.where(low, uneven, even)


def local_gram(chunks, fault, turn, parts, devices, half):
    width = chunks[0].shape[-1]
    each = chunks[0].shape[0] // parts
    noise = fault.shape[2]
    columns = turn.shape[1]
    views = by_part(chunks, parts)
    slot = -(-columns // devices // 8) * 8
    slots = (devices // 2 * slot, columns + LANES)
    out = in_hbm(slots, jnp.float32)
    return pl.pallas_call(
        functools.partial(gram_kernel, len(views), each, devices),
        grid=(3,),
        out_shape=(out, out),
        in_specs=[
            pl.BlockSpec((parts, each, 1, v.shape[3], width), lambda f: (0, 0, f, 0, 0))
            for v in views
        ] + [
            pl.BlockSpec((1, each, noise, width), lambda f: (f, 0, 0, 0)),
            pl.BlockSpec(turn.shape, lambda f: (0, 0)),
            pl.BlockSpec(memory_space=pltpu.SMEM),
        ],
        out_specs=[pl.BlockSpec(slots, lambda f: (0, 0))] * 2,
        scratch_shapes=[pltpu.VMEM((columns, columns), jnp.float32)],
        compiler_params=pltpu.CompilerParams(vmem_limit_bytes=VMEM_BYTES),
        cost_estimate=pl.CostEstimate(
            flops=2 * 3 * each * width * columns * columns,
            bytes_accessed=2 * 3 * each * width * columns,
            transcendentals=0,
        ),
        name="gram",
    )(*views, fault, turn, half)


def add_kernel(count, parts, me_ref, *refs):
    total = refs[0][...]
    for ref in refs[1:count]:
        total = total + ref[...]
    total_ref = refs[-1]
    total_ref[...] = total
    rows = total.shape[0] // parts
    for k in range(parts):
        first = pl.multiple_of(jnp.bitwise_xor(me_ref[0, 0], k) * rows, 8)
        refs[count + k][...] = total_ref[pl.ds(first, rows)]


def add_and_cut(terms, me, parts):
    rows, width = terms[0].shape
    whole = pl.BlockSpec((rows, width), lambda: (0, 0))
    block = pl.BlockSpec((rows // parts, width), lambda: (0, 0))
    return pl.pallas_call(
        functools.partial(add_kernel, len(terms), parts),
        out_shape=[in_hbm((rows // parts, width), jnp.float32) for _ in range(parts)],
        in_specs=[pl.BlockSpec(memory_space=pltpu.SMEM)] + [whole for _ in terms],
        out_specs=[block for _ in range(parts)],
        scratch_shapes=[pltpu.VMEM((rows, width), jnp.float32)],
        compiler_params=pltpu.CompilerParams(vmem_limit_bytes=VMEM_BYTES),
        cost_estimate=pl.CostEstimate(
            flops=len(terms) * rows * width,
            bytes_accessed=4 * (len(terms) + 1) * rows * width,
            transcendentals=0,
        ),
        name="add",
    )(me.reshape(1, 1), *terms)


def partners(axis, distance):
    return [(i, i ^ distance) for i in range(lax.axis_size(axis))]


def sum_over_slabs(keep, send):
    other = lax.ppermute(send, "mode", partners("mode", 1))
    count = lax.axis_size("space")
    blocks = add_and_cut([keep, other], lax.axis_index("space"), count)
    terms = [blocks[0]] + [
        lax.ppermute(blocks[k], "space", partners("space", k)) for k in range(1, count)
    ]
    return add_and_cut(terms, lax.axis_index("mode") // 2, lax.axis_size("mode") // 2)


def sum_over_modes(blocks):
    return blocks[0] + sum(
        lax.ppermute(block, "mode", partners("mode", 2 * k))
        for k, block in enumerate(blocks) if k > 0
    )


def finish_kernel(aliased, scale_ref, swap_ref, x_ref, *refs):
    out_ref = refs[aliased]
    parts, _, each, _, width = x_ref.shape
    rows = parts * each
    scale = scale_ref[0, 0]
    value = x_ref[...].reshape(rows * GROUP, width)
    for top in range(0, rows, GROUP):
        block = value[top * GROUP:(top + GROUP) * GROUP]
        block = scale * jnp.dot(swap_ref[...], block, preferred_element_type=jnp.float32)
        out_ref[:, 0, top:top + GROUP, :] = block.astype(jnp.bfloat16).reshape(GROUP, GROUP, width)


def finish_fields(first, arrived, scale, previous):
    parts, fields, each, modes, width = arrived.shape
    rows = parts * each
    swap = swap_matrix(GROUP, GROUP)
    operands = [scale.reshape(1, 1), swap, arrived, *previous]
    return pl.pallas_call(
        functools.partial(finish_kernel, len(previous)),
        grid=(fields, modes // GROUP),
        out_shape=jax.ShapeDtypeStruct((modes, 3, rows, width), jnp.bfloat16),
        in_specs=[
            pl.BlockSpec(memory_space=pltpu.SMEM),
            pl.BlockSpec(swap.shape, lambda f, m: (0, 0)),
            pl.BlockSpec((parts, 1, each, GROUP, width), lambda f, m: (0, f, 0, m, 0)),
        ] + [pl.BlockSpec(memory_space=pltpu.HBM) for _ in previous],
        out_specs=pl.BlockSpec((GROUP, 1, rows, width), lambda f, m: (m, first + f, 0, 0)),
        input_output_aliases={3: 0} if previous else {},
        compiler_params=pltpu.CompilerParams(vmem_limit_bytes=VMEM_BYTES),
        cost_estimate=pl.CostEstimate(
            flops=fields * modes * rows * width,
            bytes_accessed=4 * fields * modes * rows * width,
            transcendentals=0,
        ),
        name="finish",
    )(*operands)


def send_edges(first, last):
    count = lax.axis_size("space")
    forward = [(i, i + 1) for i in range(count - 1)]
    backward = [(target, source) for source, target in forward]
    return lax.ppermute(last, "space", forward), lax.ppermute(first, "space", backward)


def shards(sqrt_factors, model_error, water_depth, sea_mask, givens_transform):
    modes, fields, rows, width = sqrt_factors.shape
    parts = lax.axis_size("mode")
    count = modes // GROUP
    swap = functools.partial(
        lax.all_to_all, axis_name="mode", split_axis=0, concat_axis=0, tiled=True
    )

    near = min(count, 2)
    water_depth, sea_mask = (
        pltpu.with_memory_space_constraint(value, pltpu.HBM) for value in (water_depth, sea_mask)
    )
    factors = pltpu.with_memory_space_constraint(sqrt_factors, pltpu.HBM)
    head = send_edges(*cut_edges(0, near, factors, (water_depth, sea_mask)))
    cut = cut_edges(near, count - near, factors, ()) if count > near else ()
    *head, = lax.optimization_barrier((*head, *cut))
    head, cut = head[:2], head[2:]
    static = (*head, water_depth, sea_mask)
    near_block = pltpu.with_memory_space_constraint(sqrt_factors[:GROUP], pltpu.VMEM)
    chunks = [swap(forecast_groups(0, 1, 0, 0, 1, (), near_block, *head, *static))]
    rest = ()
    if near > 1:
        rest = (forecast_groups(1, 1, 1, 0, count - 1, rest, sqrt_factors, *head, *static),)
    if count > near:
        tail = send_edges(*cut)
        rest = (forecast_groups(
            near, count - near, 0, near - 1, count - 1, rest, sqrt_factors, *tail, *static
        ),)
    chunks += [swap(value) for value in rest]

    fault = model_error.transpose(1, 2, 0, 3)
    turn = givens_transform.T
    devices = lax.axis_size("space") * parts
    half = lax.rem(lax.axis_index("mode"), 2).reshape(1, 1)
    columns = turn.shape[1]
    cell_count = float(fields * rows * lax.axis_size("space") * width)

    arrived = swap(rotate_fields(0, 2, chunks, fault, turn, parts))
    blocks = sum_over_slabs(*local_gram(chunks, fault, turn, parts, devices, half))
    last = rotate_fields(2, fields - 2, chunks, fault, turn, parts)
    last, total = lax.optimization_barrier((last, sum_over_modes(blocks)))
    last = swap(last)
    gram = total[:columns // devices, :columns] / cell_count
    inflation = jnp.sqrt(total[0, columns] / total[0, columns + 1])

    reduced = finish_fields(0, arrived, inflation, ())
    reduced = finish_fields(2, last, inflation, (reduced,))
    return (reduced, gram, inflation)


def solution(mesh):
    in_specs = (
        P("mode", None, "space", None),
        P(None, None, ("space", "mode"), None),
        P("space", None),
        P("space", None),
        P(),
    )
    out_specs = (P("mode", None, "space", None), P(("space", "mode"), None), P())
    return jax.shard_map(shards, mesh=mesh, in_specs=in_specs, out_specs=out_specs, check_vma=False)
```

```python
import functools

import jax
import jax.numpy as jnp
import numpy as np
from jax import lax
from jax.experimental import pallas as pl
from jax.experimental.pallas import tpu as pltpu
from jax.sharding import PartitionSpec as P

flux_coef = 0.2
slope_coef = 0.2
turn_coef = 0.1
keep_coef = 0.95

GROUP = 16
HALO = 4
LANES = 128
VMEM_BYTES = 48 * 1024 * 1024


def column_diff(tiles):
    lane = lax.broadcasted_iota(jnp.int32, tiles[0].shape, 1)
    from_left = [pltpu.roll(tile, 1, 1) for tile in tiles]
    from_right = [pltpu.roll(tile, LANES - 1, 1) for tile in tiles]
    zero = jnp.zeros_like(tiles[0])
    out = []
    for t in range(len(tiles)):
        left = from_left[t - 1] if t > 0 else zero
        right = from_right[t + 1] if t + 1 < len(tiles) else zero
        previous = jnp.where(lane == 0, left, from_left[t])
        following = jnp.where(lane == LANES - 1, right, from_right[t])
        out.append(following - previous)
    return out


def swap_matrix(inner, outer):
    place = np.arange(inner * outer).reshape(outer, inner).T.reshape(-1)
    matrix = np.zeros((inner * outer, inner * outer), np.float32)
    matrix[np.arange(inner * outer), place] = 1.0
    return jnp.asarray(matrix, jnp.bfloat16)


def in_hbm(shape, dtype):
    return pltpu.HBM(shape, dtype)


def cut_edges_kernel(fixed, *refs):
    first_ref, last_ref = refs[:2]
    out_first, out_last = refs[-2:]
    group, fields = first_ref.shape[:2]
    for ref, out, low in ((first_ref, out_first, 0), (last_ref, out_last, GROUP - HALO)):
        for m in range(group):
            for field in range(fields):
                edge = ref[m, field].astype(jnp.float32)[low:low + HALO]
                out[m * fields + field] = edge.astype(jnp.bfloat16)
    if fixed:
        depth_ref, mask_ref = refs[2:4]
        for out, low in ((out_first, 0), (out_last, depth_ref.shape[0] - HALO)):
            rest = depth_ref[low:low + HALO]
            for piece in range(3):
                part = rest.astype(jnp.bfloat16)
                out[group * fields + piece] = part
                rest = rest - part.astype(jnp.float32)
            out[group * fields + 3] = mask_ref[low:low + HALO].astype(jnp.float32).astype(jnp.bfloat16)


def cut_edges(first, groups, factors, fixed):
    _, fields, rows, width = factors.shape
    size = GROUP * groups if fixed else GROUP
    steps = 1 if fixed else groups
    count = size * steps * fields + (4 if fixed else 0)
    block = size * fields + (4 if fixed else 0)
    place = jax.ShapeDtypeStruct if fixed else in_hbm
    out = place((count, HALO, width), jnp.bfloat16)
    return pl.pallas_call(
        functools.partial(cut_edges_kernel, bool(fixed)),
        grid=(steps,),
        out_shape=(out, out),
        in_specs=[
            pl.BlockSpec((size, fields, GROUP, width), lambda i: (first // (size // GROUP) + i, 0, 0, 0)),
            pl.BlockSpec((size, fields, GROUP, width),
                         lambda i: (first // (size // GROUP) + i, 0, rows // GROUP - 1, 0)),
        ] + [pl.BlockSpec(value.shape, lambda i: (0, 0)) for value in fixed],
        out_specs=[pl.BlockSpec((block, HALO, width), lambda i: (i, 0, 0))] * 2,
        compiler_params=pltpu.CompilerParams(vmem_limit_bytes=VMEM_BYTES),
        cost_estimate=pl.CostEstimate(
            flops=0, bytes_accessed=5 * count * HALO * width * 2, transcendentals=0
        ),
        name="cut_edges",
    )(factors, factors, *fixed)


def block_of(count):
    return max(size for size in range(1, 55) if count % size == 0)


def forecast_kernel(x_ref, low_ref, high_ref, low_static, high_static, depth_ref, mask_ref,
                    swap_ends_ref, *refs):
    out_ref, cells, ends, depth, wet, surf1, east1, north1, surf2 = refs[-9:]
    rows, fields, _, width = x_ref.shape
    tiles = width // LANES
    spots = [slice(t * LANES, (t + 1) * LANES) for t in range(tiles)]

    ends[:, :HALO] = low_ref[...].astype(jnp.float32)
    ends[:, HALO:] = high_ref[...].astype(jnp.float32)
    for field in range(fields):
        block = x_ref[:, field].astype(jnp.float32)
        block = block * slope_coef if field == 0 else block
        cells[field, HALO:HALO + rows] = block
        block = jnp.concatenate([ends[m * fields + field] for m in range(GROUP)], axis=0)
        block = jnp.dot(
            swap_ends_ref[...], block.astype(jnp.bfloat16), preferred_element_type=jnp.float32
        ).reshape(2 * HALO, GROUP, width)
        block = block * slope_coef if field == 0 else block
        cells[field, :HALO] = block[:HALO]
        cells[field, HALO + rows:] = block[HALO:]

    def place_static(place, depth_row, wet_row):
        depth[place] = jnp.broadcast_to(flux_coef * slope_coef * depth_row, (8, width))
        wet[place] = jnp.broadcast_to(wet_row, (8, width))

    for static, first in ((low_static, 0), (high_static, HALO + rows)):
        value = static[...].astype(jnp.float32)
        level = value[0] + value[1] + value[2]
        for j in range(HALO):
            place_static(first + j, level[j:j + 1], value[3, j:j + 1])
    for top in range(0, rows, 8):
        level = depth_ref[top:top + 8]
        sea = mask_ref[top:top + 8].astype(jnp.float32)
        for j in range(8):
            place_static(HALO + top + j, level[j:j + 1], sea[j:j + 1])

    def get(ref, i):
        return [ref[i, :, spot] for spot in spots]

    def get_field(field, i):
        return [cells[field, i + HALO, :, spot] for spot in spots]

    def get_static(ref, i):
        parts = [ref[i + HALO, :, spot] for spot in spots]
        return [jnp.concatenate([part] * (GROUP // 8), axis=0) for part in parts]

    def put(ref, i, values):
        for spot, value in zip(spots, values):
            ref[i, :, spot] = value

    def times(one, other):
        return [a * b for a, b in zip(one, other)]

    def over_rows(first, last, body):
        size = block_of(last - first)

        def block(k, carry):
            body(first + k * size, size)
            return carry

        lax.fori_loop(0, (last - first) // size, block, 0)

    def surfaces(i, size, surface_at, east_at, north_at, put_at):
        flux = {j: times(get_static(depth, i + j), north_at(i + j)) for j in (-1, 0)}
        for j in range(size):
            flux[j + 1] = times(get_static(depth, i + j + 1), north_at(i + j + 1))
            sides = column_diff(times(get_static(depth, i + j), east_at(i + j)))
            sea, surface = get_static(wet, i + j), surface_at(i + j)
            put_at(i + j, [
                sea[t] * (surface[t] - (sides[t] + (flux[j + 1][t] - flux[j - 1][t])))
                for t in range(tiles)
            ])

    def flows(i, size, surface_at, east_at, north_at, put_at):
        surface = {j: surface_at(i + j) for j in (-1, 0)}
        for j in range(size):
            surface[j + 1] = surface_at(i + j + 1)
            sides = column_diff(surface[j])
            sea, east, north = get_static(wet, i + j), east_at(i + j), north_at(i + j)
            put_at(i + j, surface[j], [
                sea[t] * (keep_coef * east[t] + turn_coef * north[t] - sides[t])
                for t in range(tiles)
            ], [
                sea[t] * (keep_coef * north[t] - turn_coef * east[t]
                          - (surface[j + 1][t] - surface[j - 1][t]))
                for t in range(tiles)
            ])

    def first_surface(i, size):
        surfaces(
            i, size, lambda r: get_field(0, r), lambda r: get_field(1, r),
            lambda r: get_field(2, r), lambda r, value: put(surf1, r + 3, value),
        )

    def first_flow(i, size):
        def put_flow(r, surface, east, north):
            put(east1, r + 2, east)
            put(north1, r + 2, north)

        flows(
            i, size, lambda r: get(surf1, r + 3), lambda r: get_field(1, r),
            lambda r: get_field(2, r), put_flow,
        )

    def second_surface(i, size):
        surfaces(
            i, size, lambda r: get(surf1, r + 3), lambda r: get(east1, r + 2),
            lambda r: get(north1, r + 2), lambda r, value: put(surf2, r + 1, value),
        )

    def second_flow(i, size):
        def put_out(r, surface, east, north):
            surface = [value * (1.0 / slope_coef) for value in surface]
            for field, values in enumerate((surface, east, north)):
                for spot, value in zip(spots, values):
                    out_ref[r, field, :, spot] = value.astype(jnp.bfloat16)

        flows(
            i, size, lambda r: get(surf2, r + 1), lambda r: get(east1, r + 2),
            lambda r: get(north1, r + 2), put_out,
        )

    over_rows(-3, rows + 3, first_surface)
    over_rows(-2, rows + 2, first_flow)
    over_rows(-1, rows + 1, second_surface)
    over_rows(0, rows, second_flow)


def spread_kernel(x_ref, swap_ref, out_ref):
    _, fields, rows, width = x_ref.shape
    for field in range(fields):
        for top in range(0, rows, GROUP):
            block = x_ref[:, field, top:top + GROUP, :].reshape(GROUP * GROUP, width)
            block = jnp.dot(swap_ref[...], block, preferred_element_type=jnp.float32)
            block = block.astype(jnp.bfloat16).reshape(GROUP, GROUP, width)
            out_ref[top:top + GROUP, field] = block


def spread_groups(first, count, factors):
    _, fields, rows, width = factors.shape
    swap = swap_matrix(GROUP, GROUP)
    return pl.pallas_call(
        spread_kernel,
        grid=(count,),
        out_shape=jax.ShapeDtypeStruct((rows, fields, count * GROUP, width), jnp.bfloat16),
        in_specs=[
            pl.BlockSpec((GROUP, fields, rows, width), lambda i: (first + i, 0, 0, 0)),
            pl.BlockSpec(swap.shape, lambda i: (0, 0)),
        ],
        out_specs=pl.BlockSpec((rows, fields, GROUP, width), lambda i: (0, 0, i, 0)),
        compiler_params=pltpu.CompilerParams(vmem_limit_bytes=VMEM_BYTES),
        cost_estimate=pl.CostEstimate(
            flops=2 * GROUP * count * GROUP * fields * rows * width,
            bytes_accessed=2 * 2 * count * GROUP * fields * rows * width,
            transcendentals=0,
        ),
        name="spread",
    )(factors, swap)


def forecast_groups(first, count, skip, place, whole_count, previous, spread, low, high,
                    static_low, static_high, depth, mask):
    rows, fields, _, width = spread.shape
    padded = rows + 2 * HALO
    edge = GROUP * fields
    last = static_low.shape[0] // 4 - 1
    swap_ends = swap_matrix(2 * HALO, GROUP)

    def rows_of(count):
        return pltpu.VMEM((count, GROUP, width), jnp.float32)

    def whole(value):
        return pl.BlockSpec(value.shape, lambda i: (0,) * value.ndim)

    return pl.pallas_call(
        forecast_kernel,
        grid=(count,),
        out_shape=in_hbm((rows, fields, whole_count * GROUP, width), jnp.bfloat16),
        in_specs=[
            pl.BlockSpec((rows, fields, GROUP, width), lambda i: (0, 0, first + i, 0)),
            pl.BlockSpec((edge, HALO, width), lambda i: (skip + i, 0, 0)),
            pl.BlockSpec((edge, HALO, width), lambda i: (skip + i, 0, 0)),
            pl.BlockSpec((4, HALO, width), lambda i: (last, 0, 0)),
            pl.BlockSpec((4, HALO, width), lambda i: (last, 0, 0)),
            whole(depth),
            whole(mask),
            whole(swap_ends),
        ] + [pl.BlockSpec(memory_space=pltpu.HBM) for _ in previous],
        out_specs=pl.BlockSpec((rows, fields, GROUP, width), lambda i: (0, 0, place + i, 0)),
        input_output_aliases={8: 0} if previous else {},
        scratch_shapes=[
            pltpu.VMEM((fields, padded, GROUP, width), jnp.float32),
            pltpu.VMEM((edge, 2 * HALO, width), jnp.float32),
            pltpu.VMEM((padded, 8, width), jnp.float32),
            pltpu.VMEM((padded, 8, width), jnp.float32),
            rows_of(rows + 6),
            rows_of(rows + 4),
            rows_of(rows + 4),
            rows_of(rows + 2),
        ],
        compiler_params=pltpu.CompilerParams(vmem_limit_bytes=VMEM_BYTES),
        cost_estimate=pl.CostEstimate(
            flops=60 * count * GROUP * rows * width,
            bytes_accessed=2 * 2 * count * GROUP * fields * rows * width,
            transcendentals=0,
        ),
        name="forecast",
    )(spread, low, high, static_low, static_high, depth, mask, swap_ends, *previous)


def all_columns(chunk_refs, fault_ref, j):
    own = [ref[:, j, 0] for ref in chunk_refs]
    joined = jnp.concatenate(own, axis=1)
    return joined.reshape(-1, joined.shape[-1]), fault_ref[0, j]


def rotate_kernel(count, *refs):
    chunk_refs = refs[:count]
    fault_ref, turn_ref, out_ref = refs[count:]
    parts, _, size, modes, width = out_ref.shape
    for j in range(size):
        columns = jnp.concatenate(all_columns(chunk_refs, fault_ref, j), axis=0)
        value = jnp.dot(turn_ref[...], columns, preferred_element_type=jnp.float32)
        out_ref[:, 0, j] = value.astype(jnp.bfloat16).reshape(parts, modes, width)


def by_part(chunks, parts):
    return [c.reshape((parts, c.shape[0] // parts) + c.shape[1:]) for c in chunks]


def rotate_fields(first, fields, chunks, fault, turn, parts):
    width = chunks[0].shape[-1]
    each = chunks[0].shape[0] // parts
    kept = turn.shape[0]
    noise = fault.shape[2]
    modes = kept // parts
    size = 3 if each % 3 == 0 else 1
    views = by_part(chunks, parts)
    return pl.pallas_call(
        functools.partial(rotate_kernel, len(views)),
        grid=(fields, each // size),
        out_shape=in_hbm((parts, fields, each, modes, width), jnp.bfloat16),
        in_specs=[
            pl.BlockSpec((parts, size, 1, v.shape[3], width), lambda f, j: (0, j, first + f, 0, 0))
            for v in views
        ] + [
            pl.BlockSpec((1, size, noise, width), lambda f, j: (first + f, j, 0, 0)),
            pl.BlockSpec(turn.shape, lambda f, j: (0, 0)),
        ],
        out_specs=pl.BlockSpec((parts, 1, size, modes, width), lambda f, j: (0, f, j, 0, 0)),
        compiler_params=pltpu.CompilerParams(vmem_limit_bytes=VMEM_BYTES),
        cost_estimate=pl.CostEstimate(
            flops=2 * fields * each * width * kept * turn.shape[1],
            bytes_accessed=2 * fields * each * width * (kept + turn.shape[1]),
            transcendentals=0,
        ),
        name="rotate",
    )(*views, fault, turn)


def gram_kernel(count, each, devices, *refs):
    chunk_refs = refs[:count]
    fault_ref, turn_ref, half_ref, keep_ref, send_ref, gram_ref = refs[count:]
    pairs = [all_columns(chunk_refs, fault_ref, j) for j in range(each)]
    columns = jnp.concatenate(
        [jnp.concatenate([prior, fault], axis=0) for prior, fault in pairs], axis=1
    )
    value = lax.dot_general(
        columns, columns, (((1,), (1,)), ((), ())), preferred_element_type=jnp.float32
    )
    step = pl.program_id(0)

    @pl.when(step == 0)
    def _():
        gram_ref[...] = value

    @pl.when(step > 0)
    def _():
        gram_ref[...] += value

    @pl.when(step == pl.num_programs(0) - 1)
    def _():
        gram = gram_ref[...]
        size = gram.shape[0]
        row = lax.broadcasted_iota(jnp.int32, gram.shape, 0)
        column = lax.broadcasted_iota(jnp.int32, gram.shape, 1)
        full = jnp.sum(jnp.where(row == column, gram, 0.0))
        turn = turn_ref[...]
        turned = 0.0
        for _ in range(3):
            piece = gram.astype(jnp.bfloat16)
            turned = turned + jnp.dot(turn, piece, preferred_element_type=jnp.float32)
            gram = gram - piece.astype(jnp.float32)
        kept = jnp.sum(turned * turn.astype(jnp.float32))
        own = size // devices
        slot = keep_ref.shape[0] // (devices // 2)
        lane = lax.broadcasted_iota(jnp.int32, (keep_ref.shape[0], LANES), 1)
        traces = jnp.where(lane == 0, full, jnp.where(lane == 1, kept, 0.0))
        low = half_ref[0, 0] == 0
        for out in (keep_ref, send_ref):
            if slot != own:
                out[...] = jnp.zeros_like(out)
            out[:, size:] = traces
        for q in range(devices // 2):
            even = gram_ref[2 * q * own:(2 * q + 1) * own]
            uneven = gram_ref[(2 * q + 1) * own:(2 * q + 2) * own]
            keep_ref[q * slot:q * slot + own, :size] = jnp.where(low, even, uneven)
            send_ref[q * slot:q * slot + own, :size] = jnp.where(low, uneven, even)


def local_gram(chunks, fault, turn, parts, devices, half):
    width = chunks[0].shape[-1]
    each = chunks[0].shape[0] // parts
    noise = fault.shape[2]
    columns = turn.shape[1]
    views = by_part(chunks, parts)
    slot = -(-columns // devices // 8) * 8
    slots = (devices // 2 * slot, columns + LANES)
    out = in_hbm(slots, jnp.float32)
    return pl.pallas_call(
        functools.partial(gram_kernel, len(views), each, devices),
        grid=(3,),
        out_shape=(out, out),
        in_specs=[
            pl.BlockSpec((parts, each, 1, v.shape[3], width), lambda f: (0, 0, f, 0, 0))
            for v in views
        ] + [
            pl.BlockSpec((1, each, noise, width), lambda f: (f, 0, 0, 0)),
            pl.BlockSpec(turn.shape, lambda f: (0, 0)),
            pl.BlockSpec(memory_space=pltpu.SMEM),
        ],
        out_specs=[pl.BlockSpec(slots, lambda f: (0, 0))] * 2,
        scratch_shapes=[pltpu.VMEM((columns, columns), jnp.float32)],
        compiler_params=pltpu.CompilerParams(vmem_limit_bytes=VMEM_BYTES),
        cost_estimate=pl.CostEstimate(
            flops=2 * 3 * each * width * columns * columns,
            bytes_accessed=2 * 3 * each * width * columns,
            transcendentals=0,
        ),
        name="gram",
    )(*views, fault, turn, half)


def add_kernel(count, parts, me_ref, *refs):
    total = refs[0][...]
    for ref in refs[1:count]:
        total = total + ref[...]
    total_ref = refs[-1]
    total_ref[...] = total
    rows = total.shape[0] // parts
    for k in range(parts):
        first = pl.multiple_of(jnp.bitwise_xor(me_ref[0, 0], k) * rows, 8)
        refs[count + k][...] = total_ref[pl.ds(first, rows)]


def add_and_cut(terms, me, parts):
    rows, width = terms[0].shape
    whole = pl.BlockSpec((rows, width), lambda: (0, 0))
    block = pl.BlockSpec((rows // parts, width), lambda: (0, 0))
    return pl.pallas_call(
        functools.partial(add_kernel, len(terms), parts),
        out_shape=[in_hbm((rows // parts, width), jnp.float32) for _ in range(parts)],
        in_specs=[pl.BlockSpec(memory_space=pltpu.SMEM)] + [whole for _ in terms],
        out_specs=[block for _ in range(parts)],
        scratch_shapes=[pltpu.VMEM((rows, width), jnp.float32)],
        compiler_params=pltpu.CompilerParams(vmem_limit_bytes=VMEM_BYTES),
        cost_estimate=pl.CostEstimate(
            flops=len(terms) * rows * width,
            bytes_accessed=4 * (len(terms) + 1) * rows * width,
            transcendentals=0,
        ),
        name="add",
    )(me.reshape(1, 1), *terms)


def partners(axis, distance):
    return [(i, i ^ distance) for i in range(lax.axis_size(axis))]


def sum_over_slabs(keep, send):
    other = lax.ppermute(send, "mode", partners("mode", 1))
    count = lax.axis_size("space")
    blocks = add_and_cut([keep, other], lax.axis_index("space"), count)
    terms = [blocks[0]] + [
        lax.ppermute(blocks[k], "space", partners("space", k)) for k in range(1, count)
    ]
    return add_and_cut(terms, lax.axis_index("mode") // 2, lax.axis_size("mode") // 2)


def sum_over_modes(blocks):
    return blocks[0] + sum(
        lax.ppermute(block, "mode", partners("mode", 2 * k))
        for k, block in enumerate(blocks) if k > 0
    )


def finish_kernel(aliased, scale_ref, swap_ref, x_ref, *refs):
    out_ref = refs[aliased]
    parts, _, each, _, width = x_ref.shape
    rows = parts * each
    scale = scale_ref[0, 0]
    value = x_ref[...].reshape(rows * GROUP, width)
    for top in range(0, rows, GROUP):
        block = value[top * GROUP:(top + GROUP) * GROUP]
        block = scale * jnp.dot(swap_ref[...], block, preferred_element_type=jnp.float32)
        out_ref[:, 0, top:top + GROUP, :] = block.astype(jnp.bfloat16).reshape(GROUP, GROUP, width)


def finish_fields(first, arrived, scale, previous):
    parts, fields, each, modes, width = arrived.shape
    rows = parts * each
    swap = swap_matrix(GROUP, GROUP)
    operands = [scale.reshape(1, 1), swap, arrived, *previous]
    return pl.pallas_call(
        functools.partial(finish_kernel, len(previous)),
        grid=(fields, modes // GROUP),
        out_shape=jax.ShapeDtypeStruct((modes, 3, rows, width), jnp.bfloat16),
        in_specs=[
            pl.BlockSpec(memory_space=pltpu.SMEM),
            pl.BlockSpec(swap.shape, lambda f, m: (0, 0)),
            pl.BlockSpec((parts, 1, each, GROUP, width), lambda f, m: (0, f, 0, m, 0)),
        ] + [pl.BlockSpec(memory_space=pltpu.HBM) for _ in previous],
        out_specs=pl.BlockSpec((GROUP, 1, rows, width), lambda f, m: (m, first + f, 0, 0)),
        input_output_aliases={3: 0} if previous else {},
        compiler_params=pltpu.CompilerParams(vmem_limit_bytes=VMEM_BYTES),
        cost_estimate=pl.CostEstimate(
            flops=fields * modes * rows * width,
            bytes_accessed=4 * fields * modes * rows * width,
            transcendentals=0,
        ),
        name="finish",
    )(*operands)


def send_edges(first, last):
    count = lax.axis_size("space")
    forward = [(i, i + 1) for i in range(count - 1)]
    backward = [(target, source) for source, target in forward]
    return lax.ppermute(last, "space", forward), lax.ppermute(first, "space", backward)


def shards(sqrt_factors, model_error, water_depth, sea_mask, givens_transform):
    modes, fields, rows, width = sqrt_factors.shape
    parts = lax.axis_size("mode")
    count = modes // GROUP
    swap = functools.partial(
        lax.all_to_all, axis_name="mode", split_axis=0, concat_axis=0, tiled=True
    )

    near = min(count, 2)
    water_depth, sea_mask = (
        pltpu.with_memory_space_constraint(value, pltpu.HBM) for value in (water_depth, sea_mask)
    )
    factors = pltpu.with_memory_space_constraint(sqrt_factors, pltpu.HBM)
    head = send_edges(*cut_edges(0, near, factors, (water_depth, sea_mask)))
    cut = cut_edges(near, count - near, factors, ()) if count > near else ()
    *head, = lax.optimization_barrier((*head, *cut))
    head, cut = head[:2], head[2:]
    static = (*head, water_depth, sea_mask)
    near_spread = spread_groups(0, near, sqrt_factors)
    chunks = [swap(forecast_groups(0, 1, 0, 0, 1, (), near_spread, *head, *static))]
    rest = ()
    if near > 1:
        rest = (forecast_groups(1, 1, 1, 0, count - 1, rest, near_spread, *head, *static),)
    if count > near:
        tail = send_edges(*cut)
        far_spread = spread_groups(near, count - near, sqrt_factors)
        rest = (forecast_groups(
            0, count - near, 0, near - 1, count - 1, rest, far_spread, *tail, *static
        ),)
    chunks += [swap(value) for value in rest]

    fault = model_error.transpose(1, 2, 0, 3)
    turn = givens_transform.T
    devices = lax.axis_size("space") * parts
    half = lax.rem(lax.axis_index("mode"), 2).reshape(1, 1)
    columns = turn.shape[1]
    cell_count = float(fields * rows * lax.axis_size("space") * width)

    arrived = swap(rotate_fields(0, 2, chunks, fault, turn, parts))
    blocks = sum_over_slabs(*local_gram(chunks, fault, turn, parts, devices, half))
    last = rotate_fields(2, fields - 2, chunks, fault, turn, parts)
    last, total = lax.optimization_barrier((last, sum_over_modes(blocks)))
    last = swap(last)
    gram = total[:columns // devices, :columns] / cell_count
    inflation = jnp.sqrt(total[0, columns] / total[0, columns + 1])

    reduced = finish_fields(0, arrived, inflation, ())
    reduced = finish_fields(2, last, inflation, (reduced,))
    return (reduced, gram, inflation)


def solution(mesh):
    in_specs = (
        P("mode", None, "space", None),
        P(None, None, ("space", "mode"), None),
        P("space", None),
        P("space", None),
        P(),
    )
    out_specs = (P("mode", None, "space", None), P(("space", "mode"), None), P())
    return jax.shard_map(shards, mesh=mesh, in_specs=in_specs, out_specs=out_specs, check_vma=False)
```

```python
import functools

import jax
import jax.numpy as jnp
import numpy as np
from jax import lax
from jax.experimental import pallas as pl
from jax.experimental.pallas import tpu as pltpu
from jax.sharding import PartitionSpec as P

flux_coef = 0.2
slope_coef = 0.2
turn_coef = 0.1
keep_coef = 0.95

GROUP = 16
HALO = 4
LANES = 128
VMEM_BYTES = 48 * 1024 * 1024


def column_diff(tiles):
    lane = lax.broadcasted_iota(jnp.int32, tiles[0].shape, 1)
    from_left = [pltpu.roll(tile, 1, 1) for tile in tiles]
    from_right = [pltpu.roll(tile, LANES - 1, 1) for tile in tiles]
    zero = jnp.zeros_like(tiles[0])
    out = []
    for t in range(len(tiles)):
        left = from_left[t - 1] if t > 0 else zero
        right = from_right[t + 1] if t + 1 < len(tiles) else zero
        previous = jnp.where(lane == 0, left, from_left[t])
        following = jnp.where(lane == LANES - 1, right, from_right[t])
        out.append(following - previous)
    return out


def swap_matrix(inner, outer):
    place = np.arange(inner * outer).reshape(outer, inner).T.reshape(-1)
    matrix = np.zeros((inner * outer, inner * outer), np.float32)
    matrix[np.arange(inner * outer), place] = 1.0
    return jnp.asarray(matrix, jnp.bfloat16)


def in_hbm(shape, dtype):
    return pltpu.HBM(shape, dtype)


def cut_edges_kernel(fixed, *refs):
    first_ref, last_ref = refs[:2]
    out_first, out_last = refs[-2:]
    group, fields = first_ref.shape[:2]
    for ref, out, low in ((first_ref, out_first, 0), (last_ref, out_last, GROUP - HALO)):
        for m in range(group):
            for field in range(fields):
                edge = ref[m, field].astype(jnp.float32)[low:low + HALO]
                out[m * fields + field] = edge.astype(jnp.bfloat16)
    if fixed:
        depth_ref, mask_ref = refs[2:4]
        for out, low in ((out_first, 0), (out_last, depth_ref.shape[0] - HALO)):
            rest = depth_ref[low:low + HALO]
            for piece in range(3):
                part = rest.astype(jnp.bfloat16)
                out[group * fields + piece] = part
                rest = rest - part.astype(jnp.float32)
            out[group * fields + 3] = mask_ref[low:low + HALO].astype(jnp.float32).astype(jnp.bfloat16)


def cut_edges(first, groups, factors, fixed):
    _, fields, rows, width = factors.shape
    size = GROUP * groups if fixed else GROUP
    steps = 1 if fixed else groups
    count = size * steps * fields + (4 if fixed else 0)
    block = size * fields + (4 if fixed else 0)
    place = jax.ShapeDtypeStruct if fixed else in_hbm
    out = place((count, HALO, width), jnp.bfloat16)
    return pl.pallas_call(
        functools.partial(cut_edges_kernel, bool(fixed)),
        grid=(steps,),
        out_shape=(out, out),
        in_specs=[
            pl.BlockSpec((size, fields, GROUP, width), lambda i: (first // (size // GROUP) + i, 0, 0, 0)),
            pl.BlockSpec((size, fields, GROUP, width),
                         lambda i: (first // (size // GROUP) + i, 0, rows // GROUP - 1, 0)),
        ] + [pl.BlockSpec(value.shape, lambda i: (0, 0)) for value in fixed],
        out_specs=[pl.BlockSpec((block, HALO, width), lambda i: (i, 0, 0))] * 2,
        compiler_params=pltpu.CompilerParams(vmem_limit_bytes=VMEM_BYTES),
        cost_estimate=pl.CostEstimate(
            flops=0, bytes_accessed=5 * count * HALO * width * 2, transcendentals=0
        ),
        name="cut_edges",
    )(factors, factors, *fixed)


def block_of(count):
    return max(size for size in range(1, 55) if count % size == 0)


def two_steps(rows, width, cells, depth, wet, surf1, east1, north1, surf2, put_row):
    tiles = width // LANES
    spots = [slice(t * LANES, (t + 1) * LANES) for t in range(tiles)]

    def get(ref, i):
        return [ref[i, :, spot] for spot in spots]

    def get_field(field, i):
        return [cells[field, i + HALO, :, spot] for spot in spots]

    def get_static(ref, i):
        parts = [ref[i + HALO, :, spot] for spot in spots]
        return [jnp.concatenate([part] * (GROUP // 8), axis=0) for part in parts]

    def put(ref, i, values):
        for spot, value in zip(spots, values):
            ref[i, :, spot] = value

    def times(one, other):
        return [a * b for a, b in zip(one, other)]

    def over_rows(first, last, body):
        size = block_of(last - first)

        def block(k, carry):
            body(first + k * size, size)
            return carry

        lax.fori_loop(0, (last - first) // size, block, 0)

    def surfaces(i, size, surface_at, east_at, north_at, put_at):
        flux = {j: times(get_static(depth, i + j), north_at(i + j)) for j in (-1, 0)}
        for j in range(size):
            flux[j + 1] = times(get_static(depth, i + j + 1), north_at(i + j + 1))
            sides = column_diff(times(get_static(depth, i + j), east_at(i + j)))
            sea, surface = get_static(wet, i + j), surface_at(i + j)
            put_at(i + j, [
                sea[t] * (surface[t] - (sides[t] + (flux[j + 1][t] - flux[j - 1][t])))
                for t in range(tiles)
            ])

    def flows(i, size, surface_at, east_at, north_at, put_at):
        surface = {j: surface_at(i + j) for j in (-1, 0)}
        for j in range(size):
            surface[j + 1] = surface_at(i + j + 1)
            sides = column_diff(surface[j])
            sea, east, north = get_static(wet, i + j), east_at(i + j), north_at(i + j)
            put_at(i + j, surface[j], [
                sea[t] * (keep_coef * east[t] + turn_coef * north[t] - sides[t])
                for t in range(tiles)
            ], [
                sea[t] * (keep_coef * north[t] - turn_coef * east[t]
                          - (surface[j + 1][t] - surface[j - 1][t]))
                for t in range(tiles)
            ])

    def first_surface(i, size):
        surfaces(
            i, size, lambda r: get_field(0, r), lambda r: get_field(1, r),
            lambda r: get_field(2, r), lambda r, value: put(surf1, r + 3, value),
        )

    def first_flow(i, size):
        def put_flow(r, surface, east, north):
            put(east1, r + 2, east)
            put(north1, r + 2, north)

        flows(
            i, size, lambda r: get(surf1, r + 3), lambda r: get_field(1, r),
            lambda r: get_field(2, r), put_flow,
        )

    def second_surface(i, size):
        surfaces(
            i, size, lambda r: get(surf1, r + 3), lambda r: get(east1, r + 2),
            lambda r: get(north1, r + 2), lambda r, value: put(surf2, r + 1, value),
        )

    def second_flow(i, size):
        def put_out(r, surface, east, north):
            surface = [value * (1.0 / slope_coef) for value in surface]
            for field, values in enumerate((surface, east, north)):
                for spot, value in zip(spots, values):
                    put_row(r, field, spot, value.astype(jnp.bfloat16))

        flows(
            i, size, lambda r: get(surf2, r + 1), lambda r: get(east1, r + 2),
            lambda r: get(north1, r + 2), put_out,
        )

    over_rows(-3, rows + 3, first_surface)
    over_rows(-2, rows + 2, first_flow)
    over_rows(-1, rows + 1, second_surface)
    over_rows(0, rows, second_flow)


def place_static(depth, wet, first, levels, seas):
    for j in range(levels.shape[0]):
        shape = depth.shape[1:]
        depth[first + j] = jnp.broadcast_to(flux_coef * slope_coef * levels[j:j + 1], shape)
        wet[first + j] = jnp.broadcast_to(seas[j:j + 1], shape)


def place_message_static(depth, wet, first, static_ref):
    value = static_ref[...].astype(jnp.float32)
    place_static(depth, wet, first, value[0] + value[1] + value[2], value[3])


def place_own_static(depth, wet, first, depth_ref, mask_ref, low, count):
    for top in range(low, low + count, 8):
        place_static(depth, wet, first + top - low, depth_ref[top:top + 8],
                     mask_ref[top:top + 8].astype(jnp.float32))


def spread_rows(x, swap_ref, field):
    width = x.shape[-1]
    block = jnp.dot(swap_ref[...], x.reshape(GROUP * GROUP, width), preferred_element_type=jnp.float32)
    block = block * slope_coef if field == 0 else block
    return block.reshape(GROUP, GROUP, width)


def spread_edges(ends, low_ref, high_ref, swap_ends_ref, field, fields):
    width = low_ref.shape[-1]
    if field == 0:
        ends[:, :HALO] = low_ref[...].astype(jnp.float32)
        ends[:, HALO:] = high_ref[...].astype(jnp.float32)
    block = jnp.concatenate([ends[m * fields + field] for m in range(GROUP)], axis=0)
    block = jnp.dot(
        swap_ends_ref[...], block.astype(jnp.bfloat16), preferred_element_type=jnp.float32
    ).reshape(2 * HALO, GROUP, width)
    return block * slope_coef if field == 0 else block


def forecast_kernel(x_ref, low_ref, high_ref, low_static, high_static, depth_ref, mask_ref,
                    swap_ref, swap_ends_ref, *refs):
    out_ref, cells, ends, depth, wet = refs[-9:-4]
    _, fields, rows, width = x_ref.shape

    for field in range(fields):
        for top in range(0, rows, GROUP):
            cells[field, HALO + top:HALO + top + GROUP] = spread_rows(
                x_ref[:, field, top:top + GROUP, :], swap_ref, field
            )
        block = spread_edges(ends, low_ref, high_ref, swap_ends_ref, field, fields)
        cells[field, :HALO] = block[:HALO]
        cells[field, HALO + rows:] = block[HALO:]
    place_message_static(depth, wet, 0, low_static)
    place_message_static(depth, wet, HALO + rows, high_static)
    place_own_static(depth, wet, HALO, depth_ref, mask_ref, 0, rows)

    def put_row(r, field, spot, value):
        out_ref[r, field, :, spot] = value

    two_steps(rows, width, cells, depth, wet, *refs[-4:], put_row)


def inner_kernel(x_ref, depth_ref, mask_ref, swap_ref, out_ref, cells, depth, wet, *steps):
    _, fields, rows, width = x_ref.shape
    for field in range(fields):
        for top in range(0, rows, GROUP):
            cells[field, HALO + top:HALO + top + GROUP] = spread_rows(
                x_ref[:, field, top:top + GROUP, :], swap_ref, field
            )
    for ref in (depth, wet, *(cells.at[field] for field in range(fields))):
        ref[:HALO] = jnp.zeros((HALO,) + ref.shape[1:], jnp.float32)
        ref[HALO + rows:] = jnp.zeros((HALO,) + ref.shape[1:], jnp.float32)
    place_own_static(depth, wet, HALO, depth_ref, mask_ref, 0, rows)

    def put_row(r, field, spot, value):
        out_ref[r, field, :, spot] = value

    two_steps(rows, width, cells, depth, wet, *steps, put_row)


def outer_kernel(first_ref, last_ref, low_ref, high_ref, low_static, high_static, depth_ref,
                 mask_ref, swap_ref, swap_ends_ref, inner_ref, out_ref,
                 cells, ends, edge, depth, wet, surf1, east1, north1, surf2, turned, sems):
    _, fields, _, width = first_ref.shape
    rows = out_ref.shape[0]
    for field in range(fields):
        edge[field] = spread_edges(ends, low_ref, high_ref, swap_ends_ref, field, fields)
    copies = []
    for side, (x_ref, first) in enumerate(((first_ref, 0), (last_ref, rows - HALO))):
        for field in range(fields):
            block = spread_rows(x_ref[:, field], swap_ref, field)
            if side == 0:
                cells[field, :HALO] = edge[field, :HALO]
                cells[field, HALO:] = block[:2 * HALO]
            else:
                cells[field, :2 * HALO] = block[GROUP - 2 * HALO:]
                cells[field, 2 * HALO:] = edge[field, HALO:]
        if side == 0:
            place_message_static(depth, wet, 0, low_static)
            place_own_static(depth, wet, HALO, depth_ref, mask_ref, 0, 2 * HALO)
        else:
            place_own_static(depth, wet, 0, depth_ref, mask_ref, rows - 2 * HALO, 2 * HALO)
            place_message_static(depth, wet, 2 * HALO, high_static)

        def put_row(r, field, spot, value):
            turned[side, r, field, :, spot] = value

        two_steps(HALO, width, cells, depth, wet, surf1, east1, north1, surf2, put_row)
        copies.append(pltpu.make_async_copy(
            turned.at[side], out_ref.at[pl.ds(first, HALO)], sems.at[side]
        ))
        copies[-1].start()
    for copy in copies:
        copy.wait()


def step_scratch(rows, width):
    return [pltpu.VMEM((rows + more, GROUP, width), jnp.float32) for more in (6, 4, 4, 2)]


def forecast_inner(factors, depth, mask):
    _, fields, rows, width = factors.shape
    padded = rows + 2 * HALO
    swap = swap_matrix(GROUP, GROUP)
    return pl.pallas_call(
        inner_kernel,
        grid=(1,),
        out_shape=in_hbm((rows, fields, GROUP, width), jnp.bfloat16),
        in_specs=[pl.BlockSpec((GROUP, fields, rows, width), lambda i: (0, 0, 0, 0))] + [
            pl.BlockSpec(value.shape, lambda i: (0, 0)) for value in (depth, mask, swap)
        ],
        out_specs=pl.BlockSpec((rows, fields, GROUP, width), lambda i: (0, 0, 0, 0)),
        scratch_shapes=[
            pltpu.VMEM((fields, padded, GROUP, width), jnp.float32),
            pltpu.VMEM((padded, 8, width), jnp.float32),
            pltpu.VMEM((padded, 8, width), jnp.float32),
        ] + step_scratch(rows, width),
        compiler_params=pltpu.CompilerParams(vmem_limit_bytes=VMEM_BYTES),
        cost_estimate=pl.CostEstimate(
            flops=60 * GROUP * rows * width,
            bytes_accessed=2 * 2 * GROUP * fields * rows * width,
            transcendentals=0,
        ),
        name="inner",
    )(factors, depth, mask, swap)


def forecast_outer(inner, factors, low, high, depth, mask):
    _, fields, rows, width = factors.shape
    edge = GROUP * fields
    last = low.shape[0] // 4 - 1
    swap, swap_ends = swap_matrix(GROUP, GROUP), swap_matrix(2 * HALO, GROUP)
    return pl.pallas_call(
        outer_kernel,
        grid=(1,),
        out_shape=in_hbm(inner.shape, inner.dtype),
        in_specs=[
            pl.BlockSpec((GROUP, fields, GROUP, width), lambda i: (0, 0, 0, 0)),
            pl.BlockSpec((GROUP, fields, GROUP, width), lambda i: (0, 0, rows // GROUP - 1, 0)),
            pl.BlockSpec((edge, HALO, width), lambda i: (0, 0, 0)),
            pl.BlockSpec((edge, HALO, width), lambda i: (0, 0, 0)),
            pl.BlockSpec((4, HALO, width), lambda i: (last, 0, 0)),
            pl.BlockSpec((4, HALO, width), lambda i: (last, 0, 0)),
        ] + [
            pl.BlockSpec(value.shape, lambda i: (0, 0)) for value in (depth, mask, swap, swap_ends)
        ] + [pl.BlockSpec(memory_space=pltpu.HBM)],
        out_specs=pl.BlockSpec(memory_space=pltpu.HBM),
        input_output_aliases={10: 0},
        scratch_shapes=[
            pltpu.VMEM((fields, 3 * HALO, GROUP, width), jnp.float32),
            pltpu.VMEM((edge, 2 * HALO, width), jnp.float32),
            pltpu.VMEM((fields, 2 * HALO, GROUP, width), jnp.float32),
            pltpu.VMEM((3 * HALO, 8, width), jnp.float32),
            pltpu.VMEM((3 * HALO, 8, width), jnp.float32),
        ] + step_scratch(HALO, width) + [
            pltpu.VMEM((2, HALO, fields, GROUP, width), jnp.bfloat16),
            pltpu.SemaphoreType.DMA((2,)),
        ],
        compiler_params=pltpu.CompilerParams(vmem_limit_bytes=VMEM_BYTES),
        cost_estimate=pl.CostEstimate(
            flops=20 * GROUP * rows * width,
            bytes_accessed=2 * 2 * GROUP * fields * GROUP * width,
            transcendentals=0,
        ),
        name="outer",
    )(factors, factors, low, high, low, high, depth, mask, swap, swap_ends, inner)


def forecast_groups(first, count, skip, place, whole_count, previous, factors, low, high,
                    static_low, static_high, depth, mask):
    modes, fields, rows, width = factors.shape
    padded = rows + 2 * HALO
    edge = GROUP * fields
    last = static_low.shape[0] // 4 - 1
    swap, swap_ends = swap_matrix(GROUP, GROUP), swap_matrix(2 * HALO, GROUP)

    def whole(value):
        return pl.BlockSpec(value.shape, lambda i: (0,) * value.ndim)

    return pl.pallas_call(
        forecast_kernel,
        grid=(count,),
        out_shape=in_hbm((rows, fields, whole_count * GROUP, width), jnp.bfloat16),
        in_specs=[
            pl.BlockSpec((GROUP, fields, rows, width), lambda i: (first + i, 0, 0, 0)),
            pl.BlockSpec((edge, HALO, width), lambda i: (skip + i, 0, 0)),
            pl.BlockSpec((edge, HALO, width), lambda i: (skip + i, 0, 0)),
            pl.BlockSpec((4, HALO, width), lambda i: (last, 0, 0)),
            pl.BlockSpec((4, HALO, width), lambda i: (last, 0, 0)),
            whole(depth),
            whole(mask),
            whole(swap),
            whole(swap_ends),
        ] + [pl.BlockSpec(memory_space=pltpu.HBM) for _ in previous],
        out_specs=pl.BlockSpec((rows, fields, GROUP, width), lambda i: (0, 0, place + i, 0)),
        input_output_aliases={9: 0} if previous else {},
        scratch_shapes=[
            pltpu.VMEM((fields, padded, GROUP, width), jnp.float32),
            pltpu.VMEM((edge, 2 * HALO, width), jnp.float32),
            pltpu.VMEM((padded, 8, width), jnp.float32),
            pltpu.VMEM((padded, 8, width), jnp.float32),
        ] + step_scratch(rows, width),
        compiler_params=pltpu.CompilerParams(vmem_limit_bytes=VMEM_BYTES),
        cost_estimate=pl.CostEstimate(
            flops=60 * count * GROUP * rows * width,
            bytes_accessed=2 * 2 * count * GROUP * fields * rows * width,
            transcendentals=0,
        ),
        name="forecast",
    )(factors, low, high, static_low, static_high, depth, mask, swap, swap_ends, *previous)


def all_columns(chunk_refs, fault_ref, j):
    own = [ref[:, j, 0] for ref in chunk_refs]
    joined = jnp.concatenate(own, axis=1)
    return joined.reshape(-1, joined.shape[-1]), fault_ref[0, j]


def rotate_kernel(count, *refs):
    chunk_refs = refs[:count]
    fault_ref, turn_ref, out_ref = refs[count:]
    parts, _, size, modes, width = out_ref.shape
    for j in range(size):
        columns = jnp.concatenate(all_columns(chunk_refs, fault_ref, j), axis=0)
        value = jnp.dot(turn_ref[...], columns, preferred_element_type=jnp.float32)
        out_ref[:, 0, j] = value.astype(jnp.bfloat16).reshape(parts, modes, width)


def by_part(chunks, parts):
    return [c.reshape((parts, c.shape[0] // parts) + c.shape[1:]) for c in chunks]


def rotate_fields(first, fields, chunks, fault, turn, parts):
    width = chunks[0].shape[-1]
    each = chunks[0].shape[0] // parts
    kept = turn.shape[0]
    noise = fault.shape[2]
    modes = kept // parts
    size = 3 if each % 3 == 0 else 1
    views = by_part(chunks, parts)
    return pl.pallas_call(
        functools.partial(rotate_kernel, len(views)),
        grid=(fields, each // size),
        out_shape=in_hbm((parts, fields, each, modes, width), jnp.bfloat16),
        in_specs=[
            pl.BlockSpec((parts, size, 1, v.shape[3], width), lambda f, j: (0, j, first + f, 0, 0))
            for v in views
        ] + [
            pl.BlockSpec((1, size, noise, width), lambda f, j: (first + f, j, 0, 0)),
            pl.BlockSpec(turn.shape, lambda f, j: (0, 0)),
        ],
        out_specs=pl.BlockSpec((parts, 1, size, modes, width), lambda f, j: (0, f, j, 0, 0)),
        compiler_params=pltpu.CompilerParams(vmem_limit_bytes=VMEM_BYTES),
        cost_estimate=pl.CostEstimate(
            flops=2 * fields * each * width * kept * turn.shape[1],
            bytes_accessed=2 * fields * each * width * (kept + turn.shape[1]),
            transcendentals=0,
        ),
        name="rotate",
    )(*views, fault, turn)


def gram_kernel(count, each, devices, *refs):
    chunk_refs = refs[:count]
    fault_ref, turn_ref, half_ref, keep_ref, send_ref, gram_ref = refs[count:]
    pairs = [all_columns(chunk_refs, fault_ref, j) for j in range(each)]
    columns = jnp.concatenate(
        [jnp.concatenate([prior, fault], axis=0) for prior, fault in pairs], axis=1
    )
    value = lax.dot_general(
        columns, columns, (((1,), (1,)), ((), ())), preferred_element_type=jnp.float32
    )
    step = pl.program_id(0)

    @pl.when(step == 0)
    def _():
        gram_ref[...] = value

    @pl.when(step > 0)
    def _():
        gram_ref[...] += value

    @pl.when(step == pl.num_programs(0) - 1)
    def _():
        gram = gram_ref[...]
        size = gram.shape[0]
        row = lax.broadcasted_iota(jnp.int32, gram.shape, 0)
        column = lax.broadcasted_iota(jnp.int32, gram.shape, 1)
        full = jnp.sum(jnp.where(row == column, gram, 0.0))
        turn = turn_ref[...]
        turned = 0.0
        for _ in range(3):
            piece = gram.astype(jnp.bfloat16)
            turned = turned + jnp.dot(turn, piece, preferred_element_type=jnp.float32)
            gram = gram - piece.astype(jnp.float32)
        kept = jnp.sum(turned * turn.astype(jnp.float32))
        own = size // devices
        slot = keep_ref.shape[0] // (devices // 2)
        lane = lax.broadcasted_iota(jnp.int32, (keep_ref.shape[0], LANES), 1)
        traces = jnp.where(lane == 0, full, jnp.where(lane == 1, kept, 0.0))
        low = half_ref[0, 0] == 0
        for out in (keep_ref, send_ref):
            if slot != own:
                out[...] = jnp.zeros_like(out)
            out[:, size:] = traces
        for q in range(devices // 2):
            even = gram_ref[2 * q * own:(2 * q + 1) * own]
            uneven = gram_ref[(2 * q + 1) * own:(2 * q + 2) * own]
            keep_ref[q * slot:q * slot + own, :size] = jnp.where(low, even, uneven)
            send_ref[q * slot:q * slot + own, :size] = jnp.where(low, uneven, even)


def local_gram(chunks, fault, turn, parts, devices, half):
    width = chunks[0].shape[-1]
    each = chunks[0].shape[0] // parts
    noise = fault.shape[2]
    columns = turn.shape[1]
    views = by_part(chunks, parts)
    slot = -(-columns // devices // 8) * 8
    slots = (devices // 2 * slot, columns + LANES)
    out = in_hbm(slots, jnp.float32)
    return pl.pallas_call(
        functools.partial(gram_kernel, len(views), each, devices),
        grid=(3,),
        out_shape=(out, out),
        in_specs=[
            pl.BlockSpec((parts, each, 1, v.shape[3], width), lambda f: (0, 0, f, 0, 0))
            for v in views
        ] + [
            pl.BlockSpec((1, each, noise, width), lambda f: (f, 0, 0, 0)),
            pl.BlockSpec(turn.shape, lambda f: (0, 0)),
            pl.BlockSpec(memory_space=pltpu.SMEM),
        ],
        out_specs=[pl.BlockSpec(slots, lambda f: (0, 0))] * 2,
        scratch_shapes=[pltpu.VMEM((columns, columns), jnp.float32)],
        compiler_params=pltpu.CompilerParams(vmem_limit_bytes=VMEM_BYTES),
        cost_estimate=pl.CostEstimate(
            flops=2 * 3 * each * width * columns * columns,
            bytes_accessed=2 * 3 * each * width * columns,
            transcendentals=0,
        ),
        name="gram",
    )(*views, fault, turn, half)


def add_kernel(count, parts, me_ref, *refs):
    total = refs[0][...]
    for ref in refs[1:count]:
        total = total + ref[...]
    total_ref = refs[-1]
    total_ref[...] = total
    rows = total.shape[0] // parts
    for k in range(parts):
        first = pl.multiple_of(jnp.bitwise_xor(me_ref[0, 0], k) * rows, 8)
        refs[count + k][...] = total_ref[pl.ds(first, rows)]


def add_and_cut(terms, me, parts):
    rows, width = terms[0].shape
    whole = pl.BlockSpec((rows, width), lambda: (0, 0))
    block = pl.BlockSpec((rows // parts, width), lambda: (0, 0))
    return pl.pallas_call(
        functools.partial(add_kernel, len(terms), parts),
        out_shape=[in_hbm((rows // parts, width), jnp.float32) for _ in range(parts)],
        in_specs=[pl.BlockSpec(memory_space=pltpu.SMEM)] + [whole for _ in terms],
        out_specs=[block for _ in range(parts)],
        scratch_shapes=[pltpu.VMEM((rows, width), jnp.float32)],
        compiler_params=pltpu.CompilerParams(vmem_limit_bytes=VMEM_BYTES),
        cost_estimate=pl.CostEstimate(
            flops=len(terms) * rows * width,
            bytes_accessed=4 * (len(terms) + 1) * rows * width,
            transcendentals=0,
        ),
        name="add",
    )(me.reshape(1, 1), *terms)


def partners(axis, distance):
    return [(i, i ^ distance) for i in range(lax.axis_size(axis))]


def sum_over_slabs(keep, send):
    other = lax.ppermute(send, "mode", partners("mode", 1))
    count = lax.axis_size("space")
    blocks = add_and_cut([keep, other], lax.axis_index("space"), count)
    terms = [blocks[0]] + [
        lax.ppermute(blocks[k], "space", partners("space", k)) for k in range(1, count)
    ]
    return add_and_cut(terms, lax.axis_index("mode") // 2, lax.axis_size("mode") // 2)


def sum_over_modes(blocks):
    return blocks[0] + sum(
        lax.ppermute(block, "mode", partners("mode", 2 * k))
        for k, block in enumerate(blocks) if k > 0
    )


def finish_kernel(aliased, scale_ref, swap_ref, x_ref, *refs):
    out_ref = refs[aliased]
    parts, _, each, _, width = x_ref.shape
    rows = parts * each
    scale = scale_ref[0, 0]
    value = x_ref[...].reshape(rows * GROUP, width)
    for top in range(0, rows, GROUP):
        block = value[top * GROUP:(top + GROUP) * GROUP]
        block = scale * jnp.dot(swap_ref[...], block, preferred_element_type=jnp.float32)
        out_ref[:, 0, top:top + GROUP, :] = block.astype(jnp.bfloat16).reshape(GROUP, GROUP, width)


def finish_fields(first, arrived, scale, previous):
    parts, fields, each, modes, width = arrived.shape
    rows = parts * each
    swap = swap_matrix(GROUP, GROUP)
    operands = [scale.reshape(1, 1), swap, arrived, *previous]
    return pl.pallas_call(
        functools.partial(finish_kernel, len(previous)),
        grid=(fields, modes // GROUP),
        out_shape=jax.ShapeDtypeStruct((modes, 3, rows, width), jnp.bfloat16),
        in_specs=[
            pl.BlockSpec(memory_space=pltpu.SMEM),
            pl.BlockSpec(swap.shape, lambda f, m: (0, 0)),
            pl.BlockSpec((parts, 1, each, GROUP, width), lambda f, m: (0, f, 0, m, 0)),
        ] + [pl.BlockSpec(memory_space=pltpu.HBM) for _ in previous],
        out_specs=pl.BlockSpec((GROUP, 1, rows, width), lambda f, m: (m, first + f, 0, 0)),
        input_output_aliases={3: 0} if previous else {},
        compiler_params=pltpu.CompilerParams(vmem_limit_bytes=VMEM_BYTES),
        cost_estimate=pl.CostEstimate(
            flops=fields * modes * rows * width,
            bytes_accessed=4 * fields * modes * rows * width,
            transcendentals=0,
        ),
        name="finish",
    )(*operands)


def send_edges(first, last):
    count = lax.axis_size("space")
    forward = [(i, i + 1) for i in range(count - 1)]
    backward = [(target, source) for source, target in forward]
    return lax.ppermute(last, "space", forward), lax.ppermute(first, "space", backward)


def shards(sqrt_factors, model_error, water_depth, sea_mask, givens_transform):
    modes, fields, rows, width = sqrt_factors.shape
    parts = lax.axis_size("mode")
    count = modes // GROUP
    swap = functools.partial(
        lax.all_to_all, axis_name="mode", split_axis=0, concat_axis=0, tiled=True
    )

    near = min(count, 2)
    water_depth, sea_mask = (
        pltpu.with_memory_space_constraint(value, pltpu.HBM) for value in (water_depth, sea_mask)
    )
    factors = pltpu.with_memory_space_constraint(sqrt_factors, pltpu.HBM)
    head = send_edges(*cut_edges(0, near, factors, (water_depth, sea_mask)))
    cut = cut_edges(near, count - near, factors, ()) if count > near else ()
    *head, = lax.optimization_barrier((*head, *cut))
    head, cut = head[:2], head[2:]
    static = (*head, water_depth, sea_mask)
    inner = forecast_inner(sqrt_factors, water_depth, sea_mask)
    chunks = [swap(forecast_outer(inner, sqrt_factors, *static))]
    rest = ()
    if near > 1:
        rest = (forecast_groups(1, 1, 1, 0, count - 1, rest, sqrt_factors, *head, *static),)
    if count > near:
        tail = send_edges(*cut)
        rest = (forecast_groups(
            near, count - near, 0, near - 1, count - 1, rest, sqrt_factors, *tail, *static
        ),)
    chunks += [swap(value) for value in rest]

    fault = model_error.transpose(1, 2, 0, 3)
    turn = givens_transform.T
    devices = lax.axis_size("space") * parts
    half = lax.rem(lax.axis_index("mode"), 2).reshape(1, 1)
    columns = turn.shape[1]
    cell_count = float(fields * rows * lax.axis_size("space") * width)

    arrived = swap(rotate_fields(0, 2, chunks, fault, turn, parts))
    blocks = sum_over_slabs(*local_gram(chunks, fault, turn, parts, devices, half))
    last = rotate_fields(2, fields - 2, chunks, fault, turn, parts)
    last, total = lax.optimization_barrier((last, sum_over_modes(blocks)))
    last = swap(last)
    gram = total[:columns // devices, :columns] / cell_count
    inflation = jnp.sqrt(total[0, columns] / total[0, columns + 1])

    reduced = finish_fields(0, arrived, inflation, ())
    reduced = finish_fields(2, last, inflation, (reduced,))
    return (reduced, gram, inflation)


def solution(mesh):
    in_specs = (
        P("mode", None, "space", None),
        P(None, None, ("space", "mode"), None),
        P("space", None),
        P("space", None),
        P(),
    )
    out_specs = (P("mode", None, "space", None), P(("space", "mode"), None), P())
    return jax.shard_map(shards, mesh=mesh, in_specs=in_specs, out_specs=out_specs, check_vma=False)
```

```python
import functools

import jax
import jax.numpy as jnp
import numpy as np
from jax import lax
from jax.experimental import pallas as pl
from jax.experimental.pallas import tpu as pltpu
from jax.sharding import PartitionSpec as P

flux_coef = 0.2
slope_coef = 0.2
turn_coef = 0.1
keep_coef = 0.95

GROUP = 16
HALO = 4
LANES = 128
VMEM_BYTES = 48 * 1024 * 1024


def column_diff(tiles):
    lane = lax.broadcasted_iota(jnp.int32, tiles[0].shape, 1)
    from_left = [pltpu.roll(tile, 1, 1) for tile in tiles]
    from_right = [pltpu.roll(tile, LANES - 1, 1) for tile in tiles]
    zero = jnp.zeros_like(tiles[0])
    out = []
    for t in range(len(tiles)):
        left = from_left[t - 1] if t > 0 else zero
        right = from_right[t + 1] if t + 1 < len(tiles) else zero
        previous = jnp.where(lane == 0, left, from_left[t])
        following = jnp.where(lane == LANES - 1, right, from_right[t])
        out.append(following - previous)
    return out


def swap_matrix(inner, outer):
    place = np.arange(inner * outer).reshape(outer, inner).T.reshape(-1)
    matrix = np.zeros((inner * outer, inner * outer), np.float32)
    matrix[np.arange(inner * outer), place] = 1.0
    return jnp.asarray(matrix, jnp.bfloat16)


def in_hbm(shape, dtype):
    return pltpu.HBM(shape, dtype)


def cut_edges_kernel(fixed, *refs):
    first_ref, last_ref = refs[:2]
    out_first, out_last = refs[-2:]
    group, fields = first_ref.shape[:2]
    for ref, out, low in ((first_ref, out_first, 0), (last_ref, out_last, GROUP - HALO)):
        for m in range(group):
            for field in range(fields):
                edge = ref[m, field].astype(jnp.float32)[low:low + HALO]
                out[m * fields + field] = edge.astype(jnp.bfloat16)
    if fixed:
        depth_ref, mask_ref = refs[2:4]
        for out, low in ((out_first, 0), (out_last, depth_ref.shape[0] - HALO)):
            rest = depth_ref[low:low + HALO]
            for piece in range(3):
                part = rest.astype(jnp.bfloat16)
                out[group * fields + piece] = part
                rest = rest - part.astype(jnp.float32)
            out[group * fields + 3] = mask_ref[low:low + HALO].astype(jnp.float32).astype(jnp.bfloat16)


def cut_edges(first, groups, factors, fixed):
    _, fields, rows, width = factors.shape
    size = GROUP * groups if fixed else GROUP
    steps = 1 if fixed else groups
    count = size * steps * fields + (4 if fixed else 0)
    block = size * fields + (4 if fixed else 0)
    place = jax.ShapeDtypeStruct if fixed else in_hbm
    out = place((count, HALO, width), jnp.bfloat16)
    return pl.pallas_call(
        functools.partial(cut_edges_kernel, bool(fixed)),
        grid=(steps,),
        out_shape=(out, out),
        in_specs=[
            pl.BlockSpec((size, fields, GROUP, width), lambda i: (first // (size // GROUP) + i, 0, 0, 0)),
            pl.BlockSpec((size, fields, GROUP, width),
                         lambda i: (first // (size // GROUP) + i, 0, rows // GROUP - 1, 0)),
        ] + [pl.BlockSpec(value.shape, lambda i: (0, 0)) for value in fixed],
        out_specs=[pl.BlockSpec((block, HALO, width), lambda i: (i, 0, 0))] * 2,
        compiler_params=pltpu.CompilerParams(vmem_limit_bytes=VMEM_BYTES),
        cost_estimate=pl.CostEstimate(
            flops=0, bytes_accessed=5 * count * HALO * width * 2, transcendentals=0
        ),
        name="cut_edges",
    )(factors, factors, *fixed)


def block_of(count):
    return max(size for size in range(1, 55) if count % size == 0)


def two_steps(rows, width, cells, depth, wet, surf1, east1, north1, surf2, put_row):
    tiles = width // LANES
    spots = [slice(t * LANES, (t + 1) * LANES) for t in range(tiles)]

    def get(ref, i):
        return [ref[i, :, spot] for spot in spots]

    def get_field(field, i):
        return [cells[field, i + HALO, :, spot] for spot in spots]

    def get_static(ref, i):
        parts = [ref[i + HALO, :, spot] for spot in spots]
        return [jnp.concatenate([part] * (GROUP // 8), axis=0) for part in parts]

    def put(ref, i, values):
        for spot, value in zip(spots, values):
            ref[i, :, spot] = value

    def times(one, other):
        return [a * b for a, b in zip(one, other)]

    def over_rows(first, last, body):
        size = block_of(last - first)

        def block(k, carry):
            body(first + k * size, size)
            return carry

        lax.fori_loop(0, (last - first) // size, block, 0)

    def surfaces(i, size, surface_at, east_at, north_at, put_at):
        flux = {j: times(get_static(depth, i + j), north_at(i + j)) for j in (-1, 0)}
        for j in range(size):
            flux[j + 1] = times(get_static(depth, i + j + 1), north_at(i + j + 1))
            sides = column_diff(times(get_static(depth, i + j), east_at(i + j)))
            sea, surface = get_static(wet, i + j), surface_at(i + j)
            put_at(i + j, [
                sea[t] * (surface[t] - (sides[t] + (flux[j + 1][t] - flux[j - 1][t])))
                for t in range(tiles)
            ])

    def flows(i, size, surface_at, east_at, north_at, put_at):
        surface = {j: surface_at(i + j) for j in (-1, 0)}
        for j in range(size):
            surface[j + 1] = surface_at(i + j + 1)
            sides = column_diff(surface[j])
            sea, east, north = get_static(wet, i + j), east_at(i + j), north_at(i + j)
            put_at(i + j, surface[j], [
                sea[t] * (keep_coef * east[t] + turn_coef * north[t] - sides[t])
                for t in range(tiles)
            ], [
                sea[t] * (keep_coef * north[t] - turn_coef * east[t]
                          - (surface[j + 1][t] - surface[j - 1][t]))
                for t in range(tiles)
            ])

    def first_surface(i, size):
        surfaces(
            i, size, lambda r: get_field(0, r), lambda r: get_field(1, r),
            lambda r: get_field(2, r), lambda r, value: put(surf1, r + 3, value),
        )

    def first_flow(i, size):
        def put_flow(r, surface, east, north):
            put(east1, r + 2, east)
            put(north1, r + 2, north)

        flows(
            i, size, lambda r: get(surf1, r + 3), lambda r: get_field(1, r),
            lambda r: get_field(2, r), put_flow,
        )

    def second_surface(i, size):
        surfaces(
            i, size, lambda r: get(surf1, r + 3), lambda r: get(east1, r + 2),
            lambda r: get(north1, r + 2), lambda r, value: put(surf2, r + 1, value),
        )

    def second_flow(i, size):
        def put_out(r, surface, east, north):
            surface = [value * (1.0 / slope_coef) for value in surface]
            for field, values in enumerate((surface, east, north)):
                for spot, value in zip(spots, values):
                    put_row(r, field, spot, value.astype(jnp.bfloat16))

        flows(
            i, size, lambda r: get(surf2, r + 1), lambda r: get(east1, r + 2),
            lambda r: get(north1, r + 2), put_out,
        )

    over_rows(-3, rows + 3, first_surface)
    over_rows(-2, rows + 2, first_flow)
    over_rows(-1, rows + 1, second_surface)
    over_rows(0, rows, second_flow)


def place_static(depth, wet, first, levels, seas):
    for j in range(levels.shape[0]):
        shape = depth.shape[1:]
        depth[first + j] = jnp.broadcast_to(flux_coef * slope_coef * levels[j:j + 1], shape)
        wet[first + j] = jnp.broadcast_to(seas[j:j + 1], shape)


def place_message_static(depth, wet, first, static_ref):
    value = static_ref[...].astype(jnp.float32)
    place_static(depth, wet, first, value[0] + value[1] + value[2], value[3])


def place_own_static(depth, wet, first, depth_ref, mask_ref, low, count):
    for top in range(low, low + count, 8):
        place_static(depth, wet, first + top - low, depth_ref[top:top + 8],
                     mask_ref[top:top + 8].astype(jnp.float32))


def spread_rows(x, swap_ref, field):
    width = x.shape[-1]
    block = jnp.dot(swap_ref[...], x.reshape(GROUP * GROUP, width), preferred_element_type=jnp.float32)
    block = block * slope_coef if field == 0 else block
    return block.reshape(GROUP, GROUP, width)


def spread_edges(ends, low_ref, high_ref, swap_ends_ref, field, fields):
    width = low_ref.shape[-1]
    if field == 0:
        ends[:, :HALO] = low_ref[...].astype(jnp.float32)
        ends[:, HALO:] = high_ref[...].astype(jnp.float32)
    block = jnp.concatenate([ends[m * fields + field] for m in range(GROUP)], axis=0)
    block = jnp.dot(
        swap_ends_ref[...], block.astype(jnp.bfloat16), preferred_element_type=jnp.float32
    ).reshape(2 * HALO, GROUP, width)
    return block * slope_coef if field == 0 else block


def forecast_kernel(x_ref, low_ref, high_ref, low_static, high_static, depth_ref, mask_ref,
                    swap_ref, swap_ends_ref, *refs):
    out_ref, cells, ends, depth, wet = refs[-9:-4]
    _, fields, rows, width = x_ref.shape

    for field in range(fields):
        for top in range(0, rows, GROUP):
            cells[field, HALO + top:HALO + top + GROUP] = spread_rows(
                x_ref[:, field, top:top + GROUP, :], swap_ref, field
            )
        block = spread_edges(ends, low_ref, high_ref, swap_ends_ref, field, fields)
        cells[field, :HALO] = block[:HALO]
        cells[field, HALO + rows:] = block[HALO:]
    place_message_static(depth, wet, 0, low_static)
    place_message_static(depth, wet, HALO + rows, high_static)
    place_own_static(depth, wet, HALO, depth_ref, mask_ref, 0, rows)

    def put_row(r, field, spot, value):
        out_ref[r, field, :, spot] = value

    two_steps(rows, width, cells, depth, wet, *refs[-4:], put_row)


def inner_kernel(x_ref, depth_ref, mask_ref, swap_ref, out_ref, cells, depth, wet, *steps):
    _, fields, rows, width = x_ref.shape
    for field in range(fields):
        for top in range(0, rows, GROUP):
            cells[field, HALO + top:HALO + top + GROUP] = spread_rows(
                x_ref[:, field, top:top + GROUP, :], swap_ref, field
            )
    for ref in (depth, wet, *(cells.at[field] for field in range(fields))):
        ref[:HALO] = jnp.zeros((HALO,) + ref.shape[1:], jnp.float32)
        ref[HALO + rows:] = jnp.zeros((HALO,) + ref.shape[1:], jnp.float32)
    place_own_static(depth, wet, HALO, depth_ref, mask_ref, 0, rows)

    def put_row(r, field, spot, value):
        out_ref[r, field, :, spot] = value

    two_steps(rows, width, cells, depth, wet, *steps, put_row)


def outer_kernel(first_ref, last_ref, low_ref, high_ref, low_static, high_static, depth_ref,
                 mask_ref, swap_ref, swap_ends_ref, inner_ref, out_ref,
                 cells, ends, edge, depth, wet, surf1, east1, north1, surf2, turned, sems):
    _, fields, _, width = first_ref.shape
    rows = out_ref.shape[0]
    for field in range(fields):
        edge[field] = spread_edges(ends, low_ref, high_ref, swap_ends_ref, field, fields)
    copies = []
    for side, (x_ref, first) in enumerate(((first_ref, 0), (last_ref, rows - HALO))):
        for field in range(fields):
            block = spread_rows(x_ref[:, field], swap_ref, field)
            if side == 0:
                cells[field, :HALO] = edge[field, :HALO]
                cells[field, HALO:] = block[:2 * HALO]
            else:
                cells[field, :2 * HALO] = block[GROUP - 2 * HALO:]
                cells[field, 2 * HALO:] = edge[field, HALO:]
        if side == 0:
            place_message_static(depth, wet, 0, low_static)
            place_own_static(depth, wet, HALO, depth_ref, mask_ref, 0, 2 * HALO)
        else:
            place_own_static(depth, wet, 0, depth_ref, mask_ref, rows - 2 * HALO, 2 * HALO)
            place_message_static(depth, wet, 2 * HALO, high_static)

        def put_row(r, field, spot, value):
            turned[side, r, field, :, spot] = value

        two_steps(HALO, width, cells, depth, wet, surf1, east1, north1, surf2, put_row)
        copies.append(pltpu.make_async_copy(
            turned.at[side], out_ref.at[pl.ds(first, HALO)], sems.at[side]
        ))
        copies[-1].start()
    for copy in copies:
        copy.wait()


def step_scratch(rows, width):
    return [pltpu.VMEM((rows + more, GROUP, width), jnp.float32) for more in (6, 4, 4, 2)]


def forecast_inner(factors, depth, mask):
    _, fields, rows, width = factors.shape
    padded = rows + 2 * HALO
    swap = swap_matrix(GROUP, GROUP)
    return pl.pallas_call(
        inner_kernel,
        grid=(1,),
        out_shape=in_hbm((rows, fields, GROUP, width), jnp.bfloat16),
        in_specs=[pl.BlockSpec((GROUP, fields, rows, width), lambda i: (0, 0, 0, 0))] + [
            pl.BlockSpec(value.shape, lambda i: (0, 0)) for value in (depth, mask, swap)
        ],
        out_specs=pl.BlockSpec((rows, fields, GROUP, width), lambda i: (0, 0, 0, 0)),
        scratch_shapes=[
            pltpu.VMEM((fields, padded, GROUP, width), jnp.float32),
            pltpu.VMEM((padded, 8, width), jnp.float32),
            pltpu.VMEM((padded, 8, width), jnp.float32),
        ] + step_scratch(rows, width),
        compiler_params=pltpu.CompilerParams(vmem_limit_bytes=VMEM_BYTES),
        cost_estimate=pl.CostEstimate(
            flops=60 * GROUP * rows * width,
            bytes_accessed=2 * 2 * GROUP * fields * rows * width,
            transcendentals=0,
        ),
        name="inner",
    )(factors, depth, mask, swap)


def forecast_outer(inner, factors, low, high, depth, mask):
    _, fields, rows, width = factors.shape
    edge = GROUP * fields
    last = low.shape[0] // 4 - 1
    swap, swap_ends = swap_matrix(GROUP, GROUP), swap_matrix(2 * HALO, GROUP)
    return pl.pallas_call(
        outer_kernel,
        grid=(1,),
        out_shape=in_hbm(inner.shape, inner.dtype),
        in_specs=[
            pl.BlockSpec((GROUP, fields, GROUP, width), lambda i: (0, 0, 0, 0)),
            pl.BlockSpec((GROUP, fields, GROUP, width), lambda i: (0, 0, rows // GROUP - 1, 0)),
            pl.BlockSpec((edge, HALO, width), lambda i: (0, 0, 0)),
            pl.BlockSpec((edge, HALO, width), lambda i: (0, 0, 0)),
            pl.BlockSpec((4, HALO, width), lambda i: (last, 0, 0)),
            pl.BlockSpec((4, HALO, width), lambda i: (last, 0, 0)),
        ] + [
            pl.BlockSpec(value.shape, lambda i: (0, 0)) for value in (depth, mask, swap, swap_ends)
        ] + [pl.BlockSpec(memory_space=pltpu.HBM)],
        out_specs=pl.BlockSpec(memory_space=pltpu.HBM),
        input_output_aliases={10: 0},
        scratch_shapes=[
            pltpu.VMEM((fields, 3 * HALO, GROUP, width), jnp.float32),
            pltpu.VMEM((edge, 2 * HALO, width), jnp.float32),
            pltpu.VMEM((fields, 2 * HALO, GROUP, width), jnp.float32),
            pltpu.VMEM((3 * HALO, 8, width), jnp.float32),
            pltpu.VMEM((3 * HALO, 8, width), jnp.float32),
        ] + step_scratch(HALO, width) + [
            pltpu.VMEM((2, HALO, fields, GROUP, width), jnp.bfloat16),
            pltpu.SemaphoreType.DMA((2,)),
        ],
        compiler_params=pltpu.CompilerParams(vmem_limit_bytes=VMEM_BYTES),
        cost_estimate=pl.CostEstimate(
            flops=20 * GROUP * rows * width,
            bytes_accessed=2 * 2 * GROUP * fields * GROUP * width,
            transcendentals=0,
        ),
        name="outer",
    )(factors, factors, low, high, low, high, depth, mask, swap, swap_ends, inner)


def forecast_groups(first, count, skip, place, whole_count, previous, factors, low, high,
                    static_low, static_high, depth, mask):
    modes, fields, rows, width = factors.shape
    padded = rows + 2 * HALO
    edge = GROUP * fields
    last = static_low.shape[0] // 4 - 1
    swap, swap_ends = swap_matrix(GROUP, GROUP), swap_matrix(2 * HALO, GROUP)

    def whole(value):
        return pl.BlockSpec(value.shape, lambda i: (0,) * value.ndim)

    return pl.pallas_call(
        forecast_kernel,
        grid=(count,),
        out_shape=in_hbm((rows, fields, whole_count * GROUP, width), jnp.bfloat16),
        in_specs=[
            pl.BlockSpec((GROUP, fields, rows, width), lambda i: (first + i, 0, 0, 0)),
            pl.BlockSpec((edge, HALO, width), lambda i: (skip + i, 0, 0)),
            pl.BlockSpec((edge, HALO, width), lambda i: (skip + i, 0, 0)),
            pl.BlockSpec((4, HALO, width), lambda i: (last, 0, 0)),
            pl.BlockSpec((4, HALO, width), lambda i: (last, 0, 0)),
            whole(depth),
            whole(mask),
            whole(swap),
            whole(swap_ends),
        ] + [pl.BlockSpec(memory_space=pltpu.HBM) for _ in previous],
        out_specs=pl.BlockSpec((rows, fields, GROUP, width), lambda i: (0, 0, place + i, 0)),
        input_output_aliases={9: 0} if previous else {},
        scratch_shapes=[
            pltpu.VMEM((fields, padded, GROUP, width), jnp.float32),
            pltpu.VMEM((edge, 2 * HALO, width), jnp.float32),
            pltpu.VMEM((padded, 8, width), jnp.float32),
            pltpu.VMEM((padded, 8, width), jnp.float32),
        ] + step_scratch(rows, width),
        compiler_params=pltpu.CompilerParams(vmem_limit_bytes=VMEM_BYTES),
        cost_estimate=pl.CostEstimate(
            flops=60 * count * GROUP * rows * width,
            bytes_accessed=2 * 2 * count * GROUP * fields * rows * width,
            transcendentals=0,
        ),
        name="forecast",
    )(factors, low, high, static_low, static_high, depth, mask, swap, swap_ends, *previous)


def all_columns(chunk_refs, fault_ref, j):
    own = [ref[:, j, 0] for ref in chunk_refs]
    joined = jnp.concatenate(own, axis=1)
    return joined.reshape(-1, joined.shape[-1]), fault_ref[0, j]


def rotate_kernel(count, *refs):
    chunk_refs = refs[:count]
    fault_ref, turn_ref, out_ref = refs[count:]
    parts, _, size, modes, width = out_ref.shape
    columns = jnp.concatenate(
        [jnp.concatenate(all_columns(chunk_refs, fault_ref, j), axis=0) for j in range(size)], axis=1
    )
    value = jnp.dot(turn_ref[...], columns, preferred_element_type=jnp.float32).astype(jnp.bfloat16)
    for j in range(size):
        out_ref[:, 0, j] = value[:, j * width:(j + 1) * width].reshape(parts, modes, width)


def by_part(chunks, parts):
    return [c.reshape((parts, c.shape[0] // parts) + c.shape[1:]) for c in chunks]


def rotate_fields(first, fields, chunks, fault, turn, parts):
    width = chunks[0].shape[-1]
    each = chunks[0].shape[0] // parts
    kept = turn.shape[0]
    noise = fault.shape[2]
    modes = kept // parts
    size = 3 if each % 3 == 0 else 1
    views = by_part(chunks, parts)
    return pl.pallas_call(
        functools.partial(rotate_kernel, len(views)),
        grid=(fields, each // size),
        out_shape=in_hbm((parts, fields, each, modes, width), jnp.bfloat16),
        in_specs=[
            pl.BlockSpec((parts, size, 1, v.shape[3], width), lambda f, j: (0, j, first + f, 0, 0))
            for v in views
        ] + [
            pl.BlockSpec((1, size, noise, width), lambda f, j: (first + f, j, 0, 0)),
            pl.BlockSpec(turn.shape, lambda f, j: (0, 0)),
        ],
        out_specs=pl.BlockSpec((parts, 1, size, modes, width), lambda f, j: (0, f, j, 0, 0)),
        compiler_params=pltpu.CompilerParams(vmem_limit_bytes=VMEM_BYTES),
        cost_estimate=pl.CostEstimate(
            flops=2 * fields * each * width * kept * turn.shape[1],
            bytes_accessed=2 * fields * each * width * (kept + turn.shape[1]),
            transcendentals=0,
        ),
        name="rotate",
    )(*views, fault, turn)


def gram_kernel(count, each, devices, *refs):
    chunk_refs = refs[:count]
    fault_ref, turn_ref, half_ref, keep_ref, send_ref, gram_ref = refs[count:]
    pairs = [all_columns(chunk_refs, fault_ref, j) for j in range(each)]
    columns = jnp.concatenate(
        [jnp.concatenate([prior, fault], axis=0) for prior, fault in pairs], axis=1
    )
    value = lax.dot_general(
        columns, columns, (((1,), (1,)), ((), ())), preferred_element_type=jnp.float32
    )
    step = pl.program_id(0)

    @pl.when(step == 0)
    def _():
        gram_ref[...] = value

    @pl.when(step > 0)
    def _():
        gram_ref[...] += value

    @pl.when(step == pl.num_programs(0) - 1)
    def _():
        gram = gram_ref[...]
        size = gram.shape[0]
        row = lax.broadcasted_iota(jnp.int32, gram.shape, 0)
        column = lax.broadcasted_iota(jnp.int32, gram.shape, 1)
        full = jnp.sum(jnp.where(row == column, gram, 0.0))
        turn = turn_ref[...]
        turned = 0.0
        for _ in range(3):
            piece = gram.astype(jnp.bfloat16)
            turned = turned + jnp.dot(turn, piece, preferred_element_type=jnp.float32)
            gram = gram - piece.astype(jnp.float32)
        kept = jnp.sum(turned * turn.astype(jnp.float32))
        own = size // devices
        slot = keep_ref.shape[0] // (devices // 2)
        lane = lax.broadcasted_iota(jnp.int32, (keep_ref.shape[0], LANES), 1)
        traces = jnp.where(lane == 0, full, jnp.where(lane == 1, kept, 0.0))
        low = half_ref[0, 0] == 0
        for out in (keep_ref, send_ref):
            if slot != own:
                out[...] = jnp.zeros_like(out)
            out[:, size:] = traces
        for q in range(devices // 2):
            even = gram_ref[2 * q * own:(2 * q + 1) * own]
            uneven = gram_ref[(2 * q + 1) * own:(2 * q + 2) * own]
            keep_ref[q * slot:q * slot + own, :size] = jnp.where(low, even, uneven)
            send_ref[q * slot:q * slot + own, :size] = jnp.where(low, uneven, even)


def local_gram(chunks, fault, turn, parts, devices, half):
    width = chunks[0].shape[-1]
    each = chunks[0].shape[0] // parts
    noise = fault.shape[2]
    columns = turn.shape[1]
    views = by_part(chunks, parts)
    slot = -(-columns // devices // 8) * 8
    slots = (devices // 2 * slot, columns + LANES)
    out = in_hbm(slots, jnp.float32)
    return pl.pallas_call(
        functools.partial(gram_kernel, len(views), each, devices),
        grid=(3,),
        out_shape=(out, out),
        in_specs=[
            pl.BlockSpec((parts, each, 1, v.shape[3], width), lambda f: (0, 0, f, 0, 0))
            for v in views
        ] + [
            pl.BlockSpec((1, each, noise, width), lambda f: (f, 0, 0, 0)),
            pl.BlockSpec(turn.shape, lambda f: (0, 0)),
            pl.BlockSpec(memory_space=pltpu.SMEM),
        ],
        out_specs=[pl.BlockSpec(slots, lambda f: (0, 0))] * 2,
        scratch_shapes=[pltpu.VMEM((columns, columns), jnp.float32)],
        compiler_params=pltpu.CompilerParams(vmem_limit_bytes=VMEM_BYTES),
        cost_estimate=pl.CostEstimate(
            flops=2 * 3 * each * width * columns * columns,
            bytes_accessed=2 * 3 * each * width * columns,
            transcendentals=0,
        ),
        name="gram",
    )(*views, fault, turn, half)


def add_kernel(count, parts, me_ref, *refs):
    total = refs[0][...]
    for ref in refs[1:count]:
        total = total + ref[...]
    total_ref = refs[-1]
    total_ref[...] = total
    rows = total.shape[0] // parts
    for k in range(parts):
        first = pl.multiple_of(jnp.bitwise_xor(me_ref[0, 0], k) * rows, 8)
        refs[count + k][...] = total_ref[pl.ds(first, rows)]


def add_and_cut(terms, me, parts):
    rows, width = terms[0].shape
    whole = pl.BlockSpec((rows, width), lambda: (0, 0))
    block = pl.BlockSpec((rows // parts, width), lambda: (0, 0))
    return pl.pallas_call(
        functools.partial(add_kernel, len(terms), parts),
        out_shape=[in_hbm((rows // parts, width), jnp.float32) for _ in range(parts)],
        in_specs=[pl.BlockSpec(memory_space=pltpu.SMEM)] + [whole for _ in terms],
        out_specs=[block for _ in range(parts)],
        scratch_shapes=[pltpu.VMEM((rows, width), jnp.float32)],
        compiler_params=pltpu.CompilerParams(vmem_limit_bytes=VMEM_BYTES),
        cost_estimate=pl.CostEstimate(
            flops=len(terms) * rows * width,
            bytes_accessed=4 * (len(terms) + 1) * rows * width,
            transcendentals=0,
        ),
        name="add",
    )(me.reshape(1, 1), *terms)


def partners(axis, distance):
    return [(i, i ^ distance) for i in range(lax.axis_size(axis))]


def sum_over_slabs(keep, send):
    other = lax.ppermute(send, "mode", partners("mode", 1))
    count = lax.axis_size("space")
    blocks = add_and_cut([keep, other], lax.axis_index("space"), count)
    terms = [blocks[0]] + [
        lax.ppermute(blocks[k], "space", partners("space", k)) for k in range(1, count)
    ]
    return add_and_cut(terms, lax.axis_index("mode") // 2, lax.axis_size("mode") // 2)


def sum_over_modes(blocks):
    return blocks[0] + sum(
        lax.ppermute(block, "mode", partners("mode", 2 * k))
        for k, block in enumerate(blocks) if k > 0
    )


def finish_kernel(aliased, scale_ref, swap_ref, x_ref, *refs):
    out_ref = refs[aliased]
    parts, _, each, _, width = x_ref.shape
    rows = parts * each
    scale = scale_ref[0, 0]
    value = x_ref[...].reshape(rows * GROUP, width)
    for top in range(0, rows, GROUP):
        block = value[top * GROUP:(top + GROUP) * GROUP]
        block = scale * jnp.dot(swap_ref[...], block, preferred_element_type=jnp.float32)
        out_ref[:, 0, top:top + GROUP, :] = block.astype(jnp.bfloat16).reshape(GROUP, GROUP, width)


def finish_fields(first, arrived, scale, previous):
    parts, fields, each, modes, width = arrived.shape
    rows = parts * each
    swap = swap_matrix(GROUP, GROUP)
    operands = [scale.reshape(1, 1), swap, arrived, *previous]
    return pl.pallas_call(
        functools.partial(finish_kernel, len(previous)),
        grid=(fields, modes // GROUP),
        out_shape=jax.ShapeDtypeStruct((modes, 3, rows, width), jnp.bfloat16),
        in_specs=[
            pl.BlockSpec(memory_space=pltpu.SMEM),
            pl.BlockSpec(swap.shape, lambda f, m: (0, 0)),
            pl.BlockSpec((parts, 1, each, GROUP, width), lambda f, m: (0, f, 0, m, 0)),
        ] + [pl.BlockSpec(memory_space=pltpu.HBM) for _ in previous],
        out_specs=pl.BlockSpec((GROUP, 1, rows, width), lambda f, m: (m, first + f, 0, 0)),
        input_output_aliases={3: 0} if previous else {},
        compiler_params=pltpu.CompilerParams(vmem_limit_bytes=VMEM_BYTES),
        cost_estimate=pl.CostEstimate(
            flops=fields * modes * rows * width,
            bytes_accessed=4 * fields * modes * rows * width,
            transcendentals=0,
        ),
        name="finish",
    )(*operands)


def send_edges(first, last):
    count = lax.axis_size("space")
    forward = [(i, i + 1) for i in range(count - 1)]
    backward = [(target, source) for source, target in forward]
    return lax.ppermute(last, "space", forward), lax.ppermute(first, "space", backward)


def shards(sqrt_factors, model_error, water_depth, sea_mask, givens_transform):
    modes, fields, rows, width = sqrt_factors.shape
    parts = lax.axis_size("mode")
    count = modes // GROUP
    swap = functools.partial(
        lax.all_to_all, axis_name="mode", split_axis=0, concat_axis=0, tiled=True
    )

    near = min(count, 2)
    water_depth, sea_mask = (
        pltpu.with_memory_space_constraint(value, pltpu.HBM) for value in (water_depth, sea_mask)
    )
    factors = pltpu.with_memory_space_constraint(sqrt_factors, pltpu.HBM)
    head = send_edges(*cut_edges(0, near, factors, (water_depth, sea_mask)))
    cut = cut_edges(near, count - near, factors, ()) if count > near else ()
    *head, = lax.optimization_barrier((*head, *cut))
    head, cut = head[:2], head[2:]
    static = (*head, water_depth, sea_mask)
    inner = forecast_inner(sqrt_factors, water_depth, sea_mask)
    chunks = [swap(forecast_outer(inner, sqrt_factors, *static))]
    rest = ()
    if near > 1:
        rest = (forecast_groups(1, 1, 1, 0, count - 1, rest, sqrt_factors, *head, *static),)
    if count > near:
        tail = send_edges(*cut)
        rest = (forecast_groups(
            near, count - near, 0, near - 1, count - 1, rest, sqrt_factors, *tail, *static
        ),)
    chunks += [swap(value) for value in rest]

    fault = model_error.transpose(1, 2, 0, 3)
    turn = givens_transform.T
    devices = lax.axis_size("space") * parts
    half = lax.rem(lax.axis_index("mode"), 2).reshape(1, 1)
    columns = turn.shape[1]
    cell_count = float(fields * rows * lax.axis_size("space") * width)

    arrived = swap(rotate_fields(0, 2, chunks, fault, turn, parts))
    blocks = sum_over_slabs(*local_gram(chunks, fault, turn, parts, devices, half))
    last = rotate_fields(2, fields - 2, chunks, fault, turn, parts)
    last, total = lax.optimization_barrier((last, sum_over_modes(blocks)))
    last = swap(last)
    gram = total[:columns // devices, :columns] / cell_count
    inflation = jnp.sqrt(total[0, columns] / total[0, columns + 1])

    reduced = finish_fields(0, arrived, inflation, ())
    reduced = finish_fields(2, last, inflation, (reduced,))
    return (reduced, gram, inflation)


def solution(mesh):
    in_specs = (
        P("mode", None, "space", None),
        P(None, None, ("space", "mode"), None),
        P("space", None),
        P("space", None),
        P(),
    )
    out_specs = (P("mode", None, "space", None), P(("space", "mode"), None), P())
    return jax.shard_map(shards, mesh=mesh, in_specs=in_specs, out_specs=out_specs, check_vma=False)
```

```python
import functools

import jax
import jax.numpy as jnp
import numpy as np
from jax import lax
from jax.experimental import pallas as pl
from jax.experimental.pallas import tpu as pltpu
from jax.sharding import PartitionSpec as P

flux_coef = 0.2
slope_coef = 0.2
turn_coef = 0.1
keep_coef = 0.95

GROUP = 16
HALO = 4
LANES = 128
VMEM_BYTES = 48 * 1024 * 1024


def column_diff(tiles):
    lane = lax.broadcasted_iota(jnp.int32, tiles[0].shape, 1)
    from_left = [pltpu.roll(tile, 1, 1) for tile in tiles]
    from_right = [pltpu.roll(tile, LANES - 1, 1) for tile in tiles]
    zero = jnp.zeros_like(tiles[0])
    out = []
    for t in range(len(tiles)):
        left = from_left[t - 1] if t > 0 else zero
        right = from_right[t + 1] if t + 1 < len(tiles) else zero
        previous = jnp.where(lane == 0, left, from_left[t])
        following = jnp.where(lane == LANES - 1, right, from_right[t])
        out.append(following - previous)
    return out


def swap_matrix(inner, outer):
    place = np.arange(inner * outer).reshape(outer, inner).T.reshape(-1)
    matrix = np.zeros((inner * outer, inner * outer), np.float32)
    matrix[np.arange(inner * outer), place] = 1.0
    return jnp.asarray(matrix, jnp.bfloat16)


def in_hbm(shape, dtype):
    return pltpu.HBM(shape, dtype)


def cut_edges_kernel(fixed, *refs):
    first_ref, last_ref = refs[:2]
    out_first, out_last = refs[-2:]
    group, fields = first_ref.shape[:2]
    for ref, out, low in ((first_ref, out_first, 0), (last_ref, out_last, GROUP - HALO)):
        for m in range(group):
            for field in range(fields):
                edge = ref[m, field].astype(jnp.float32)[low:low + HALO]
                out[m * fields + field] = edge.astype(jnp.bfloat16)
    if fixed:
        depth_ref, mask_ref = refs[2:4]
        for out, low in ((out_first, 0), (out_last, depth_ref.shape[0] - HALO)):
            rest = depth_ref[low:low + HALO]
            for piece in range(3):
                part = rest.astype(jnp.bfloat16)
                out[group * fields + piece] = part
                rest = rest - part.astype(jnp.float32)
            out[group * fields + 3] = mask_ref[low:low + HALO].astype(jnp.float32).astype(jnp.bfloat16)


def cut_edges(first, groups, factors, fixed):
    _, fields, rows, width = factors.shape
    size = GROUP * groups if fixed else GROUP
    steps = 1 if fixed else groups
    count = size * steps * fields + (4 if fixed else 0)
    block = size * fields + (4 if fixed else 0)
    place = jax.ShapeDtypeStruct if fixed else in_hbm
    out = place((count, HALO, width), jnp.bfloat16)
    return pl.pallas_call(
        functools.partial(cut_edges_kernel, bool(fixed)),
        grid=(steps,),
        out_shape=(out, out),
        in_specs=[
            pl.BlockSpec((size, fields, GROUP, width), lambda i: (first // (size // GROUP) + i, 0, 0, 0)),
            pl.BlockSpec((size, fields, GROUP, width),
                         lambda i: (first // (size // GROUP) + i, 0, rows // GROUP - 1, 0)),
        ] + [pl.BlockSpec(value.shape, lambda i: (0, 0)) for value in fixed],
        out_specs=[pl.BlockSpec((block, HALO, width), lambda i: (i, 0, 0))] * 2,
        compiler_params=pltpu.CompilerParams(vmem_limit_bytes=VMEM_BYTES),
        cost_estimate=pl.CostEstimate(
            flops=0, bytes_accessed=5 * count * HALO * width * 2, transcendentals=0
        ),
        name="cut_edges",
    )(factors, factors, *fixed)


def block_of(count):
    return max(size for size in range(1, 55) if count % size == 0)


def two_steps(rows, width, cells, depth, wet, surf1, east1, north1, surf2, put_row):
    tiles = width // LANES
    spots = [slice(t * LANES, (t + 1) * LANES) for t in range(tiles)]

    def get(ref, i):
        return [ref[i, :, spot] for spot in spots]

    def get_field(field, i):
        return [cells[field, i + HALO, :, spot] for spot in spots]

    def get_static(ref, i):
        parts = [ref[i + HALO, :, spot] for spot in spots]
        return [jnp.concatenate([part] * (GROUP // 8), axis=0) for part in parts]

    def put(ref, i, values):
        for spot, value in zip(spots, values):
            ref[i, :, spot] = value

    def times(one, other):
        return [a * b for a, b in zip(one, other)]

    def over_rows(first, last, body):
        size = block_of(last - first)

        def block(k, carry):
            body(first + k * size, size)
            return carry

        lax.fori_loop(0, (last - first) // size, block, 0)

    def surfaces(i, size, surface_at, east_at, north_at, put_at):
        flux = {j: times(get_static(depth, i + j), north_at(i + j)) for j in (-1, 0)}
        for j in range(size):
            flux[j + 1] = times(get_static(depth, i + j + 1), north_at(i + j + 1))
            sides = column_diff(times(get_static(depth, i + j), east_at(i + j)))
            sea, surface = get_static(wet, i + j), surface_at(i + j)
            put_at(i + j, [
                sea[t] * (surface[t] - (sides[t] + (flux[j + 1][t] - flux[j - 1][t])))
                for t in range(tiles)
            ])

    def flows(i, size, surface_at, east_at, north_at, put_at):
        surface = {j: surface_at(i + j) for j in (-1, 0)}
        for j in range(size):
            surface[j + 1] = surface_at(i + j + 1)
            sides = column_diff(surface[j])
            sea, east, north = get_static(wet, i + j), east_at(i + j), north_at(i + j)
            put_at(i + j, surface[j], [
                sea[t] * (keep_coef * east[t] + turn_coef * north[t] - sides[t])
                for t in range(tiles)
            ], [
                sea[t] * (keep_coef * north[t] - turn_coef * east[t]
                          - (surface[j + 1][t] - surface[j - 1][t]))
                for t in range(tiles)
            ])

    def first_surface(i, size):
        surfaces(
            i, size, lambda r: get_field(0, r), lambda r: get_field(1, r),
            lambda r: get_field(2, r), lambda r, value: put(surf1, r + 3, value),
        )

    def first_flow(i, size):
        def put_flow(r, surface, east, north):
            put(east1, r + 2, east)
            put(north1, r + 2, north)

        flows(
            i, size, lambda r: get(surf1, r + 3), lambda r: get_field(1, r),
            lambda r: get_field(2, r), put_flow,
        )

    def second_surface(i, size):
        surfaces(
            i, size, lambda r: get(surf1, r + 3), lambda r: get(east1, r + 2),
            lambda r: get(north1, r + 2), lambda r, value: put(surf2, r + 1, value),
        )

    def second_flow(i, size):
        def put_out(r, surface, east, north):
            surface = [value * (1.0 / slope_coef) for value in surface]
            for field, values in enumerate((surface, east, north)):
                for spot, value in zip(spots, values):
                    put_row(r, field, spot, value.astype(jnp.bfloat16))

        flows(
            i, size, lambda r: get(surf2, r + 1), lambda r: get(east1, r + 2),
            lambda r: get(north1, r + 2), put_out,
        )

    over_rows(-3, rows + 3, first_surface)
    over_rows(-2, rows + 2, first_flow)
    over_rows(-1, rows + 1, second_surface)
    over_rows(0, rows, second_flow)


def place_static(depth, wet, first, levels, seas):
    for j in range(levels.shape[0]):
        shape = depth.shape[1:]
        depth[first + j] = jnp.broadcast_to(flux_coef * slope_coef * levels[j:j + 1], shape)
        wet[first + j] = jnp.broadcast_to(seas[j:j + 1], shape)


def place_message_static(depth, wet, first, static_ref):
    value = static_ref[...].astype(jnp.float32)
    place_static(depth, wet, first, value[0] + value[1] + value[2], value[3])


def place_own_static(depth, wet, first, depth_ref, mask_ref, low, count):
    for top in range(low, low + count, 8):
        place_static(depth, wet, first + top - low, depth_ref[top:top + 8],
                     mask_ref[top:top + 8].astype(jnp.float32))


def spread_rows(x, swap_ref, field):
    width = x.shape[-1]
    block = jnp.dot(swap_ref[...], x.reshape(GROUP * GROUP, width), preferred_element_type=jnp.float32)
    block = block * slope_coef if field == 0 else block
    return block.reshape(GROUP, GROUP, width)


def spread_edges(ends, low_ref, high_ref, swap_ends_ref, field, fields):
    width = low_ref.shape[-1]
    if field == 0:
        ends[:, :HALO] = low_ref[...].astype(jnp.float32)
        ends[:, HALO:] = high_ref[...].astype(jnp.float32)
    block = jnp.concatenate([ends[m * fields + field] for m in range(GROUP)], axis=0)
    block = jnp.dot(
        swap_ends_ref[...], block.astype(jnp.bfloat16), preferred_element_type=jnp.float32
    ).reshape(2 * HALO, GROUP, width)
    return block * slope_coef if field == 0 else block


def forecast_kernel(x_ref, low_ref, high_ref, low_static, high_static, depth_ref, mask_ref,
                    swap_ref, swap_ends_ref, *refs):
    out_ref, cells, ends, depth, wet = refs[-9:-4]
    _, fields, rows, width = x_ref.shape

    for field in range(fields):
        for top in range(0, rows, GROUP):
            cells[field, HALO + top:HALO + top + GROUP] = spread_rows(
                x_ref[:, field, top:top + GROUP, :], swap_ref, field
            )
        block = spread_edges(ends, low_ref, high_ref, swap_ends_ref, field, fields)
        cells[field, :HALO] = block[:HALO]
        cells[field, HALO + rows:] = block[HALO:]
    place_message_static(depth, wet, 0, low_static)
    place_message_static(depth, wet, HALO + rows, high_static)
    place_own_static(depth, wet, HALO, depth_ref, mask_ref, 0, rows)

    def put_row(r, field, spot, value):
        out_ref[r, field, :, spot] = value

    two_steps(rows, width, cells, depth, wet, *refs[-4:], put_row)


def inner_kernel(x_ref, depth_ref, mask_ref, swap_ref, out_ref, cells, depth, wet, *steps):
    _, fields, rows, width = x_ref.shape
    for field in range(fields):
        for top in range(0, rows, GROUP):
            cells[field, HALO + top:HALO + top + GROUP] = spread_rows(
                x_ref[:, field, top:top + GROUP, :], swap_ref, field
            )
    for ref in (depth, wet, *(cells.at[field] for field in range(fields))):
        ref[:HALO] = jnp.zeros((HALO,) + ref.shape[1:], jnp.float32)
        ref[HALO + rows:] = jnp.zeros((HALO,) + ref.shape[1:], jnp.float32)
    place_own_static(depth, wet, HALO, depth_ref, mask_ref, 0, rows)

    def put_row(r, field, spot, value):
        out_ref[r, field, :, spot] = value

    two_steps(rows, width, cells, depth, wet, *steps, put_row)


def outer_kernel(first_ref, last_ref, low_ref, high_ref, low_static, high_static, depth_ref,
                 mask_ref, swap_ref, swap_ends_ref, inner_ref, out_ref,
                 cells, ends, edge, depth, wet, surf1, east1, north1, surf2, turned, sems):
    _, fields, _, width = first_ref.shape
    rows = out_ref.shape[0]
    for field in range(fields):
        edge[field] = spread_edges(ends, low_ref, high_ref, swap_ends_ref, field, fields)
    copies = []
    for side, (x_ref, first) in enumerate(((first_ref, 0), (last_ref, rows - HALO))):
        for field in range(fields):
            block = spread_rows(x_ref[:, field], swap_ref, field)
            if side == 0:
                cells[field, :HALO] = edge[field, :HALO]
                cells[field, HALO:] = block[:2 * HALO]
            else:
                cells[field, :2 * HALO] = block[GROUP - 2 * HALO:]
                cells[field, 2 * HALO:] = edge[field, HALO:]
        if side == 0:
            place_message_static(depth, wet, 0, low_static)
            place_own_static(depth, wet, HALO, depth_ref, mask_ref, 0, 2 * HALO)
        else:
            place_own_static(depth, wet, 0, depth_ref, mask_ref, rows - 2 * HALO, 2 * HALO)
            place_message_static(depth, wet, 2 * HALO, high_static)

        def put_row(r, field, spot, value):
            turned[side, r, field, :, spot] = value

        two_steps(HALO, width, cells, depth, wet, surf1, east1, north1, surf2, put_row)
        copies.append(pltpu.make_async_copy(
            turned.at[side], out_ref.at[pl.ds(first, HALO)], sems.at[side]
        ))
        copies[-1].start()
    for copy in copies:
        copy.wait()


def step_scratch(rows, width):
    return [pltpu.VMEM((rows + more, GROUP, width), jnp.float32) for more in (6, 4, 4, 2)]


def forecast_inner(factors, depth, mask):
    _, fields, rows, width = factors.shape
    padded = rows + 2 * HALO
    swap = swap_matrix(GROUP, GROUP)
    return pl.pallas_call(
        inner_kernel,
        grid=(1,),
        out_shape=in_hbm((rows, fields, GROUP, width), jnp.bfloat16),
        in_specs=[pl.BlockSpec((GROUP, fields, rows, width), lambda i: (0, 0, 0, 0))] + [
            pl.BlockSpec(value.shape, lambda i: (0, 0)) for value in (depth, mask, swap)
        ],
        out_specs=pl.BlockSpec((rows, fields, GROUP, width), lambda i: (0, 0, 0, 0)),
        scratch_shapes=[
            pltpu.VMEM((fields, padded, GROUP, width), jnp.float32),
            pltpu.VMEM((padded, 8, width), jnp.float32),
            pltpu.VMEM((padded, 8, width), jnp.float32),
        ] + step_scratch(rows, width),
        compiler_params=pltpu.CompilerParams(vmem_limit_bytes=VMEM_BYTES),
        cost_estimate=pl.CostEstimate(
            flops=60 * GROUP * rows * width,
            bytes_accessed=2 * 2 * GROUP * fields * rows * width,
            transcendentals=0,
        ),
        name="inner",
    )(factors, depth, mask, swap)


def forecast_outer(inner, factors, low, high, depth, mask):
    _, fields, rows, width = factors.shape
    edge = GROUP * fields
    last = low.shape[0] // 4 - 1
    swap, swap_ends = swap_matrix(GROUP, GROUP), swap_matrix(2 * HALO, GROUP)
    return pl.pallas_call(
        outer_kernel,
        grid=(1,),
        out_shape=in_hbm(inner.shape, inner.dtype),
        in_specs=[
            pl.BlockSpec((GROUP, fields, GROUP, width), lambda i: (0, 0, 0, 0)),
            pl.BlockSpec((GROUP, fields, GROUP, width), lambda i: (0, 0, rows // GROUP - 1, 0)),
            pl.BlockSpec((edge, HALO, width), lambda i: (0, 0, 0)),
            pl.BlockSpec((edge, HALO, width), lambda i: (0, 0, 0)),
            pl.BlockSpec((4, HALO, width), lambda i: (last, 0, 0)),
            pl.BlockSpec((4, HALO, width), lambda i: (last, 0, 0)),
        ] + [
            pl.BlockSpec(value.shape, lambda i: (0, 0)) for value in (depth, mask, swap, swap_ends)
        ] + [pl.BlockSpec(memory_space=pltpu.HBM)],
        out_specs=pl.BlockSpec(memory_space=pltpu.HBM),
        input_output_aliases={10: 0},
        scratch_shapes=[
            pltpu.VMEM((fields, 3 * HALO, GROUP, width), jnp.float32),
            pltpu.VMEM((edge, 2 * HALO, width), jnp.float32),
            pltpu.VMEM((fields, 2 * HALO, GROUP, width), jnp.float32),
            pltpu.VMEM((3 * HALO, 8, width), jnp.float32),
            pltpu.VMEM((3 * HALO, 8, width), jnp.float32),
        ] + step_scratch(HALO, width) + [
            pltpu.VMEM((2, HALO, fields, GROUP, width), jnp.bfloat16),
            pltpu.SemaphoreType.DMA((2,)),
        ],
        compiler_params=pltpu.CompilerParams(vmem_limit_bytes=VMEM_BYTES),
        cost_estimate=pl.CostEstimate(
            flops=20 * GROUP * rows * width,
            bytes_accessed=2 * 2 * GROUP * fields * GROUP * width,
            transcendentals=0,
        ),
        name="outer",
    )(factors, factors, low, high, low, high, depth, mask, swap, swap_ends, inner)


def forecast_groups(first, count, skip, place, whole_count, previous, factors, low, high,
                    static_low, static_high, depth, mask):
    modes, fields, rows, width = factors.shape
    padded = rows + 2 * HALO
    edge = GROUP * fields
    last = static_low.shape[0] // 4 - 1
    swap, swap_ends = swap_matrix(GROUP, GROUP), swap_matrix(2 * HALO, GROUP)

    def whole(value):
        return pl.BlockSpec(value.shape, lambda i: (0,) * value.ndim)

    return pl.pallas_call(
        forecast_kernel,
        grid=(count,),
        out_shape=in_hbm((rows, fields, whole_count * GROUP, width), jnp.bfloat16),
        in_specs=[
            pl.BlockSpec((GROUP, fields, rows, width), lambda i: (first + i, 0, 0, 0)),
            pl.BlockSpec((edge, HALO, width), lambda i: (skip + i, 0, 0)),
            pl.BlockSpec((edge, HALO, width), lambda i: (skip + i, 0, 0)),
            pl.BlockSpec((4, HALO, width), lambda i: (last, 0, 0)),
            pl.BlockSpec((4, HALO, width), lambda i: (last, 0, 0)),
            whole(depth),
            whole(mask),
            whole(swap),
            whole(swap_ends),
        ] + [pl.BlockSpec(memory_space=pltpu.HBM) for _ in previous],
        out_specs=pl.BlockSpec((rows, fields, GROUP, width), lambda i: (0, 0, place + i, 0)),
        input_output_aliases={9: 0} if previous else {},
        scratch_shapes=[
            pltpu.VMEM((fields, padded, GROUP, width), jnp.float32),
            pltpu.VMEM((edge, 2 * HALO, width), jnp.float32),
            pltpu.VMEM((padded, 8, width), jnp.float32),
            pltpu.VMEM((padded, 8, width), jnp.float32),
        ] + step_scratch(rows, width),
        compiler_params=pltpu.CompilerParams(vmem_limit_bytes=VMEM_BYTES),
        cost_estimate=pl.CostEstimate(
            flops=60 * count * GROUP * rows * width,
            bytes_accessed=2 * 2 * count * GROUP * fields * rows * width,
            transcendentals=0,
        ),
        name="forecast",
    )(factors, low, high, static_low, static_high, depth, mask, swap, swap_ends, *previous)


def all_columns(chunk_refs, fault_ref, j):
    own = [ref[:, j, 0] for ref in chunk_refs]
    joined = jnp.concatenate(own, axis=1)
    return joined.reshape(-1, joined.shape[-1]), fault_ref[0, j]


def rotate_kernel(count, first, *refs):
    near_ref, *chunk_refs = refs[:count]
    fault_ref, turn_ref, out_ref = refs[count:]
    parts, _, size, modes, width = out_ref.shape
    field, top = first + pl.program_id(0), pl.program_id(1) * size
    for j in range(size):
        own = [near_ref[:, top + j, field]] + [ref[:, j, 0] for ref in chunk_refs]
        prior = jnp.concatenate(own, axis=1).reshape(-1, width)
        columns = jnp.concatenate([prior, fault_ref[0, j]], axis=0)
        value = jnp.dot(turn_ref[...], columns, preferred_element_type=jnp.float32)
        out_ref[:, 0, j] = value.astype(jnp.bfloat16).reshape(parts, modes, width)


def by_part(chunks, parts):
    return [c.reshape((parts, c.shape[0] // parts) + c.shape[1:]) for c in chunks]


def rotate_fields(first, fields, chunks, fault, turn, parts):
    width = chunks[0].shape[-1]
    each = chunks[0].shape[0] // parts
    kept = turn.shape[0]
    noise = fault.shape[2]
    modes = kept // parts
    size = 3 if each % 3 == 0 else 1
    views = by_part(chunks, parts)
    return pl.pallas_call(
        functools.partial(rotate_kernel, len(views), first),
        grid=(fields, each // size),
        out_shape=in_hbm((parts, fields, each, modes, width), jnp.bfloat16),
        in_specs=[pl.BlockSpec(memory_space=pltpu.VMEM)] + [
            pl.BlockSpec((parts, size, 1, v.shape[3], width), lambda f, j: (0, j, first + f, 0, 0))
            for v in views[1:]
        ] + [
            pl.BlockSpec((1, size, noise, width), lambda f, j: (first + f, j, 0, 0)),
            pl.BlockSpec(memory_space=pltpu.VMEM),
        ],
        out_specs=pl.BlockSpec((parts, 1, size, modes, width), lambda f, j: (0, f, j, 0, 0)),
        compiler_params=pltpu.CompilerParams(vmem_limit_bytes=VMEM_BYTES),
        cost_estimate=pl.CostEstimate(
            flops=2 * fields * each * width * kept * turn.shape[1],
            bytes_accessed=2 * fields * each * width * (kept + turn.shape[1]),
            transcendentals=0,
        ),
        name="rotate",
    )(*views, fault, turn)


def gram_kernel(count, each, devices, *refs):
    chunk_refs = refs[:count]
    fault_ref, turn_ref, half_ref, keep_ref, send_ref, gram_ref = refs[count:]
    pairs = [all_columns(chunk_refs, fault_ref, j) for j in range(each)]
    columns = jnp.concatenate(
        [jnp.concatenate([prior, fault], axis=0) for prior, fault in pairs], axis=1
    )
    value = lax.dot_general(
        columns, columns, (((1,), (1,)), ((), ())), preferred_element_type=jnp.float32
    )
    step = pl.program_id(0)

    @pl.when(step == 0)
    def _():
        gram_ref[...] = value

    @pl.when(step > 0)
    def _():
        gram_ref[...] += value

    @pl.when(step == pl.num_programs(0) - 1)
    def _():
        gram = gram_ref[...]
        size = gram.shape[0]
        row = lax.broadcasted_iota(jnp.int32, gram.shape, 0)
        column = lax.broadcasted_iota(jnp.int32, gram.shape, 1)
        full = jnp.sum(jnp.where(row == column, gram, 0.0))
        turn = turn_ref[...]
        turned = 0.0
        for _ in range(3):
            piece = gram.astype(jnp.bfloat16)
            turned = turned + jnp.dot(turn, piece, preferred_element_type=jnp.float32)
            gram = gram - piece.astype(jnp.float32)
        kept = jnp.sum(turned * turn.astype(jnp.float32))
        own = size // devices
        slot = keep_ref.shape[0] // (devices // 2)
        lane = lax.broadcasted_iota(jnp.int32, (keep_ref.shape[0], LANES), 1)
        traces = jnp.where(lane == 0, full, jnp.where(lane == 1, kept, 0.0))
        low = half_ref[0, 0] == 0
        for out in (keep_ref, send_ref):
            if slot != own:
                out[...] = jnp.zeros_like(out)
            out[:, size:] = traces
        for q in range(devices // 2):
            even = gram_ref[2 * q * own:(2 * q + 1) * own]
            uneven = gram_ref[(2 * q + 1) * own:(2 * q + 2) * own]
            keep_ref[q * slot:q * slot + own, :size] = jnp.where(low, even, uneven)
            send_ref[q * slot:q * slot + own, :size] = jnp.where(low, uneven, even)


def local_gram(chunks, fault, turn, parts, devices, half):
    width = chunks[0].shape[-1]
    each = chunks[0].shape[0] // parts
    noise = fault.shape[2]
    columns = turn.shape[1]
    views = by_part(chunks, parts)
    slot = -(-columns // devices // 8) * 8
    slots = (devices // 2 * slot, columns + LANES)
    out = in_hbm(slots, jnp.float32)
    return pl.pallas_call(
        functools.partial(gram_kernel, len(views), each, devices),
        grid=(3,),
        out_shape=(out, out),
        in_specs=[
            pl.BlockSpec((parts, each, 1, v.shape[3], width), lambda f: (0, 0, f, 0, 0))
            for v in views
        ] + [
            pl.BlockSpec((1, each, noise, width), lambda f: (f, 0, 0, 0)),
            pl.BlockSpec(turn.shape, lambda f: (0, 0)),
            pl.BlockSpec(memory_space=pltpu.SMEM),
        ],
        out_specs=[pl.BlockSpec(slots, lambda f: (0, 0))] * 2,
        scratch_shapes=[pltpu.VMEM((columns, columns), jnp.float32)],
        compiler_params=pltpu.CompilerParams(vmem_limit_bytes=VMEM_BYTES),
        cost_estimate=pl.CostEstimate(
            flops=2 * 3 * each * width * columns * columns,
            bytes_accessed=2 * 3 * each * width * columns,
            transcendentals=0,
        ),
        name="gram",
    )(*views, fault, turn, half)


def add_kernel(count, parts, me_ref, *refs):
    total = refs[0][...]
    for ref in refs[1:count]:
        total = total + ref[...]
    total_ref = refs[-1]
    total_ref[...] = total
    rows = total.shape[0] // parts
    for k in range(parts):
        first = pl.multiple_of(jnp.bitwise_xor(me_ref[0, 0], k) * rows, 8)
        refs[count + k][...] = total_ref[pl.ds(first, rows)]


def add_and_cut(terms, me, parts):
    rows, width = terms[0].shape
    whole = pl.BlockSpec((rows, width), lambda: (0, 0))
    block = pl.BlockSpec((rows // parts, width), lambda: (0, 0))
    return pl.pallas_call(
        functools.partial(add_kernel, len(terms), parts),
        out_shape=[in_hbm((rows // parts, width), jnp.float32) for _ in range(parts)],
        in_specs=[pl.BlockSpec(memory_space=pltpu.SMEM)] + [whole for _ in terms],
        out_specs=[block for _ in range(parts)],
        scratch_shapes=[pltpu.VMEM((rows, width), jnp.float32)],
        compiler_params=pltpu.CompilerParams(vmem_limit_bytes=VMEM_BYTES),
        cost_estimate=pl.CostEstimate(
            flops=len(terms) * rows * width,
            bytes_accessed=4 * (len(terms) + 1) * rows * width,
            transcendentals=0,
        ),
        name="add",
    )(me.reshape(1, 1), *terms)


def partners(axis, distance):
    return [(i, i ^ distance) for i in range(lax.axis_size(axis))]


def sum_over_slabs(keep, send):
    other = lax.ppermute(send, "mode", partners("mode", 1))
    count = lax.axis_size("space")
    blocks = add_and_cut([keep, other], lax.axis_index("space"), count)
    terms = [blocks[0]] + [
        lax.ppermute(blocks[k], "space", partners("space", k)) for k in range(1, count)
    ]
    return add_and_cut(terms, lax.axis_index("mode") // 2, lax.axis_size("mode") // 2)


def sum_over_modes(blocks):
    return blocks[0] + sum(
        lax.ppermute(block, "mode", partners("mode", 2 * k))
        for k, block in enumerate(blocks) if k > 0
    )


def finish_kernel(aliased, scale_ref, swap_ref, x_ref, *refs):
    out_ref = refs[aliased]
    parts, _, each, _, width = x_ref.shape
    rows = parts * each
    scale = scale_ref[0, 0]
    value = x_ref[...].reshape(rows * GROUP, width)
    for top in range(0, rows, GROUP):
        block = value[top * GROUP:(top + GROUP) * GROUP]
        block = scale * jnp.dot(swap_ref[...], block, preferred_element_type=jnp.float32)
        out_ref[:, 0, top:top + GROUP, :] = block.astype(jnp.bfloat16).reshape(GROUP, GROUP, width)


def finish_fields(first, arrived, scale, previous):
    parts, fields, each, modes, width = arrived.shape
    rows = parts * each
    swap = swap_matrix(GROUP, GROUP)
    operands = [scale.reshape(1, 1), swap, arrived, *previous]
    return pl.pallas_call(
        functools.partial(finish_kernel, len(previous)),
        grid=(fields, modes // GROUP),
        out_shape=jax.ShapeDtypeStruct((modes, 3, rows, width), jnp.bfloat16),
        in_specs=[
            pl.BlockSpec(memory_space=pltpu.SMEM),
            pl.BlockSpec(swap.shape, lambda f, m: (0, 0)),
            pl.BlockSpec((parts, 1, each, GROUP, width), lambda f, m: (0, f, 0, m, 0)),
        ] + [pl.BlockSpec(memory_space=pltpu.HBM) for _ in previous],
        out_specs=pl.BlockSpec((GROUP, 1, rows, width), lambda f, m: (m, first + f, 0, 0)),
        input_output_aliases={3: 0} if previous else {},
        compiler_params=pltpu.CompilerParams(vmem_limit_bytes=VMEM_BYTES),
        cost_estimate=pl.CostEstimate(
            flops=fields * modes * rows * width,
            bytes_accessed=4 * fields * modes * rows * width,
            transcendentals=0,
        ),
        name="finish",
    )(*operands)


def send_edges(first, last):
    count = lax.axis_size("space")
    forward = [(i, i + 1) for i in range(count - 1)]
    backward = [(target, source) for source, target in forward]
    return lax.ppermute(last, "space", forward), lax.ppermute(first, "space", backward)


def shards(sqrt_factors, model_error, water_depth, sea_mask, givens_transform):
    modes, fields, rows, width = sqrt_factors.shape
    parts = lax.axis_size("mode")
    count = modes // GROUP
    swap = functools.partial(
        lax.all_to_all, axis_name="mode", split_axis=0, concat_axis=0, tiled=True
    )

    near = min(count, 2)
    water_depth, sea_mask = (
        pltpu.with_memory_space_constraint(value, pltpu.HBM) for value in (water_depth, sea_mask)
    )
    factors = pltpu.with_memory_space_constraint(sqrt_factors, pltpu.HBM)
    head = send_edges(*cut_edges(0, near, factors, (water_depth, sea_mask)))
    cut = cut_edges(near, count - near, factors, ()) if count > near else ()
    *head, = lax.optimization_barrier((*head, *cut))
    head, cut = head[:2], head[2:]
    static = (*head, water_depth, sea_mask)
    inner = forecast_inner(sqrt_factors, water_depth, sea_mask)
    chunks = [swap(forecast_outer(inner, sqrt_factors, *static))]
    rest = ()
    if near > 1:
        rest = (forecast_groups(1, 1, 1, 0, count - 1, rest, sqrt_factors, *head, *static),)
    if count > near:
        tail = send_edges(*cut)
        rest = (forecast_groups(
            near, count - near, 0, near - 1, count - 1, rest, sqrt_factors, *tail, *static
        ),)
    chunks += [swap(value) for value in rest]

    fault = model_error.transpose(1, 2, 0, 3)
    turn = givens_transform.T
    devices = lax.axis_size("space") * parts
    half = lax.rem(lax.axis_index("mode"), 2).reshape(1, 1)
    columns = turn.shape[1]
    cell_count = float(fields * rows * lax.axis_size("space") * width)

    arrived = swap(rotate_fields(0, 2, chunks, fault, turn, parts))
    blocks = sum_over_slabs(*local_gram(chunks, fault, turn, parts, devices, half))
    last = rotate_fields(2, fields - 2, chunks, fault, turn, parts)
    last, total = lax.optimization_barrier((last, sum_over_modes(blocks)))
    last = swap(last)
    gram = total[:columns // devices, :columns] / cell_count
    inflation = jnp.sqrt(total[0, columns] / total[0, columns + 1])

    reduced = finish_fields(0, arrived, inflation, ())
    reduced = finish_fields(2, last, inflation, (reduced,))
    return (reduced, gram, inflation)


def solution(mesh):
    in_specs = (
        P("mode", None, "space", None),
        P(None, None, ("space", "mode"), None),
        P("space", None),
        P("space", None),
        P(),
    )
    out_specs = (P("mode", None, "space", None), P(("space", "mode"), None), P())
    return jax.shard_map(shards, mesh=mesh, in_specs=in_specs, out_specs=out_specs, check_vma=False)
```
